32 devices in a mesh: block: 8 (over y, x, core), walker: 4 (over z).
Axes of the slice: x: 2, y: 2, z: 4, core: 2. Of those that a mesh axis runs over, the one named last changes fastest.
Arguments:
- green: bfloat16 [20, 294912], P('walker', 'block'), may hold values from -6 to 6
- chol: bfloat16 [64, 192, 1536], P('block'), may hold values from -0.15625 to 0.15625
- counts: int32 [4], replicated, may hold values from 1 to 5, as said below
- move_slot: int32 [4, 2], replicated, may hold values from -1 to 4, as said below
- move_dest: int32 [4, 2], replicated, may hold values from -1 to 3, as said below
Outputs:
- new_green: bfloat16 [12, 294912], P('walker', 'block')
- energy: float32 [12], P('walker')
The draws below stay inside these ranges and needn't reach their ends.
Inputs may be any that keep to these rules, and one draw needn't show every extreme that they name: On every device, counts minus the walkers it sends plus the walkers it receives equals 3; in every draw some device has count 5 and some device has count 1. `move_slot`: in each row the entries >= 0 come first, are distinct, and name live slots of that device; the rest are -1. `move_dest`: -1 exactly where move_slot is -1, else another device's index; from one device at most 1 walker goes to any one device, and some device sends that many to one.
All inputs are finite; a program needn't handle non-finite values.
Results may differ from the reference program's by a relative error of at most 0.0004.
Values may be sent and summed in bfloat16 or wider, within the bound.
No kernel may reach another device: no remote copies, remote signals or barrier semaphores. Data moves between devices by JAX's collectives and lax.ppermute only.
A program may use at most 64 MiB of HBM per device.

```python
import jax
import jax.numpy as jnp
from jax import lax

NORB = 1536
NOCC = 192
MOVE = 2
BAL = 3
WSLOT = 5
GFLAT = 294912
NCHOL = 64
W_IN = 20
N_WALKER = 4


def population(key):
    base_key = jax.random.fold_in(key, 7)
    key_cycle, key_out, key_slot = jax.random.split(base_key, 3)
    walker_total = N_WALKER
    device_ids = jnp.arange(walker_total, dtype=jnp.int32)
    cycle_scores = jax.random.randint(key_cycle, (walker_total,), 0, 1 << 20).astype(jnp.int32) * walker_total + device_ids
    cycle_order = jnp.argsort(cycle_scores, stable=True).astype(jnp.int32)
    places = jnp.arange(walker_total, dtype=jnp.int32)
    out_by_place = jax.random.randint(key_out, (walker_total,), 0, MOVE + 1).astype(jnp.int32)
    out_by_place = jnp.where((places >= 1) & (places <= MOVE), MOVE, out_by_place)
    zero_place = (places == 0) | (places == MOVE + 1) | (places >= walker_total - MOVE + 1)
    out_by_place = jnp.where(zero_place, 0, out_by_place).astype(jnp.int32)
    place_of = jnp.zeros((walker_total,), jnp.int32).at[cycle_order].set(places)
    outgoing = out_by_place[place_of]
    move_ids = jnp.arange(MOVE, dtype=jnp.int32)
    dest_all = cycle_order[(place_of[:, None] + 1 + move_ids[None, :] % (walker_total - 1)) % walker_total]
    active = move_ids[None, :] < outgoing[:, None]
    arriving = jnp.sum(((dest_all[:, :, None] == device_ids[None, None, :]) & active[:, :, None]).astype(jnp.int32), axis=(0, 1))
    counts = (BAL + outgoing - arriving).astype(jnp.int32)
    slot_ids = jnp.arange(WSLOT, dtype=jnp.int32)
    scores = jax.random.randint(key_slot, (walker_total, WSLOT), 0, 4096).astype(jnp.int32) * WSLOT + slot_ids[None, :]
    scores = jnp.where(slot_ids[None, :] < counts[:, None], scores, scores + 8192 * WSLOT)
    forced = (place_of[:, None] == 1) & (slot_ids[None, :] == WSLOT - 1)
    scores = jnp.where(forced, -1, scores)
    picked = jnp.argsort(scores, axis=1, stable=True)[:, :MOVE].astype(jnp.int32)
    slot_list = jnp.where(active, picked, -1).astype(jnp.int32)
    dest_list = jnp.where(active, dest_all, -1).astype(jnp.int32)
    return (counts, slot_list, dest_list)


def draw_counts(key, part):
    return population(key)[0]


def draw_move_slot(key, part):
    return population(key)[1]


def draw_move_dest(key, part):
    return population(key)[2]


def level_of(stream_key, dims, cuts, smallest, top_value):
    gain = 1.0
    for dim, shards_of in cuts:
        draws = jax.random.uniform(jax.random.fold_in(jax.random.fold_in(stream_key, 6), dim), (shards_of,), jnp.float32, smallest / len(cuts), top_value / len(cuts))
        gain = gain * jnp.repeat(jnp.exp(draws), dims[dim] // shards_of).reshape((-1,) + (1,) * (len(dims) - 1 - dim))
    return gain


def noise(stream_key, extent, width, reach, cuts=(), held_as=jnp.bfloat16):
    level = level_of(stream_key, extent, cuts, -0.22, 0.18) if cuts else 1.0
    values = jax.random.normal(stream_key, extent, jnp.float32) * width * level
    return jnp.minimum(jnp.maximum(values, -reach), reach).astype(held_as)


def setup_inputs(seed: int = 0) -> dict:
    streams_of = jax.random.split(jax.random.key(seed), 6)
    green = noise(streams_of[0], (W_IN, GFLAT), 1.0, 6.0, ((0, 4), (1, 8)))
    chol = noise(streams_of[1], (NCHOL, NOCC, NORB), NORB ** -0.5, 0.15625, ((0, 8),))
    counts = draw_counts(jax.random.fold_in(streams_of[5], 71), 0)
    move_slot = draw_move_slot(jax.random.fold_in(streams_of[5], 71), 0)
    move_dest = draw_move_dest(jax.random.fold_in(streams_of[5], 71), 0)
    return {"green": green, "chol": chol, "counts": counts, "move_slot": move_slot, "move_dest": move_dest}


def layout(counts, move_slot, move_dest, target):
    slot_ids = jnp.arange(WSLOT, dtype=jnp.int32)
    device_ids = jnp.arange(N_WALKER, dtype=jnp.int32)
    move_ids = jnp.arange(MOVE, dtype=jnp.int32)
    occupied = slot_ids[None, :] < counts[:, None]
    leaving = jnp.any(move_slot[:, :, None] == slot_ids[None, None, :], axis=1)
    staying = (occupied & jnp.logical_not(leaving))[target]
    far_key = jnp.int32(1 << 20)
    stay_keys = jnp.where(staying, slot_ids, far_key)
    arrive_keys = jnp.where(move_dest == target, WSLOT + device_ids[:, None] * MOVE + move_ids[None, :], far_key).reshape(-1)
    stay_rows = target * WSLOT + slot_ids
    arrive_rows = (device_ids[:, None] * WSLOT + jnp.maximum(move_slot, 0)).reshape(-1)
    sort_keys = jnp.concatenate([stay_keys, arrive_keys.astype(jnp.int32)])
    source_rows = jnp.concatenate([stay_rows, arrive_rows.astype(jnp.int32)])
    ranking = jnp.argsort(sort_keys, stable=True)[:BAL]
    return source_rows[ranking].astype(jnp.int32)


def reference(green, chol, counts, move_slot, move_dest):
    row_index = jnp.concatenate([layout(counts, move_slot, move_dest, target) for target in range(N_WALKER)])
    new_green = green[row_index]
    chol_float = chol.astype(jnp.float32)
    energy_scale = 0.5 / (NOCC * (NCHOL ** 0.5))

    def walker_energy(walker_row):
        green_mat = walker_row.astype(jnp.float32).reshape(NOCC, NORB)
        transfer = jnp.einsum("gip,jp->gij", chol_float, green_mat, precision=lax.Precision.HIGHEST)
        return jnp.sum(transfer * jnp.swapaxes(transfer, 1, 2))

    energy = -energy_scale * lax.map(walker_energy, new_green)
    return new_green, energy
```

```python
import functools
import math

import jax
import jax.numpy as jnp
from jax import lax
from jax.experimental import pallas as pl
from jax.experimental.pallas import tpu as pltpu
from jax.sharding import PartitionSpec as P


def arrival_ranks(move_slot, move_dest):
    active = move_slot >= 0
    move_total = move_slot.shape[1]
    earlier = jnp.arange(move_total)[None, :] < jnp.arange(move_total)[:, None]
    same_target = (
        (move_dest[:, :, None] == move_dest[:, None, :]) & earlier[None, :, :] & active[:, None, :]
    )
    return (active, jnp.sum(same_target.astype(jnp.int32), axis=2))


def general_body(green, chol, counts, move_slot, move_dest):
    walker_total = lax.axis_size("walker")
    own_index = lax.axis_index("walker")
    slot_total = green.shape[0]
    share_width = green.shape[1]
    keep_total = slot_total - move_slot.shape[1]
    capacity = (move_slot.shape[1] + walker_total - 2) // (walker_total - 1)
    occ_count = chol.shape[1]
    orb_count = chol.shape[2]
    energy_scale = 0.5 / (occ_count * math.sqrt(chol.shape[0] * lax.axis_size("block")))
    active, move_rank = arrival_ranks(move_slot, move_dest)
    own_slots = move_slot[own_index]
    own_dests = move_dest[own_index]
    own_active = active[own_index]
    own_rank = move_rank[own_index]
    peer_ids = jnp.arange(walker_total)
    place_ids = jnp.arange(capacity)
    chosen = (
        (own_dests[None, None, :] == peer_ids[:, None, None])
        & (own_rank[None, None, :] == place_ids[None, :, None])
        & own_active[None, None, :]
    )
    send_slot = jnp.sum(jnp.where(chosen, own_slots[None, None, :], 0), axis=2).reshape(-1)
    present = jnp.any(chosen, axis=2).reshape(-1)
    arrive = jnp.any(
        (move_dest[:, None, :] == own_index)
        & (move_rank[:, None, :] == place_ids[None, :, None])
        & active[:, None, :],
        axis=2,
    ).reshape(-1)
    slot_ids = jnp.arange(slot_total)
    occupied = slot_ids < counts[own_index]
    leaving = jnp.any(own_slots[:, None] == slot_ids[None, :], axis=0)
    staying = occupied & jnp.logical_not(leaving)
    stay_rank = jnp.cumsum(staying.astype(jnp.int32)) - 1
    arrive_rank = jnp.cumsum(arrive.astype(jnp.int32)) - 1
    stay_total = jnp.sum(staying.astype(jnp.int32))
    targets = jnp.arange(keep_total)
    from_stay = jnp.sum(
        jnp.where(
            staying[None, :] & (stay_rank[None, :] == targets[:, None]), slot_ids[None, :], 0
        ),
        axis=1,
    )
    arrive_ids = jnp.arange(arrive.shape[0]) + slot_total
    from_arrive = jnp.sum(
        jnp.where(
            arrive[None, :] & (arrive_rank[None, :] == (targets - stay_total)[:, None]),
            arrive_ids[None, :],
            0,
        ),
        axis=1,
    )
    source_row = jnp.where(targets < stay_total, from_stay, from_arrive)
    outgoing = jnp.where(
        present[:, None], jnp.take(green, send_slot, axis=0), jnp.zeros((), jnp.bfloat16)
    )
    outgoing = outgoing.reshape(walker_total, capacity, share_width)

    def walker_energy(walker_row):
        green_mat = walker_row.reshape(occ_count, orb_count)
        transfer = jnp.einsum("gip,jp->gij", chol, green_mat, preferred_element_type=jnp.float32)
        return jnp.sum(transfer * jnp.swapaxes(transfer, 1, 2))

    got_rows = lax.all_to_all(outgoing, "walker", split_axis=0, concat_axis=0, tiled=True)
    source_pool = jnp.concatenate([green, got_rows.reshape(-1, share_width)], axis=0)
    new_green = jnp.take(source_pool, source_row, axis=0)
    complete = lax.all_gather(new_green, "block", axis=1, tiled=True)
    partial_value = lax.map(walker_energy, complete)
    energy = -energy_scale * lax.psum(partial_value, "block")
    return (new_green, energy)


LANES = 128
ROWS = 8


def spread_slots(green_ref, spread, share_rows):
    slots = green_ref.shape[0]
    tiles = spread.shape[0]
    for row in range(share_rows):
        for tile in range(tiles):
            col = (row * tiles + tile) * LANES
            block = green_ref[:, col : col + LANES].astype(jnp.float32)
            spread[tile, row * ROWS : row * ROWS + slots, :] = block


def pack_kernel(dims, ident_ref, slot_ref, dest_ref, green_ref, *refs):
    slots, share_rows, orb_count, walkers, parts, pad_rows = dims
    part_refs = refs[:parts]
    leave_refs = refs[parts : parts + walkers - 1]
    spread = refs[-1]
    spread_slots(green_ref, spread, share_rows)
    width = orb_count // parts
    for tile in range(orb_count // LANES):
        dense = [spread[tile, pl.ds(slot, share_rows, stride=ROWS), :] for slot in range(slots)]
        if pad_rows > slots * share_rows:
            dense.append(jnp.zeros((pad_rows - slots * share_rows, LANES), jnp.float32))
        part, col = divmod(tile * LANES, width)
        packed = jnp.concatenate(dense, axis=0).astype(jnp.bfloat16)
        part_refs[part][:, col : col + LANES] = packed
    own = ident_ref[0]
    for shift in range(1, walkers):
        target = lax.rem(own + shift, walkers)
        chosen = jnp.int32(0)
        for move in range(slot_ref.shape[1]):
            hit = (dest_ref[own, move] == target) & (slot_ref[own, move] >= 0)
            chosen = jnp.where(hit, slot_ref[own, move], chosen)
        for tile in range(orb_count // LANES):
            row = spread[tile, pl.ds(chosen, share_rows, stride=ROWS), :]
            leave_refs[shift - 1][:, tile * LANES : (tile + 1) * LANES] = row.astype(jnp.bfloat16)


def stay_count(device, slots, count_ref, slot_ref):
    total = count_ref[device]
    for move in range(slot_ref.shape[1]):
        total = total - jnp.where(slot_ref[device, move] >= 0, 1, 0)
    return total


def assemble_kernel(dims, ident_ref, count_ref, slot_ref, dest_ref, green_ref, *refs):
    slots, share_rows, orb_count, walkers, keep = dims
    come_refs = refs[: walkers - 1]
    new_ref, place_ref, spread, pool, out = refs[walkers - 1 :]
    own = ident_ref[0]
    moves = slot_ref.shape[1]
    tiles = orb_count // LANES
    spread_slots(green_ref, spread, share_rows)
    for slot in range(slots):
        for tile in range(tiles):
            pool[
                slot * share_rows : (slot + 1) * share_rows, tile * LANES : (tile + 1) * LANES
            ] = spread[tile, pl.ds(slot, share_rows, stride=ROWS), :]
    for shift in range(1, walkers):
        start = (slots + shift - 1) * share_rows
        pool[start : start + share_rows, :] = come_refs[shift - 1][...].astype(jnp.float32)

    sources = [jnp.int32(0)] * keep
    rank = jnp.int32(0)
    for slot in range(slots):
        live = slot < count_ref[own]
        gone_to = jnp.int32(-1)
        for move in range(moves):
            hit = slot_ref[own, move] == slot
            gone_to = jnp.where(hit, dest_ref[own, move], gone_to)
        stays = live & (gone_to < 0)
        for target in range(keep):
            sources[target] = jnp.where(stays & (rank == target), slot, sources[target])
        there = jnp.maximum(gone_to, 0)
        ahead = stay_count(there, slots, count_ref, slot_ref)
        for device in range(walkers):
            for move in range(moves):
                hit = (
                    (device < own)
                    & (dest_ref[device, move] == there)
                    & (slot_ref[device, move] >= 0)
                )
                ahead = ahead + jnp.where(hit, 1, 0)
        place = jnp.where(stays, own * keep + rank, there * keep + ahead)
        place_ref[slot] = jnp.where(live, place, -1)
        rank = rank + jnp.where(stays, 1, 0)
    for device in range(walkers):
        comes = jnp.bool_(False)
        for move in range(moves):
            comes = comes | ((dest_ref[device, move] == own) & (slot_ref[device, move] >= 0))
        comes = comes & (device != own)
        shift = lax.rem(own - device + walkers, walkers)
        for target in range(keep):
            sources[target] = jnp.where(
                comes & (rank == target), slots + shift - 1, sources[target]
            )
        rank = rank + jnp.where(comes, 1, 0)
    for target in range(keep):
        start = pl.multiple_of(sources[target] * share_rows, ROWS)
        for tile in range(tiles):
            out[tile, pl.ds(target, share_rows, stride=ROWS), :] = pool[
                pl.ds(start, share_rows), tile * LANES : (tile + 1) * LANES
            ]
    for row in range(share_rows):
        for tile in range(tiles):
            col = (row * tiles + tile) * LANES
            new_ref[:, col : col + LANES] = out[
                tile, row * ROWS : row * ROWS + keep, :
            ].astype(jnp.bfloat16)


def energy_kernel(dims, ident_ref, place_ref, chol_ref, *refs):
    slots, share_rows, blocks, parts, group, occ_count, offsets = dims
    count = blocks * parts
    piece_refs = refs[:count]
    sum_ref = refs[count]
    trans, total = refs[count + 1 :]
    low = occ_count - LANES
    step = pl.program_id(0)
    own = ident_ref[0]
    width = piece_refs[0].shape[1]
    pad_rows = piece_refs[0].shape[0]
    chol = chol_ref[...]
    high_rows = [chol[vec, :LANES, :] for vec in range(group)]
    low_rows = [chol[vec, LANES:, :] for vec in range(group)]
    weights = jnp.concatenate(high_rows + low_rows, axis=0)
    result = None
    for part in range(parts):
        left = jnp.concatenate(
            [piece_refs[index * parts + part][...] for index in range(blocks)], axis=0
        )
        right = weights[:, part * width : (part + 1) * width]
        term = lax.dot_general(
            left, right, (((1,), (1,)), ((), ())), preferred_element_type=jnp.float32
        )
        result = term if result is None else result + term
    for index in range(blocks):
        source = jnp.bitwise_xor(own, offsets[index])
        for slot in range(slots):
            start = index * pad_rows + slot * share_rows
            place = pl.multiple_of(slot * occ_count + source * share_rows, ROWS)
            trans[pl.ds(place, share_rows), :] = result[start : start + share_rows, :]

    @pl.when(step == 0)
    def _():
        total[...] = jnp.zeros_like(total)

    cols = lax.broadcasted_iota(jnp.int32, (LANES, LANES), 1)
    rows = lax.broadcasted_iota(jnp.int32, (LANES, LANES), 0)
    same_half = (cols >= low) == (rows >= low)
    for slot in range(slots):
        base = slot * occ_count
        acc = jnp.zeros((LANES, LANES), jnp.float32)
        for vec in range(group):
            high = trans[base : base + LANES, vec * LANES : (vec + 1) * LANES]
            acc = acc + high * high.T
        corners = []
        for pair in range(group // 2):
            col = group * LANES + pair * LANES
            across = trans[base : base + LANES, col : col + LANES]
            below = [
                trans[
                    base + LANES : base + occ_count,
                    (2 * pair + half) * LANES : (2 * pair + half + 1) * LANES,
                ]
                for half in range(2)
            ]
            acc = acc + 2.0 * (jnp.concatenate(below, axis=0) * across.T)
            corners.append(trans[base + LANES : base + occ_count, col : col + LANES])
        for index in range(0, len(corners), 2):
            one = jnp.concatenate([corners[index], corners[index + 1]], axis=0)
            two = jnp.concatenate([corners[index + 1], corners[index]], axis=0)
            acc = acc + jnp.where(same_half, one * one.T + two * two.T, 0.0)
        total[slot * ROWS : (slot + 1) * ROWS, :] += jnp.sum(
            acc.reshape(LANES // ROWS, ROWS, LANES), axis=0
        )

    @pl.when(step == pl.num_programs(0) - 1)
    def _():
        lane = lax.broadcasted_iota(jnp.int32, (ROWS, LANES), 1)
        row = lax.broadcasted_iota(jnp.int32, (ROWS, LANES), 0)
        value = jnp.zeros((ROWS, LANES), jnp.float32)
        for slot in range(slots):
            slot_sum = jnp.sum(total[slot * ROWS : (slot + 1) * ROWS, :])
            hit = (lane == place_ref[slot]) & (row == 0)
            value = jnp.where(hit, slot_sum, value)
        sum_ref[...] = value


def gather_offsets(blocks, order):
    offsets = [0]
    for mask in order:
        offsets = offsets + [offset ^ mask for offset in offsets]
    return offsets


def swap(value, mask, blocks):
    return lax.ppermute(value, "block", [(index, index ^ mask) for index in range(blocks)])


def body(green, chol, counts, move_slot, move_dest):
    walkers = lax.axis_size("walker")
    blocks = lax.axis_size("block")
    slots, share_width = green.shape
    vectors, occ_count, orb_count = chol.shape
    moves = move_slot.shape[1]
    keep = slots - moves
    share_rows = share_width // orb_count
    parts = 2
    width = orb_count // parts
    pad_rows = -(-slots * share_rows // 16) * 16
    walker_index = lax.axis_index("walker").astype(jnp.int32).reshape(1)
    block_index = lax.axis_index("block").astype(jnp.int32).reshape(1)
    smem = pl.BlockSpec(memory_space=pltpu.SMEM)
    vmem = pl.BlockSpec(memory_space=pltpu.VMEM)
    limit = pltpu.CompilerParams(vmem_limit_bytes=32 * 1024 * 1024)

    packed = pl.pallas_call(
        functools.partial(pack_kernel, (slots, share_rows, orb_count, walkers, parts, pad_rows)),
        out_shape=[jax.ShapeDtypeStruct((pad_rows, width), jnp.bfloat16)] * parts
        + [jax.ShapeDtypeStruct((share_rows, orb_count), jnp.bfloat16)] * (walkers - 1),
        in_specs=[smem, smem, smem, vmem],
        out_specs=[vmem] * (parts + walkers - 1),
        scratch_shapes=[pltpu.VMEM((orb_count // LANES, share_rows * ROWS, LANES), jnp.float32)],
        compiler_params=limit,
        name="pack",
    )(walker_index, move_slot, move_dest, green)
    own_parts, leaving = packed[:parts], packed[parts:]

    masks = []
    mask = 2
    while mask < blocks:
        masks.append(mask)
        mask *= 2
    orders = [masks[::-1], masks]
    pieces = {}
    for part in range(parts):
        have = {0: own_parts[part]}
        for mask in orders[part]:
            for offset in list(have):
                have[offset ^ mask] = swap(have[offset], mask, blocks)
        for offset in list(have):
            have[offset ^ 1] = swap(have[offset], 1, blocks)
        for offset, value in have.items():
            pieces[offset, part] = value

    coming = [
        lax.ppermute(
            leaving[shift - 1], "walker", [(z, (z + shift) % walkers) for z in range(walkers)]
        )
        for shift in range(1, walkers)
    ]
    new_green, place = pl.pallas_call(
        functools.partial(assemble_kernel, (slots, share_rows, orb_count, walkers, keep)),
        out_shape=[
            jax.ShapeDtypeStruct((keep, share_width), jnp.bfloat16),
            jax.ShapeDtypeStruct((slots,), jnp.int32),
        ],
        in_specs=[smem] * 4 + [vmem] * walkers,
        out_specs=[vmem, smem],
        scratch_shapes=[
            pltpu.VMEM((orb_count // LANES, share_rows * ROWS, LANES), jnp.float32),
            pltpu.VMEM(((slots + walkers - 1) * share_rows, orb_count), jnp.float32),
            pltpu.VMEM((orb_count // LANES, share_rows * ROWS, LANES), jnp.float32),
        ],
        compiler_params=limit,
        name="assemble",
    )(walker_index, counts, move_slot, move_dest, green, *coming)

    group = 4
    offsets = tuple(range(blocks))
    inputs = [pieces[offset, part] for offset in offsets for part in range(parts)]
    dims = (slots, share_rows, blocks, parts, group, occ_count, offsets)
    sums = pl.pallas_call(
        functools.partial(energy_kernel, dims),
        grid=(vectors // group,),
        out_shape=jax.ShapeDtypeStruct((ROWS, LANES), jnp.float32),
        in_specs=[smem, smem, pl.BlockSpec((group, occ_count, orb_count), lambda g: (g, 0, 0))]
        + [pl.BlockSpec((pad_rows, width), lambda g: (0, 0))] * len(inputs),
        out_specs=pl.BlockSpec((ROWS, LANES), lambda g: (0, 0)),
        scratch_shapes=[
            pltpu.VMEM((slots * occ_count, group * occ_count), jnp.float32),
            pltpu.VMEM((slots * ROWS, LANES), jnp.float32),
        ],
        compiler_params=pltpu.CompilerParams(vmem_limit_bytes=40 * 1024 * 1024),
        cost_estimate=pl.CostEstimate(
            flops=2 * slots * vectors * occ_count * occ_count * orb_count,
            bytes_accessed=2 * chol.size + 2 * blocks * parts * pad_rows * width,
            transcendentals=0,
        ),
        name="energies",
    )(block_index, place, chol, *inputs)

    energy_scale = 0.5 / (occ_count * math.sqrt(vectors * blocks))
    all_sums = lax.psum(sums[0], ("block", "walker"))
    own_sums = lax.dynamic_slice(all_sums, (walker_index[0] * keep,), (keep,))
    return (new_green, -energy_scale * own_sums)


def fits(mesh):
    blocks = mesh.shape["block"]
    walkers = mesh.shape["walker"]

    def check(green, chol, counts, move_slot, move_dest):
        vectors, occ_count, orb_count = chol.shape
        share_width = green.shape[1] // blocks
        moves = move_slot.shape[1]
        slots = green.shape[0] // walkers
        return (
            blocks & (blocks - 1) == 0
            and blocks >= 2
            and walkers >= 2
            and (moves + walkers - 2) // (walkers - 1) == 1
            and slots <= ROWS
            and share_width % (orb_count * ROWS) == 0
            and orb_count % (2 * LANES) == 0
            and occ_count == LANES + LANES // 2
            and (vectors // blocks) % 4 == 0
            and walkers * (slots - moves) <= LANES
        )

    return check


def solution(mesh):
    in_specs = (P("walker", "block"), P("block", None, None), P(), P(), P())
    out_specs = (P("walker", "block"), P("walker"))
    check = fits(mesh)

    def run(*args):
        chosen = body if check(*args) else general_body
        return jax.shard_map(
            chosen, mesh=mesh, in_specs=in_specs, out_specs=out_specs, check_vma=False
        )(*args)

    return run
```

```python
import functools
import math

import jax
import jax.numpy as jnp
from jax import lax
from jax.experimental import pallas as pl
from jax.experimental.pallas import tpu as pltpu
from jax.sharding import PartitionSpec as P


def arrival_ranks(move_slot, move_dest):
    active = move_slot >= 0
    move_total = move_slot.shape[1]
    earlier = jnp.arange(move_total)[None, :] < jnp.arange(move_total)[:, None]
    same_target = (
        (move_dest[:, :, None] == move_dest[:, None, :]) & earlier[None, :, :] & active[:, None, :]
    )
    return (active, jnp.sum(same_target.astype(jnp.int32), axis=2))


def general_body(green, chol, counts, move_slot, move_dest):
    walker_total = lax.axis_size("walker")
    own_index = lax.axis_index("walker")
    slot_total = green.shape[0]
    share_width = green.shape[1]
    keep_total = slot_total - move_slot.shape[1]
    capacity = (move_slot.shape[1] + walker_total - 2) // (walker_total - 1)
    occ_count = chol.shape[1]
    orb_count = chol.shape[2]
    energy_scale = 0.5 / (occ_count * math.sqrt(chol.shape[0] * lax.axis_size("block")))
    active, move_rank = arrival_ranks(move_slot, move_dest)
    own_slots = move_slot[own_index]
    own_dests = move_dest[own_index]
    own_active = active[own_index]
    own_rank = move_rank[own_index]
    peer_ids = jnp.arange(walker_total)
    place_ids = jnp.arange(capacity)
    chosen = (
        (own_dests[None, None, :] == peer_ids[:, None, None])
        & (own_rank[None, None, :] == place_ids[None, :, None])
        & own_active[None, None, :]
    )
    send_slot = jnp.sum(jnp.where(chosen, own_slots[None, None, :], 0), axis=2).reshape(-1)
    present = jnp.any(chosen, axis=2).reshape(-1)
    arrive = jnp.any(
        (move_dest[:, None, :] == own_index)
        & (move_rank[:, None, :] == place_ids[None, :, None])
        & active[:, None, :],
        axis=2,
    ).reshape(-1)
    slot_ids = jnp.arange(slot_total)
    occupied = slot_ids < counts[own_index]
    leaving = jnp.any(own_slots[:, None] == slot_ids[None, :], axis=0)
    staying = occupied & jnp.logical_not(leaving)
    stay_rank = jnp.cumsum(staying.astype(jnp.int32)) - 1
    arrive_rank = jnp.cumsum(arrive.astype(jnp.int32)) - 1
    stay_total = jnp.sum(staying.astype(jnp.int32))
    targets = jnp.arange(keep_total)
    from_stay = jnp.sum(
        jnp.where(
            staying[None, :] & (stay_rank[None, :] == targets[:, None]), slot_ids[None, :], 0
        ),
        axis=1,
    )
    arrive_ids = jnp.arange(arrive.shape[0]) + slot_total
    from_arrive = jnp.sum(
        jnp.where(
            arrive[None, :] & (arrive_rank[None, :] == (targets - stay_total)[:, None]),
            arrive_ids[None, :],
            0,
        ),
        axis=1,
    )
    source_row = jnp.where(targets < stay_total, from_stay, from_arrive)
    outgoing = jnp.where(
        present[:, None], jnp.take(green, send_slot, axis=0), jnp.zeros((), jnp.bfloat16)
    )
    outgoing = outgoing.reshape(walker_total, capacity, share_width)

    def walker_energy(walker_row):
        green_mat = walker_row.reshape(occ_count, orb_count)
        transfer = jnp.einsum("gip,jp->gij", chol, green_mat, preferred_element_type=jnp.float32)
        return jnp.sum(transfer * jnp.swapaxes(transfer, 1, 2))

    got_rows = lax.all_to_all(outgoing, "walker", split_axis=0, concat_axis=0, tiled=True)
    source_pool = jnp.concatenate([green, got_rows.reshape(-1, share_width)], axis=0)
    new_green = jnp.take(source_pool, source_row, axis=0)
    complete = lax.all_gather(new_green, "block", axis=1, tiled=True)
    partial_value = lax.map(walker_energy, complete)
    energy = -energy_scale * lax.psum(partial_value, "block")
    return (new_green, energy)


LANES = 128
ROWS = 8


def spread_slots(green_ref, spread, share_rows):
    slots = green_ref.shape[0]
    tiles = spread.shape[0]
    for row in range(share_rows):
        for tile in range(tiles):
            col = (row * tiles + tile) * LANES
            block = green_ref[:, col : col + LANES].astype(jnp.float32)
            spread[tile, row * ROWS : row * ROWS + slots, :] = block


def pack_kernel(dims, ident_ref, slot_ref, dest_ref, green_ref, *refs):
    slots, share_rows, orb_count, walkers, pad_rows = dims
    own_ref, leave_refs, spread = refs[0], refs[1:-1], refs[-1]
    spread_slots(green_ref, spread, share_rows)
    for tile in range(orb_count // LANES):
        dense = [spread[tile, pl.ds(slot, share_rows, stride=ROWS), :] for slot in range(slots)]
        if pad_rows > slots * share_rows:
            dense.append(jnp.zeros((pad_rows - slots * share_rows, LANES), jnp.float32))
        packed = jnp.concatenate(dense, axis=0).astype(jnp.bfloat16)
        own_ref[:, tile * LANES : (tile + 1) * LANES] = packed
    own = ident_ref[0]
    for shift in range(1, walkers):
        target = lax.rem(own + shift, walkers)
        chosen = jnp.int32(0)
        for move in range(slot_ref.shape[0]):
            hit = (dest_ref[move, own] == target) & (slot_ref[move, own] >= 0)
            chosen = jnp.where(hit, slot_ref[move, own], chosen)
        for tile in range(orb_count // LANES):
            row = spread[tile, pl.ds(chosen, share_rows, stride=ROWS), :]
            leave_refs[shift - 1][:, tile * LANES : (tile + 1) * LANES] = row.astype(jnp.bfloat16)


def stay_count(device, count_ref, slot_ref):
    total = count_ref[device]
    for move in range(slot_ref.shape[0]):
        total = total - jnp.where(slot_ref[move, device] >= 0, 1, 0)
    return total


def find_places(dims, own, count_ref, slot_ref, dest_ref, place_ref):
    slots, walkers, keep = dims
    moves = slot_ref.shape[0]
    rank = jnp.int32(0)
    for slot in range(slots):
        live = slot < count_ref[own]
        gone_to = jnp.int32(-1)
        for move in range(moves):
            gone_to = jnp.where(slot_ref[move, own] == slot, dest_ref[move, own], gone_to)
        stays = live & (gone_to < 0)
        there = jnp.maximum(gone_to, 0)
        ahead = stay_count(there, count_ref, slot_ref)
        for device in range(walkers):
            for move in range(moves):
                hit = (
                    (device < own)
                    & (dest_ref[move, device] == there)
                    & (slot_ref[move, device] >= 0)
                )
                ahead = ahead + jnp.where(hit, 1, 0)
        place = jnp.where(stays, own * keep + rank, there * keep + ahead)
        place_ref[slot] = jnp.where(live, place, -1)
        rank = rank + jnp.where(stays, 1, 0)


def assemble_kernel(dims, ident_ref, count_ref, slot_ref, dest_ref, green_ref, *refs):
    slots, share_rows, orb_count, walkers, keep = dims
    come_refs = refs[: walkers - 1]
    new_ref, spread, pool, out = refs[walkers - 1 :]
    own = ident_ref[0]
    moves = slot_ref.shape[0]
    tiles = orb_count // LANES
    spread_slots(green_ref, spread, share_rows)
    for slot in range(slots):
        for tile in range(tiles):
            pool[
                slot * share_rows : (slot + 1) * share_rows, tile * LANES : (tile + 1) * LANES
            ] = spread[tile, pl.ds(slot, share_rows, stride=ROWS), :]
    for shift in range(1, walkers):
        start = (slots + shift - 1) * share_rows
        pool[start : start + share_rows, :] = come_refs[shift - 1][...].astype(jnp.float32)

    sources = [jnp.int32(0)] * keep
    rank = jnp.int32(0)
    for slot in range(slots):
        live = slot < count_ref[own]
        gone_to = jnp.int32(-1)
        for move in range(moves):
            hit = slot_ref[move, own] == slot
            gone_to = jnp.where(hit, dest_ref[move, own], gone_to)
        stays = live & (gone_to < 0)
        for target in range(keep):
            sources[target] = jnp.where(stays & (rank == target), slot, sources[target])
        rank = rank + jnp.where(stays, 1, 0)
    for device in range(walkers):
        comes = jnp.bool_(False)
        for move in range(moves):
            comes = comes | ((dest_ref[move, device] == own) & (slot_ref[move, device] >= 0))
        comes = comes & (device != own)
        shift = lax.rem(own - device + walkers, walkers)
        for target in range(keep):
            sources[target] = jnp.where(
                comes & (rank == target), slots + shift - 1, sources[target]
            )
        rank = rank + jnp.where(comes, 1, 0)
    for target in range(keep):
        start = pl.multiple_of(sources[target] * share_rows, ROWS)
        for tile in range(tiles):
            out[tile, pl.ds(target, share_rows, stride=ROWS), :] = pool[
                pl.ds(start, share_rows), tile * LANES : (tile + 1) * LANES
            ]
    for row in range(share_rows):
        for tile in range(tiles):
            col = (row * tiles + tile) * LANES
            new_ref[:, col : col + LANES] = out[
                tile, row * ROWS : row * ROWS + keep, :
            ].astype(jnp.bfloat16)


def order_kernel(
    dims, ident_ref, index_ref, count_ref, slot_ref, dest_ref, chol_ref, own_ref, out_ref, place_ref, sems
):
    del own_ref
    group, groups, chip_rows, place_dims = dims
    chip = ident_ref[0] // 2
    edge = LANES - 2 * chip_rows
    rest = 2 * chip_rows - edge
    copies = []

    def add(vec, distance, start, size, place):
        row = pl.multiple_of(jnp.bitwise_xor(chip, distance) * chip_rows + start, 16)
        copies.append(
            pltpu.make_async_copy(
                chol_ref.at[vec, pl.ds(row, size), :],
                out_ref.at[pl.ds(place, size), :],
                sems.at[len(copies)],
            )
        )

    for index in range(groups):
        for item in range(group):
            vec = index * group + item
            place = index * group * 4 * chip_rows + item * LANES
            add(vec, 0, 0, chip_rows, place)
            add(vec, 1, 0, chip_rows, place + chip_rows)
            add(vec, 2, 0, edge, place + 2 * chip_rows)
            place = index * group * 4 * chip_rows + group * LANES + item * rest
            add(vec, 2, edge, chip_rows - edge, place)
            add(vec, 3, 0, chip_rows, place + chip_rows - edge)
    for copy in copies:
        copy.start()
    find_places(place_dims, index_ref[0], count_ref, slot_ref, dest_ref, place_ref)
    for copy in copies:
        copy.wait()


def times(left, right):
    return lax.dot_general(
        left, right, (((1,), (1,)), ((), ())), preferred_element_type=jnp.float32
    )


def near_kernel(dims, ident_ref, weight_ref, *refs):
    slots, share_rows, group, groups, chip_rows = dims
    piece_refs = refs[:6]
    sum_ref, late_ref = refs[6:8]
    trans_refs = refs[8:]
    own = ident_ref[0]
    core = lax.rem(own, 2)
    pad_rows = piece_refs[0].shape[0]
    near = 3 * chip_rows
    size = 4 * chip_rows * group
    edge = near - LANES
    half = LANES // 2
    left = jnp.concatenate([ref[...] for ref in piece_refs], axis=0)
    lane = lax.broadcasted_iota(jnp.int32, (1, LANES), 1)
    low_half = lane < half
    in_edge = jnp.where(low_half, lane, lane - half) < edge
    sums = [jnp.zeros((ROWS, LANES), jnp.float32) for _ in range(slots)]

    def fold(value):
        return jnp.sum(value.reshape(-1, ROWS, LANES), axis=0)

    for index in range(groups):
        trans = trans_refs[index]
        result = times(left, weight_ref[index * size : (index + 1) * size, :])
        for piece in range(6):
            source = jnp.bitwise_xor(core, piece % 2)
            for slot in range(slots):
                start = piece * pad_rows + slot * share_rows
                place = slot * near + (piece // 2) * chip_rows + source * share_rows
                trans[pl.ds(pl.multiple_of(place, ROWS), share_rows), :] = result[
                    start : start + share_rows, :
                ]
        for slot in range(slots):
            base = slot * near
            late = slice(slot * chip_rows, (slot + 1) * chip_rows)
            acc = sums[slot]
            for pair in range(group // 2):
                col = (group + pair) * LANES
                top = trans[base : base + LANES, col : col + LANES].T
                edge_rows = trans[base + LANES : base + near, col : col + LANES]
                gap = jnp.zeros((half - edge, LANES), jnp.float32)
                bottom = jnp.concatenate([edge_rows, gap, edge_rows, gap], axis=0).T
                for side in range(2):
                    vec = 2 * pair + side
                    high = trans[base : base + LANES, vec * LANES : (vec + 1) * LANES]
                    acc = acc + fold(high * high.T)
                    across = trans[base + LANES : base + near, vec * LANES : (vec + 1) * LANES]
                    acc = acc + 2.0 * fold(across * top[side * half : side * half + edge, :])
                    late_ref[
                        late, (index * (group + group // 2) + vec) * LANES : (
                            index * (group + group // 2) + vec + 1
                        ) * LANES
                    ] = top[side * half + edge : (side + 1) * half, :]
                corner = jnp.where(low_half, bottom[:edge, :], bottom[half : half + edge, :])
                acc = acc + fold(jnp.where(in_edge, edge_rows * corner, 0.0))
                rest = jnp.where(low_half, bottom[edge:half, :], bottom[half + edge :, :])
                place = (index * (group + group // 2) + group + pair) * LANES
                late_ref[late, place : place + LANES] = jnp.where(in_edge, rest, 0.0)
            sums[slot] = acc
    sum_ref[...] = jnp.concatenate(sums, axis=0)


def far_kernel(dims, ident_ref, place_ref, weight_ref, near_sum_ref, late_ref, *refs):
    slots, share_rows, group, groups, chip_rows = dims
    piece_refs = refs[:4]
    sum_ref = refs[4]
    trans_refs = refs[5:]
    own = ident_ref[0]
    core = lax.rem(own, 2)
    pad_rows, width = piece_refs[0].shape
    half = LANES // 2
    edge = half - chip_rows
    size = 4 * chip_rows * group
    lane = lax.broadcasted_iota(jnp.int32, (1, LANES), 1)
    low_half = lane < half
    in_rest = jnp.where(low_half, lane, lane - half) >= edge
    lefts = [
        jnp.concatenate([piece_refs[part][...], piece_refs[2 + part][...]], axis=0)
        for part in range(2)
    ]
    twice = [jnp.zeros((ROWS, LANES), jnp.float32) for _ in range(slots)]
    once = [near_sum_ref[slot * ROWS : (slot + 1) * ROWS, :] for slot in range(slots)]

    def fold(value):
        return jnp.sum(value.reshape(-1, ROWS, LANES), axis=0)

    tiles = group + group // 2
    for index in range(groups):
        trans = trans_refs[index]
        rows = slice(index * size, (index + 1) * size)
        result = times(lefts[0], weight_ref[rows, :width])
        result = result + times(lefts[1], weight_ref[rows, width:])
        for piece in range(2):
            source = jnp.bitwise_xor(core, piece)
            for slot in range(slots):
                start = piece * pad_rows + slot * share_rows
                place = slot * chip_rows + source * share_rows
                trans[pl.ds(pl.multiple_of(place, ROWS), share_rows), :] = result[
                    start : start + share_rows, :
                ]
        for slot in range(slots):
            rows = slice(slot * chip_rows, (slot + 1) * chip_rows)
            for tile in range(tiles):
                here = trans[rows, tile * LANES : (tile + 1) * LANES]
                met = late_ref[rows, (index * tiles + tile) * LANES : (index * tiles + tile + 1) * LANES]
                twice[slot] = twice[slot] + fold(here * met)
                if tile >= group:
                    gap = jnp.zeros((edge, LANES), jnp.float32)
                    turned = jnp.concatenate([gap, here, gap, here], axis=0).T
                    corner = jnp.where(low_half, turned[edge:half, :], turned[half + edge :, :])
                    once[slot] = once[slot] + fold(jnp.where(in_rest, here * corner, 0.0))
    value = jnp.zeros((1, LANES), jnp.float32)
    for slot in range(slots):
        slot_sum = jnp.sum(once[slot] + 2.0 * twice[slot])
        value = jnp.where(lane == place_ref[slot], slot_sum, value)
    sum_ref[...] = value


def swap(value, mask, blocks):
    return lax.ppermute(value, "block", [(index, index ^ mask) for index in range(blocks)])


def body(green, chol, counts, move_slot, move_dest):
    walkers = lax.axis_size("walker")
    blocks = lax.axis_size("block")
    slots, share_width = green.shape
    vectors, occ_count, orb_count = chol.shape
    moves = move_slot.shape[1]
    keep = slots - moves
    share_rows = share_width // orb_count
    pad_rows = -(-slots * share_rows // 16) * 16
    slots_by_move, dests_by_move = move_slot.T, move_dest.T
    walker_index = lax.axis_index("walker").astype(jnp.int32).reshape(1)
    block_index = lax.axis_index("block").astype(jnp.int32).reshape(1)
    smem = pl.BlockSpec(memory_space=pltpu.SMEM)
    vmem = pl.BlockSpec(memory_space=pltpu.VMEM)
    limit = pltpu.CompilerParams(vmem_limit_bytes=32 * 1024 * 1024)

    packed = pl.pallas_call(
        functools.partial(pack_kernel, (slots, share_rows, orb_count, walkers, pad_rows)),
        out_shape=[jax.ShapeDtypeStruct((pad_rows, orb_count), jnp.bfloat16)]
        + [jax.ShapeDtypeStruct((share_rows, orb_count), jnp.bfloat16)] * (walkers - 1),
        in_specs=[smem, smem, smem, vmem],
        out_specs=[vmem] * walkers,
        scratch_shapes=[pltpu.VMEM((orb_count // LANES, share_rows * ROWS, LANES), jnp.float32)],
        compiler_params=limit,
        name="pack",
    )(walker_index, slots_by_move, dests_by_move, green)
    own_rows, leaving = packed[0], packed[1:]

    group = 4
    groups = vectors // group
    chip_rows = 2 * share_rows
    weights, place = pl.pallas_call(
        functools.partial(order_kernel, (group, groups, chip_rows, (slots, walkers, keep))),
        out_shape=[
            jax.ShapeDtypeStruct((vectors * occ_count, orb_count), jnp.bfloat16),
            jax.ShapeDtypeStruct((slots,), jnp.int32),
        ],
        in_specs=[smem] * 5 + [pl.BlockSpec(memory_space=pl.ANY)] * 2,
        out_specs=[vmem, smem],
        scratch_shapes=[pltpu.SemaphoreType.DMA((5 * vectors,))],
        compiler_params=limit,
        cost_estimate=pl.CostEstimate(
            flops=0, bytes_accessed=4 * chol.size, transcendentals=0
        ),
        name="order",
    )(block_index, walker_index, counts, slots_by_move, dests_by_move, chol, own_rows)

    core, near_x, near_y = 1, 2, 4
    from_x = swap(own_rows, near_x, blocks)
    from_y = swap(own_rows, near_y, blocks)
    from_core = swap(own_rows, core, blocks)
    width = orb_count // 2
    from_x, from_y, weights = lax.optimization_barrier((from_x, from_y, weights))
    far = [swap(from_y[:, :width], near_x, blocks), swap(from_x[:, width:], near_y, blocks)]
    near_pieces = [own_rows, from_core]
    for piece in (from_x, from_y):
        near_pieces += [piece, swap(piece, core, blocks)]

    coming = [
        lax.ppermute(
            leaving[shift - 1], "walker", [(z, (z + shift) % walkers) for z in range(walkers)]
        )
        for shift in range(1, walkers)
    ]
    dims = (slots, share_rows, group, groups, chip_rows)
    work = 2 * vectors * occ_count * orb_count * pad_rows
    near_sums, late = pl.pallas_call(
        functools.partial(near_kernel, dims),
        out_shape=[
            jax.ShapeDtypeStruct((slots * ROWS, LANES), jnp.float32),
            jax.ShapeDtypeStruct((slots * chip_rows, vectors * occ_count), jnp.float32),
        ],
        in_specs=[smem] + [vmem] * 7,
        out_specs=[vmem] * 2,
        scratch_shapes=[pltpu.VMEM((slots * 3 * chip_rows, group * occ_count), jnp.float32)]
        * groups,
        compiler_params=limit,
        cost_estimate=pl.CostEstimate(
            flops=6 * work, bytes_accessed=2 * chol.size, transcendentals=0
        ),
        name="near",
    )(block_index, weights, *near_pieces)
    far, near_sums = lax.optimization_barrier((far, near_sums))
    far_pieces = far + [swap(piece, core, blocks) for piece in far]
    all_sums = pl.pallas_call(
        functools.partial(far_kernel, dims),
        out_shape=jax.ShapeDtypeStruct((1, LANES), jnp.float32),
        in_specs=[smem] * 2 + [vmem] * 7,
        out_specs=vmem,
        scratch_shapes=[pltpu.VMEM((slots * chip_rows, group * occ_count), jnp.float32)] * groups,
        compiler_params=limit,
        cost_estimate=pl.CostEstimate(
            flops=2 * work, bytes_accessed=2 * chol.size, transcendentals=0
        ),
        name="far",
    )(block_index, place, weights, near_sums, late, *far_pieces)

    coming, _ = lax.optimization_barrier((coming, all_sums))
    new_green = pl.pallas_call(
        functools.partial(assemble_kernel, (slots, share_rows, orb_count, walkers, keep)),
        out_shape=jax.ShapeDtypeStruct((keep, share_width), jnp.bfloat16),
        in_specs=[smem] * 4 + [vmem] * walkers,
        out_specs=vmem,
        scratch_shapes=[
            pltpu.VMEM((orb_count // LANES, share_rows * ROWS, LANES), jnp.float32),
            pltpu.VMEM(((slots + walkers - 1) * share_rows, orb_count), jnp.float32),
            pltpu.VMEM((orb_count // LANES, share_rows * ROWS, LANES), jnp.float32),
        ],
        compiler_params=limit,
        name="assemble",
    )(walker_index, counts, slots_by_move, dests_by_move, green, *coming)

    energy_scale = 0.5 / (occ_count * math.sqrt(vectors * blocks))
    for mask in (core, near_x, near_y):
        all_sums = all_sums + swap(all_sums, mask, blocks)
    mask = 1
    while mask < walkers:
        pairs = [(index, index ^ mask) for index in range(walkers)]
        all_sums = all_sums + lax.ppermute(all_sums, "walker", pairs)
        mask *= 2
    own_sums = lax.dynamic_slice(all_sums[0], (walker_index[0] * keep,), (keep,))
    return (new_green, -energy_scale * own_sums)


def fits(mesh):
    blocks = mesh.shape["block"]
    walkers = mesh.shape["walker"]

    def check(green, chol, counts, move_slot, move_dest):
        vectors, occ_count, orb_count = chol.shape
        share_width = green.shape[1] // blocks
        moves = move_slot.shape[1]
        slots = green.shape[0] // walkers
        return (
            blocks == 8
            and walkers >= 2
            and walkers & (walkers - 1) == 0
            and (moves + walkers - 2) // (walkers - 1) == 1
            and slots <= ROWS
            and share_width % (orb_count * ROWS) == 0
            and orb_count % (2 * LANES) == 0
            and occ_count == blocks * (share_width // orb_count)
            and occ_count == LANES + LANES // 2
            and (vectors // blocks) % 4 == 0
            and walkers * (slots - moves) <= LANES
        )

    return check


def solution(mesh):
    in_specs = (P("walker", "block"), P("block", None, None), P(), P(), P())
    out_specs = (P("walker", "block"), P("walker"))
    check = fits(mesh)

    def run(*args):
        chosen = body if check(*args) else general_body
        return jax.shard_map(
            chosen, mesh=mesh, in_specs=in_specs, out_specs=out_specs, check_vma=False
        )(*args)

    return run
```

```python
import functools
import math

import jax
import jax.numpy as jnp
from jax import lax
from jax.experimental import pallas as pl
from jax.experimental.pallas import tpu as pltpu
from jax.sharding import PartitionSpec as P


def arrival_ranks(move_slot, move_dest):
    active = move_slot >= 0
    move_total = move_slot.shape[1]
    earlier = jnp.arange(move_total)[None, :] < jnp.arange(move_total)[:, None]
    same_target = (
        (move_dest[:, :, None] == move_dest[:, None, :]) & earlier[None, :, :] & active[:, None, :]
    )
    return (active, jnp.sum(same_target.astype(jnp.int32), axis=2))


def general_body(green, chol, counts, move_slot, move_dest):
    walker_total = lax.axis_size("walker")
    own_index = lax.axis_index("walker")
    slot_total = green.shape[0]
    share_width = green.shape[1]
    keep_total = slot_total - move_slot.shape[1]
    capacity = (move_slot.shape[1] + walker_total - 2) // (walker_total - 1)
    occ_count = chol.shape[1]
    orb_count = chol.shape[2]
    energy_scale = 0.5 / (occ_count * math.sqrt(chol.shape[0] * lax.axis_size("block")))
    active, move_rank = arrival_ranks(move_slot, move_dest)
    own_slots = move_slot[own_index]
    own_dests = move_dest[own_index]
    own_active = active[own_index]
    own_rank = move_rank[own_index]
    peer_ids = jnp.arange(walker_total)
    place_ids = jnp.arange(capacity)
    chosen = (
        (own_dests[None, None, :] == peer_ids[:, None, None])
        & (own_rank[None, None, :] == place_ids[None, :, None])
        & own_active[None, None, :]
    )
    send_slot = jnp.sum(jnp.where(chosen, own_slots[None, None, :], 0), axis=2).reshape(-1)
    present = jnp.any(chosen, axis=2).reshape(-1)
    arrive = jnp.any(
        (move_dest[:, None, :] == own_index)
        & (move_rank[:, None, :] == place_ids[None, :, None])
        & active[:, None, :],
        axis=2,
    ).reshape(-1)
    slot_ids = jnp.arange(slot_total)
    occupied = slot_ids < counts[own_index]
    leaving = jnp.any(own_slots[:, None] == slot_ids[None, :], axis=0)
    staying = occupied & jnp.logical_not(leaving)
    stay_rank = jnp.cumsum(staying.astype(jnp.int32)) - 1
    arrive_rank = jnp.cumsum(arrive.astype(jnp.int32)) - 1
    stay_total = jnp.sum(staying.astype(jnp.int32))
    targets = jnp.arange(keep_total)
    from_stay = jnp.sum(
        jnp.where(
            staying[None, :] & (stay_rank[None, :] == targets[:, None]), slot_ids[None, :], 0
        ),
        axis=1,
    )
    arrive_ids = jnp.arange(arrive.shape[0]) + slot_total
    from_arrive = jnp.sum(
        jnp.where(
            arrive[None, :] & (arrive_rank[None, :] == (targets - stay_total)[:, None]),
            arrive_ids[None, :],
            0,
        ),
        axis=1,
    )
    source_row = jnp.where(targets < stay_total, from_stay, from_arrive)
    outgoing = jnp.where(
        present[:, None], jnp.take(green, send_slot, axis=0), jnp.zeros((), jnp.bfloat16)
    )
    outgoing = outgoing.reshape(walker_total, capacity, share_width)

    def walker_energy(walker_row):
        green_mat = walker_row.reshape(occ_count, orb_count)
        transfer = jnp.einsum("gip,jp->gij", chol, green_mat, preferred_element_type=jnp.float32)
        return jnp.sum(transfer * jnp.swapaxes(transfer, 1, 2))

    got_rows = lax.all_to_all(outgoing, "walker", split_axis=0, concat_axis=0, tiled=True)
    source_pool = jnp.concatenate([green, got_rows.reshape(-1, share_width)], axis=0)
    new_green = jnp.take(source_pool, source_row, axis=0)
    complete = lax.all_gather(new_green, "block", axis=1, tiled=True)
    partial_value = lax.map(walker_energy, complete)
    energy = -energy_scale * lax.psum(partial_value, "block")
    return (new_green, energy)


LANES = 128
ROWS = 8


def spread_slots(green_ref, spread, share_rows):
    slots = green_ref.shape[0]
    tiles = spread.shape[0]
    for row in range(share_rows):
        for tile in range(tiles):
            col = (row * tiles + tile) * LANES
            block = green_ref[:, col : col + LANES].astype(jnp.float32)
            spread[tile, row * ROWS : row * ROWS + slots, :] = block


def pack_kernel(dims, green_ref, own_ref, spread):
    slots, share_rows, orb_count, pad_rows = dims
    spread_slots(green_ref, spread, share_rows)
    for tile in range(orb_count // LANES):
        dense = [spread[tile, pl.ds(slot, share_rows, stride=ROWS), :] for slot in range(slots)]
        if pad_rows > slots * share_rows:
            dense.append(jnp.zeros((pad_rows - slots * share_rows, LANES), jnp.float32))
        packed = jnp.concatenate(dense, axis=0).astype(jnp.bfloat16)
        own_ref[:, tile * LANES : (tile + 1) * LANES] = packed


class Moves:
    def __init__(self, table_ref, moves):
        self.table, self.moves = table_ref, moves

    def count(self, device):
        return self.table[0, device]

    def slot(self, device, move):
        return self.table[1 + move, device]

    def dest(self, device, move):
        return self.table[1 + self.moves + move, device]

    def staying(self, device):
        total = self.count(device)
        for move in range(self.moves):
            total = total - jnp.where(self.slot(device, move) >= 0, 1, 0)
        return total

    def goes_to(self, own, slot):
        target = jnp.int32(-1)
        for move in range(self.moves):
            target = jnp.where(self.slot(own, move) == slot, self.dest(own, move), target)
        return target


def leave_kernel(dims, ident_ref, table_ref, own_ref, *refs):
    slots, share_rows, orb_count, walkers, moves, keep = dims
    leave_refs, place_ref, wide = refs[:-2], refs[-2], refs[-1]
    table = Moves(table_ref, moves)
    wide[...] = own_ref[...].astype(jnp.float32)
    own = ident_ref[0]
    for shift in range(1, walkers):
        target = lax.rem(own + shift, walkers)
        chosen = jnp.int32(0)
        for move in range(moves):
            hit = (table.dest(own, move) == target) & (table.slot(own, move) >= 0)
            chosen = jnp.where(hit, table.slot(own, move), chosen)
        start = pl.multiple_of(chosen * share_rows, ROWS)
        leave_refs[shift - 1][...] = wide[pl.ds(start, share_rows), :].astype(jnp.bfloat16)
    rank = jnp.int32(0)
    for slot in range(slots):
        live = slot < table.count(own)
        gone_to = table.goes_to(own, slot)
        stays = live & (gone_to < 0)
        there = jnp.maximum(gone_to, 0)
        ahead = table.staying(there)
        for device in range(walkers):
            for move in range(moves):
                hit = (
                    (device < own)
                    & (table.dest(device, move) == there)
                    & (table.slot(device, move) >= 0)
                )
                ahead = ahead + jnp.where(hit, 1, 0)
        place = jnp.where(stays, own * keep + rank, there * keep + ahead)
        place_ref[slot] = jnp.where(live, place, -1)
        rank = rank + jnp.where(stays, 1, 0)


def assemble_kernel(dims, ident_ref, table_ref, green_ref, *refs):
    slots, share_rows, orb_count, walkers, moves, keep = dims
    table = Moves(table_ref, moves)
    come_refs = refs[: walkers - 1]
    new_ref, spread, pool, out = refs[walkers - 1 :]
    own = ident_ref[0]
    tiles = orb_count // LANES
    spread_slots(green_ref, spread, share_rows)
    for slot in range(slots):
        for tile in range(tiles):
            pool[
                slot * share_rows : (slot + 1) * share_rows, tile * LANES : (tile + 1) * LANES
            ] = spread[tile, pl.ds(slot, share_rows, stride=ROWS), :]
    for shift in range(1, walkers):
        start = (slots + shift - 1) * share_rows
        pool[start : start + share_rows, :] = come_refs[shift - 1][...].astype(jnp.float32)

    sources = [jnp.int32(0)] * keep
    rank = jnp.int32(0)
    for slot in range(slots):
        stays = (slot < table.count(own)) & (table.goes_to(own, slot) < 0)
        for target in range(keep):
            sources[target] = jnp.where(stays & (rank == target), slot, sources[target])
        rank = rank + jnp.where(stays, 1, 0)
    for device in range(walkers):
        comes = jnp.bool_(False)
        for move in range(moves):
            comes = comes | ((table.dest(device, move) == own) & (table.slot(device, move) >= 0))
        comes = comes & (device != own)
        shift = lax.rem(own - device + walkers, walkers)
        for target in range(keep):
            sources[target] = jnp.where(
                comes & (rank == target), slots + shift - 1, sources[target]
            )
        rank = rank + jnp.where(comes, 1, 0)
    for target in range(keep):
        start = pl.multiple_of(sources[target] * share_rows, ROWS)
        for tile in range(tiles):
            out[tile, pl.ds(target, share_rows, stride=ROWS), :] = pool[
                pl.ds(start, share_rows), tile * LANES : (tile + 1) * LANES
            ]
    for row in range(share_rows):
        for tile in range(tiles):
            col = (row * tiles + tile) * LANES
            new_ref[:, col : col + LANES] = out[
                tile, row * ROWS : row * ROWS + keep, :
            ].astype(jnp.bfloat16)


def order_kernel(dims, ident_ref, chol_ref, own_ref, out_ref, sems):
    del own_ref
    group, groups, chip_rows = dims
    chip = ident_ref[0] // 2
    edge = LANES - 2 * chip_rows
    rest = 2 * chip_rows - edge
    copies = []

    def add(vec, distance, start, size, place):
        row = pl.multiple_of(jnp.bitwise_xor(chip, distance) * chip_rows + start, 16)
        copies.append(
            pltpu.make_async_copy(
                chol_ref.at[vec, pl.ds(row, size), :],
                out_ref.at[pl.ds(place, size), :],
                sems.at[len(copies)],
            )
        )

    for index in range(groups):
        for item in range(group):
            vec = index * group + item
            place = index * group * 4 * chip_rows + item * LANES
            add(vec, 0, 0, chip_rows, place)
            add(vec, 1, 0, chip_rows, place + chip_rows)
            add(vec, 2, 0, edge, place + 2 * chip_rows)
            place = index * group * 4 * chip_rows + group * LANES + item * rest
            add(vec, 2, edge, chip_rows - edge, place)
            add(vec, 3, 0, chip_rows, place + chip_rows - edge)
    for copy in copies:
        copy.start()
    for copy in copies:
        copy.wait()


def times(left, right):
    return lax.dot_general(
        left, right, (((1,), (1,)), ((), ())), preferred_element_type=jnp.float32
    )


def near_kernel(dims, ident_ref, weight_ref, *refs):
    slots, share_rows, group, groups, chip_rows = dims
    piece_refs = refs[:6]
    sum_ref, late_ref = refs[6:8]
    trans_refs = refs[8:]
    own = ident_ref[0]
    core = lax.rem(own, 2)
    pad_rows = piece_refs[0].shape[0]
    near = 3 * chip_rows
    size = 4 * chip_rows * group
    edge = near - LANES
    half = LANES // 2
    left = jnp.concatenate([ref[...] for ref in piece_refs], axis=0)
    lane = lax.broadcasted_iota(jnp.int32, (1, LANES), 1)
    low_half = lane < half
    in_edge = jnp.where(low_half, lane, lane - half) < edge
    sums = [jnp.zeros((ROWS, LANES), jnp.float32) for _ in range(slots)]

    def fold(value):
        return jnp.sum(value.reshape(-1, ROWS, LANES), axis=0)

    for index in range(groups):
        trans = trans_refs[index]
        result = times(left, weight_ref[index * size : (index + 1) * size, :])
        for piece in range(6):
            source = jnp.bitwise_xor(core, piece % 2)
            for slot in range(slots):
                start = piece * pad_rows + slot * share_rows
                place = slot * near + (piece // 2) * chip_rows + source * share_rows
                trans[pl.ds(pl.multiple_of(place, ROWS), share_rows), :] = result[
                    start : start + share_rows, :
                ]
        for slot in range(slots):
            base = slot * near
            late = slice(slot * chip_rows, (slot + 1) * chip_rows)
            acc = sums[slot]
            for pair in range(group // 2):
                col = (group + pair) * LANES
                top = trans[base : base + LANES, col : col + LANES].T
                edge_rows = trans[base + LANES : base + near, col : col + LANES]
                gap = jnp.zeros((half - edge, LANES), jnp.float32)
                bottom = jnp.concatenate([edge_rows, gap, edge_rows, gap], axis=0).T
                for side in range(2):
                    vec = 2 * pair + side
                    high = trans[base : base + LANES, vec * LANES : (vec + 1) * LANES]
                    acc = acc + fold(high * high.T)
                    across = trans[base + LANES : base + near, vec * LANES : (vec + 1) * LANES]
                    acc = acc + 2.0 * fold(across * top[side * half : side * half + edge, :])
                    late_ref[
                        late, (index * (group + group // 2) + vec) * LANES : (
                            index * (group + group // 2) + vec + 1
                        ) * LANES
                    ] = top[side * half + edge : (side + 1) * half, :]
                corner = jnp.where(low_half, bottom[:edge, :], bottom[half : half + edge, :])
                acc = acc + fold(jnp.where(in_edge, edge_rows * corner, 0.0))
                rest = jnp.where(low_half, bottom[edge:half, :], bottom[half + edge :, :])
                place = (index * (group + group // 2) + group + pair) * LANES
                late_ref[late, place : place + LANES] = jnp.where(in_edge, rest, 0.0)
            sums[slot] = acc
    sum_ref[...] = jnp.concatenate(sums, axis=0)


def far_kernel(dims, ident_ref, place_ref, weight_ref, near_sum_ref, late_ref, *refs):
    slots, share_rows, group, groups, chip_rows = dims
    piece_refs = refs[:4]
    sum_ref = refs[4]
    trans_refs = refs[5:]
    own = ident_ref[0]
    core = lax.rem(own, 2)
    pad_rows, width = piece_refs[0].shape
    half = LANES // 2
    edge = half - chip_rows
    size = 4 * chip_rows * group
    lane = lax.broadcasted_iota(jnp.int32, (1, LANES), 1)
    low_half = lane < half
    in_rest = jnp.where(low_half, lane, lane - half) >= edge
    lefts = [
        jnp.concatenate([piece_refs[part][...], piece_refs[2 + part][...]], axis=0)
        for part in range(2)
    ]
    twice = [jnp.zeros((ROWS, LANES), jnp.float32) for _ in range(slots)]
    once = [near_sum_ref[slot * ROWS : (slot + 1) * ROWS, :] for slot in range(slots)]

    def fold(value):
        return jnp.sum(value.reshape(-1, ROWS, LANES), axis=0)

    tiles = group + group // 2
    for index in range(groups):
        trans = trans_refs[index]
        rows = slice(index * size, (index + 1) * size)
        result = times(lefts[0], weight_ref[rows, :width])
        result = result + times(lefts[1], weight_ref[rows, width:])
        for piece in range(2):
            source = jnp.bitwise_xor(core, piece)
            for slot in range(slots):
                start = piece * pad_rows + slot * share_rows
                place = slot * chip_rows + source * share_rows
                trans[pl.ds(pl.multiple_of(place, ROWS), share_rows), :] = result[
                    start : start + share_rows, :
                ]
        for slot in range(slots):
            rows = slice(slot * chip_rows, (slot + 1) * chip_rows)
            for tile in range(tiles):
                here = trans[rows, tile * LANES : (tile + 1) * LANES]
                met = late_ref[rows, (index * tiles + tile) * LANES : (index * tiles + tile + 1) * LANES]
                twice[slot] = twice[slot] + fold(here * met)
                if tile >= group:
                    gap = jnp.zeros((edge, LANES), jnp.float32)
                    turned = jnp.concatenate([gap, here, gap, here], axis=0).T
                    corner = jnp.where(low_half, turned[edge:half, :], turned[half + edge :, :])
                    once[slot] = once[slot] + fold(jnp.where(in_rest, here * corner, 0.0))
    value = jnp.zeros((1, LANES), jnp.float32)
    for slot in range(slots):
        slot_sum = jnp.sum(once[slot] + 2.0 * twice[slot])
        value = jnp.where(lane == place_ref[slot], slot_sum, value)
    sum_ref[...] = value


def swap(value, mask, blocks):
    return lax.ppermute(value, "block", [(index, index ^ mask) for index in range(blocks)])


def body(green, chol, counts, move_slot, move_dest):
    walkers = lax.axis_size("walker")
    blocks = lax.axis_size("block")
    slots, share_width = green.shape
    vectors, occ_count, orb_count = chol.shape
    moves = move_slot.shape[1]
    keep = slots - moves
    share_rows = share_width // orb_count
    pad_rows = -(-slots * share_rows // 16) * 16
    table = jnp.concatenate([counts[None, :], move_slot.T, move_dest.T], axis=0)
    walker_index = lax.axis_index("walker").astype(jnp.int32).reshape(1)
    block_index = lax.axis_index("block").astype(jnp.int32).reshape(1)
    smem = pl.BlockSpec(memory_space=pltpu.SMEM)
    vmem = pl.BlockSpec(memory_space=pltpu.VMEM)
    limit = pltpu.CompilerParams(vmem_limit_bytes=32 * 1024 * 1024)

    spread = pltpu.VMEM((orb_count // LANES, share_rows * ROWS, LANES), jnp.float32)
    own_rows = pl.pallas_call(
        functools.partial(pack_kernel, (slots, share_rows, orb_count, pad_rows)),
        out_shape=jax.ShapeDtypeStruct((pad_rows, orb_count), jnp.bfloat16),
        in_specs=[vmem],
        out_specs=vmem,
        scratch_shapes=[spread],
        compiler_params=limit,
        name="pack",
    )(green)
    move_dims = (slots, share_rows, orb_count, walkers, moves, keep)
    *leaving, place = pl.pallas_call(
        functools.partial(leave_kernel, move_dims),
        out_shape=[jax.ShapeDtypeStruct((share_rows, orb_count), jnp.bfloat16)] * (walkers - 1)
        + [jax.ShapeDtypeStruct((slots,), jnp.int32)],
        in_specs=[smem, smem, vmem],
        out_specs=[vmem] * (walkers - 1) + [smem],
        scratch_shapes=[pltpu.VMEM((pad_rows, orb_count), jnp.float32)],
        compiler_params=limit,
        name="leave",
    )(walker_index, table, own_rows)
    coming = [
        lax.ppermute(
            leaving[shift - 1], "walker", [(z, (z + shift) % walkers) for z in range(walkers)]
        )
        for shift in range(1, walkers)
    ]

    group = 4
    groups = vectors // group
    chip_rows = 2 * share_rows
    weights = pl.pallas_call(
        functools.partial(order_kernel, (group, groups, chip_rows)),
        out_shape=jax.ShapeDtypeStruct((vectors * occ_count, orb_count), jnp.bfloat16),
        in_specs=[smem] + [pl.BlockSpec(memory_space=pl.ANY)] * 2,
        out_specs=vmem,
        scratch_shapes=[pltpu.SemaphoreType.DMA((5 * vectors,))],
        compiler_params=pltpu.CompilerParams(vmem_limit_bytes=48 * 1024 * 1024),
        cost_estimate=pl.CostEstimate(
            flops=0, bytes_accessed=4 * chol.size, transcendentals=0
        ),
        name="order",
    )(block_index, chol, own_rows)

    core, near_x, near_y = 1, 2, 4
    from_x = swap(own_rows, near_x, blocks)
    from_y = swap(own_rows, near_y, blocks)
    from_core = swap(own_rows, core, blocks)
    width = orb_count // 2
    from_x, from_y, weights, coming[:2] = lax.optimization_barrier(
        (from_x, from_y, weights, coming[:2])
    )
    far = [swap(from_y[:, :width], near_x, blocks), swap(from_x[:, width:], near_y, blocks)]
    near_pieces = [own_rows, from_core]
    for piece in (from_x, from_y):
        near_pieces += [piece, swap(piece, core, blocks)]

    dims = (slots, share_rows, group, groups, chip_rows)
    work = 2 * vectors * occ_count * orb_count * pad_rows
    near_sums, late = pl.pallas_call(
        functools.partial(near_kernel, dims),
        out_shape=[
            jax.ShapeDtypeStruct((slots * ROWS, LANES), jnp.float32),
            jax.ShapeDtypeStruct((slots * chip_rows, vectors * occ_count), jnp.float32),
        ],
        in_specs=[smem] + [vmem] * 7,
        out_specs=[vmem] * 2,
        scratch_shapes=[pltpu.VMEM((slots * 3 * chip_rows, group * occ_count), jnp.float32)]
        * groups,
        compiler_params=limit,
        cost_estimate=pl.CostEstimate(
            flops=6 * work, bytes_accessed=2 * chol.size, transcendentals=0
        ),
        name="near",
    )(block_index, weights, *near_pieces)
    far, near_sums = lax.optimization_barrier((far, near_sums))
    far_pieces = far + [swap(piece, core, blocks) for piece in far]
    all_sums = pl.pallas_call(
        functools.partial(far_kernel, dims),
        out_shape=jax.ShapeDtypeStruct((1, LANES), jnp.float32),
        in_specs=[smem] * 2 + [vmem] * 7,
        out_specs=vmem,
        scratch_shapes=[pltpu.VMEM((slots * chip_rows, group * occ_count), jnp.float32)] * groups,
        compiler_params=limit,
        cost_estimate=pl.CostEstimate(
            flops=2 * work, bytes_accessed=2 * chol.size, transcendentals=0
        ),
        name="far",
    )(block_index, place, weights, near_sums, late, *far_pieces)

    coming, _ = lax.optimization_barrier((coming, all_sums))
    new_green = pl.pallas_call(
        functools.partial(assemble_kernel, move_dims),
        out_shape=jax.ShapeDtypeStruct((keep, share_width), jnp.bfloat16),
        in_specs=[smem] * 2 + [vmem] * walkers,
        out_specs=vmem,
        scratch_shapes=[
            pltpu.VMEM((orb_count // LANES, share_rows * ROWS, LANES), jnp.float32),
            pltpu.VMEM(((slots + walkers - 1) * share_rows, orb_count), jnp.float32),
            pltpu.VMEM((orb_count // LANES, share_rows * ROWS, LANES), jnp.float32),
        ],
        compiler_params=limit,
        name="assemble",
    )(walker_index, table, green, *coming)

    energy_scale = 0.5 / (occ_count * math.sqrt(vectors * blocks))
    for mask in (core, near_x, near_y):
        all_sums = all_sums + swap(all_sums, mask, blocks)
    mask = 1
    while mask < walkers:
        pairs = [(index, index ^ mask) for index in range(walkers)]
        all_sums = all_sums + lax.ppermute(all_sums, "walker", pairs)
        mask *= 2
    own_sums = lax.dynamic_slice(all_sums[0], (walker_index[0] * keep,), (keep,))
    return (new_green, -energy_scale * own_sums)


def fits(mesh):
    blocks = mesh.shape["block"]
    walkers = mesh.shape["walker"]

    def check(green, chol, counts, move_slot, move_dest):
        vectors, occ_count, orb_count = chol.shape
        share_width = green.shape[1] // blocks
        moves = move_slot.shape[1]
        slots = green.shape[0] // walkers
        return (
            blocks == 8
            and walkers >= 2
            and walkers & (walkers - 1) == 0
            and (moves + walkers - 2) // (walkers - 1) == 1
            and slots <= ROWS
            and share_width % (orb_count * ROWS) == 0
            and orb_count % (2 * LANES) == 0
            and occ_count == blocks * (share_width // orb_count)
            and occ_count == LANES + LANES // 2
            and (vectors // blocks) % 4 == 0
            and walkers * (slots - moves) <= LANES
        )

    return check


def solution(mesh):
    in_specs = (P("walker", "block"), P("block", None, None), P(), P(), P())
    out_specs = (P("walker", "block"), P("walker"))
    check = fits(mesh)

    def run(*args):
        chosen = body if check(*args) else general_body
        return jax.shard_map(
            chosen, mesh=mesh, in_specs=in_specs, out_specs=out_specs, check_vma=False
        )(*args)

    return run
```

```python
import functools
import math

import jax
import jax.numpy as jnp
from jax import lax
from jax.experimental import pallas as pl
from jax.experimental.pallas import tpu as pltpu
from jax.sharding import PartitionSpec as P


def arrival_ranks(move_slot, move_dest):
    active = move_slot >= 0
    move_total = move_slot.shape[1]
    earlier = jnp.arange(move_total)[None, :] < jnp.arange(move_total)[:, None]
    same_target = (
        (move_dest[:, :, None] == move_dest[:, None, :]) & earlier[None, :, :] & active[:, None, :]
    )
    return (active, jnp.sum(same_target.astype(jnp.int32), axis=2))


def general_body(green, chol, counts, move_slot, move_dest):
    walker_total = lax.axis_size("walker")
    own_index = lax.axis_index("walker")
    slot_total = green.shape[0]
    share_width = green.shape[1]
    keep_total = slot_total - move_slot.shape[1]
    capacity = (move_slot.shape[1] + walker_total - 2) // (walker_total - 1)
    occ_count = chol.shape[1]
    orb_count = chol.shape[2]
    energy_scale = 0.5 / (occ_count * math.sqrt(chol.shape[0] * lax.axis_size("block")))
    active, move_rank = arrival_ranks(move_slot, move_dest)
    own_slots = move_slot[own_index]
    own_dests = move_dest[own_index]
    own_active = active[own_index]
    own_rank = move_rank[own_index]
    peer_ids = jnp.arange(walker_total)
    place_ids = jnp.arange(capacity)
    chosen = (
        (own_dests[None, None, :] == peer_ids[:, None, None])
        & (own_rank[None, None, :] == place_ids[None, :, None])
        & own_active[None, None, :]
    )
    send_slot = jnp.sum(jnp.where(chosen, own_slots[None, None, :], 0), axis=2).reshape(-1)
    present = jnp.any(chosen, axis=2).reshape(-1)
    arrive = jnp.any(
        (move_dest[:, None, :] == own_index)
        & (move_rank[:, None, :] == place_ids[None, :, None])
        & active[:, None, :],
        axis=2,
    ).reshape(-1)
    slot_ids = jnp.arange(slot_total)
    occupied = slot_ids < counts[own_index]
    leaving = jnp.any(own_slots[:, None] == slot_ids[None, :], axis=0)
    staying = occupied & jnp.logical_not(leaving)
    stay_rank = jnp.cumsum(staying.astype(jnp.int32)) - 1
    arrive_rank = jnp.cumsum(arrive.astype(jnp.int32)) - 1
    stay_total = jnp.sum(staying.astype(jnp.int32))
    targets = jnp.arange(keep_total)
    from_stay = jnp.sum(
        jnp.where(
            staying[None, :] & (stay_rank[None, :] == targets[:, None]), slot_ids[None, :], 0
        ),
        axis=1,
    )
    arrive_ids = jnp.arange(arrive.shape[0]) + slot_total
    from_arrive = jnp.sum(
        jnp.where(
            arrive[None, :] & (arrive_rank[None, :] == (targets - stay_total)[:, None]),
            arrive_ids[None, :],
            0,
        ),
        axis=1,
    )
    source_row = jnp.where(targets < stay_total, from_stay, from_arrive)
    outgoing = jnp.where(
        present[:, None], jnp.take(green, send_slot, axis=0), jnp.zeros((), jnp.bfloat16)
    )
    outgoing = outgoing.reshape(walker_total, capacity, share_width)

    def walker_energy(walker_row):
        green_mat = walker_row.reshape(occ_count, orb_count)
        transfer = jnp.einsum("gip,jp->gij", chol, green_mat, preferred_element_type=jnp.float32)
        return jnp.sum(transfer * jnp.swapaxes(transfer, 1, 2))

    got_rows = lax.all_to_all(outgoing, "walker", split_axis=0, concat_axis=0, tiled=True)
    source_pool = jnp.concatenate([green, got_rows.reshape(-1, share_width)], axis=0)
    new_green = jnp.take(source_pool, source_row, axis=0)
    complete = lax.all_gather(new_green, "block", axis=1, tiled=True)
    partial_value = lax.map(walker_energy, complete)
    energy = -energy_scale * lax.psum(partial_value, "block")
    return (new_green, energy)


LANES = 128
ROWS = 8


def spread_slots(green_ref, spread, share_rows):
    slots = green_ref.shape[0]
    tiles = spread.shape[0]
    for row in range(share_rows):
        for tile in range(tiles):
            col = (row * tiles + tile) * LANES
            block = green_ref[:, col : col + LANES].astype(jnp.float32)
            spread[tile, row * ROWS : row * ROWS + slots, :] = block


def pack_kernel(dims, green_ref, own_ref, spread):
    slots, share_rows, orb_count, pad_rows = dims
    spread_slots(green_ref, spread, share_rows)
    for tile in range(orb_count // LANES):
        dense = [spread[tile, pl.ds(slot, share_rows, stride=ROWS), :] for slot in range(slots)]
        if pad_rows > slots * share_rows:
            dense.append(jnp.zeros((pad_rows - slots * share_rows, LANES), jnp.float32))
        packed = jnp.concatenate(dense, axis=0).astype(jnp.bfloat16)
        own_ref[:, tile * LANES : (tile + 1) * LANES] = packed


class Moves:
    def __init__(self, table_ref, moves):
        self.table, self.moves = table_ref, moves

    def count(self, device):
        return self.table[0, device]

    def slot(self, device, move):
        return self.table[1 + move, device]

    def dest(self, device, move):
        return self.table[1 + self.moves + move, device]

    def staying(self, device):
        total = self.count(device)
        for move in range(self.moves):
            total = total - jnp.where(self.slot(device, move) >= 0, 1, 0)
        return total

    def goes_to(self, own, slot):
        target = jnp.int32(-1)
        for move in range(self.moves):
            target = jnp.where(self.slot(own, move) == slot, self.dest(own, move), target)
        return target


def leave_kernel(dims, ident_ref, table_ref, own_ref, *refs):
    slots, share_rows, orb_count, walkers, moves, keep = dims
    leave_refs, place_ref, wide = refs[:-2], refs[-2], refs[-1]
    table = Moves(table_ref, moves)
    wide[...] = own_ref[...].astype(jnp.float32)
    own = ident_ref[0]
    for shift in range(1, walkers):
        target = lax.rem(own + shift, walkers)
        chosen = jnp.int32(0)
        for move in range(moves):
            hit = (table.dest(own, move) == target) & (table.slot(own, move) >= 0)
            chosen = jnp.where(hit, table.slot(own, move), chosen)
        start = pl.multiple_of(chosen * share_rows, ROWS)
        leave_refs[shift - 1][...] = wide[pl.ds(start, share_rows), :].astype(jnp.bfloat16)
    rank = jnp.int32(0)
    for slot in range(slots):
        live = slot < table.count(own)
        gone_to = table.goes_to(own, slot)
        stays = live & (gone_to < 0)
        there = jnp.maximum(gone_to, 0)
        ahead = table.staying(there)
        for device in range(walkers):
            for move in range(moves):
                hit = (
                    (device < own)
                    & (table.dest(device, move) == there)
                    & (table.slot(device, move) >= 0)
                )
                ahead = ahead + jnp.where(hit, 1, 0)
        place = jnp.where(stays, own * keep + rank, there * keep + ahead)
        place_ref[slot] = jnp.where(live, place, -1)
        rank = rank + jnp.where(stays, 1, 0)


def assemble_kernel(dims, ident_ref, table_ref, green_ref, *refs):
    slots, share_rows, orb_count, walkers, moves, keep = dims
    table = Moves(table_ref, moves)
    come_refs = refs[: walkers - 1]
    new_ref, spread, pool, out = refs[walkers - 1 :]
    own = ident_ref[0]
    tiles = orb_count // LANES
    spread_slots(green_ref, spread, share_rows)
    for slot in range(slots):
        for tile in range(tiles):
            pool[
                slot * share_rows : (slot + 1) * share_rows, tile * LANES : (tile + 1) * LANES
            ] = spread[tile, pl.ds(slot, share_rows, stride=ROWS), :]
    for shift in range(1, walkers):
        start = (slots + shift - 1) * share_rows
        pool[start : start + share_rows, :] = come_refs[shift - 1][...].astype(jnp.float32)

    sources = [jnp.int32(0)] * keep
    rank = jnp.int32(0)
    for slot in range(slots):
        stays = (slot < table.count(own)) & (table.goes_to(own, slot) < 0)
        for target in range(keep):
            sources[target] = jnp.where(stays & (rank == target), slot, sources[target])
        rank = rank + jnp.where(stays, 1, 0)
    for device in range(walkers):
        comes = jnp.bool_(False)
        for move in range(moves):
            comes = comes | ((table.dest(device, move) == own) & (table.slot(device, move) >= 0))
        comes = comes & (device != own)
        shift = lax.rem(own - device + walkers, walkers)
        for target in range(keep):
            sources[target] = jnp.where(
                comes & (rank == target), slots + shift - 1, sources[target]
            )
        rank = rank + jnp.where(comes, 1, 0)
    for target in range(keep):
        start = pl.multiple_of(sources[target] * share_rows, ROWS)
        for tile in range(tiles):
            out[tile, pl.ds(target, share_rows, stride=ROWS), :] = pool[
                pl.ds(start, share_rows), tile * LANES : (tile + 1) * LANES
            ]
    for row in range(share_rows):
        for tile in range(tiles):
            col = (row * tiles + tile) * LANES
            new_ref[:, col : col + LANES] = out[
                tile, row * ROWS : row * ROWS + keep, :
            ].astype(jnp.bfloat16)


def order_kernel(dims, ident_ref, chol_ref, own_ref, out_ref, sems):
    del own_ref
    group, groups, chip_rows = dims
    chip = ident_ref[0] // 2
    edge = LANES - 2 * chip_rows
    rest = 2 * chip_rows - edge
    copies = []

    def add(vec, distance, start, size, place):
        row = pl.multiple_of(jnp.bitwise_xor(chip, distance) * chip_rows + start, 16)
        copies.append(
            pltpu.make_async_copy(
                chol_ref.at[vec, pl.ds(row, size), :],
                out_ref.at[pl.ds(place, size), :],
                sems.at[len(copies)],
            )
        )

    for index in range(groups):
        for item in range(group):
            vec = index * group + item
            place = index * group * 4 * chip_rows + item * LANES
            add(vec, 0, 0, chip_rows, place)
            add(vec, 1, 0, chip_rows, place + chip_rows)
            add(vec, 2, 0, edge, place + 2 * chip_rows)
            place = index * group * 4 * chip_rows + group * LANES + item * rest
            add(vec, 2, edge, chip_rows - edge, place)
            add(vec, 3, 0, chip_rows, place + chip_rows - edge)
    for copy in copies:
        copy.start()
    for copy in copies:
        copy.wait()


def times(left, right):
    return lax.dot_general(
        left, right, (((1,), (1,)), ((), ())), preferred_element_type=jnp.float32
    )


def near_kernel(dims, ident_ref, weight_ref, *refs):
    slots, share_rows, group, groups, chip_rows = dims
    piece_refs = refs[:6]
    sum_ref, late_ref = refs[6:8]
    trans_refs = refs[8:]
    own = ident_ref[0]
    core = lax.rem(own, 2)
    pad_rows = piece_refs[0].shape[0]
    near = 3 * chip_rows
    size = 4 * chip_rows * group
    edge = near - LANES
    half = LANES // 2
    left = jnp.concatenate([ref[...] for ref in piece_refs], axis=0)
    lane = lax.broadcasted_iota(jnp.int32, (1, LANES), 1)
    low_half = lane < half
    in_edge = jnp.where(low_half, lane, lane - half) < edge
    sums = [jnp.zeros((ROWS, LANES), jnp.float32) for _ in range(slots)]

    def fold(value):
        return jnp.sum(value.reshape(-1, ROWS, LANES), axis=0)

    for index in range(groups):
        trans = trans_refs[index]
        result = times(left, weight_ref[index * size : (index + 1) * size, :])
        for piece in range(6):
            source = jnp.bitwise_xor(core, piece % 2)
            for slot in range(slots):
                start = piece * pad_rows + slot * share_rows
                place = slot * near + (piece // 2) * chip_rows + source * share_rows
                trans[pl.ds(pl.multiple_of(place, ROWS), share_rows), :] = result[
                    start : start + share_rows, :
                ]
        for slot in range(slots):
            base = slot * near
            late = slice(slot * chip_rows, (slot + 1) * chip_rows)
            acc = sums[slot]
            for pair in range(group // 2):
                col = (group + pair) * LANES
                top = trans[base : base + LANES, col : col + LANES].T
                edge_rows = trans[base + LANES : base + near, col : col + LANES]
                gap = jnp.zeros((half - edge, LANES), jnp.float32)
                bottom = jnp.concatenate([edge_rows, gap, edge_rows, gap], axis=0).T
                for side in range(2):
                    vec = 2 * pair + side
                    high = trans[base : base + LANES, vec * LANES : (vec + 1) * LANES]
                    acc = acc + fold(high * high.T)
                    across = trans[base + LANES : base + near, vec * LANES : (vec + 1) * LANES]
                    acc = acc + 2.0 * fold(across * top[side * half : side * half + edge, :])
                    late_ref[
                        late, (index * (group + group // 2) + vec) * LANES : (
                            index * (group + group // 2) + vec + 1
                        ) * LANES
                    ] = top[side * half + edge : (side + 1) * half, :]
                corner = jnp.where(low_half, bottom[:edge, :], bottom[half : half + edge, :])
                acc = acc + fold(jnp.where(in_edge, edge_rows * corner, 0.0))
                rest = jnp.where(low_half, bottom[edge:half, :], bottom[half + edge :, :])
                place = (index * (group + group // 2) + group + pair) * LANES
                late_ref[late, place : place + LANES] = jnp.where(in_edge, rest, 0.0)
            sums[slot] = acc
    sum_ref[...] = jnp.concatenate(sums, axis=0)


def far_kernel(dims, ident_ref, place_ref, weight_ref, near_sum_ref, late_ref, *refs):
    slots, share_rows, group, groups, chip_rows = dims
    piece_refs = refs[:4]
    sum_ref = refs[4]
    trans_refs = refs[5:]
    own = ident_ref[0]
    core = lax.rem(own, 2)
    pad_rows, width = piece_refs[0].shape
    half = LANES // 2
    edge = half - chip_rows
    size = 4 * chip_rows * group
    lane = lax.broadcasted_iota(jnp.int32, (1, LANES), 1)
    low_half = lane < half
    in_rest = jnp.where(low_half, lane, lane - half) >= edge
    lefts = [
        jnp.concatenate([piece_refs[part][...], piece_refs[2 + part][...]], axis=0)
        for part in range(2)
    ]
    twice = [jnp.zeros((ROWS, LANES), jnp.float32) for _ in range(slots)]
    once = [near_sum_ref[slot * ROWS : (slot + 1) * ROWS, :] for slot in range(slots)]

    def fold(value):
        return jnp.sum(value.reshape(-1, ROWS, LANES), axis=0)

    tiles = group + group // 2
    for index in range(groups):
        trans = trans_refs[index]
        rows = slice(index * size, (index + 1) * size)
        result = times(lefts[0], weight_ref[rows, :width])
        result = result + times(lefts[1], weight_ref[rows, width:])
        for piece in range(2):
            source = jnp.bitwise_xor(core, piece)
            for slot in range(slots):
                start = piece * pad_rows + slot * share_rows
                place = slot * chip_rows + source * share_rows
                trans[pl.ds(pl.multiple_of(place, ROWS), share_rows), :] = result[
                    start : start + share_rows, :
                ]
        for slot in range(slots):
            rows = slice(slot * chip_rows, (slot + 1) * chip_rows)
            for tile in range(tiles):
                here = trans[rows, tile * LANES : (tile + 1) * LANES]
                met = late_ref[rows, (index * tiles + tile) * LANES : (index * tiles + tile + 1) * LANES]
                twice[slot] = twice[slot] + fold(here * met)
                if tile >= group:
                    gap = jnp.zeros((edge, LANES), jnp.float32)
                    turned = jnp.concatenate([gap, here, gap, here], axis=0).T
                    corner = jnp.where(low_half, turned[edge:half, :], turned[half + edge :, :])
                    once[slot] = once[slot] + fold(jnp.where(in_rest, here * corner, 0.0))
    value = jnp.zeros((1, LANES), jnp.float32)
    for slot in range(slots):
        slot_sum = jnp.sum(once[slot] + 2.0 * twice[slot])
        value = jnp.where(lane == place_ref[slot], slot_sum, value)
    sum_ref[...] = jnp.broadcast_to(value, sum_ref.shape)


def swap(value, mask, blocks):
    return lax.ppermute(value, "block", [(index, index ^ mask) for index in range(blocks)])


def body(green, chol, counts, move_slot, move_dest):
    walkers = lax.axis_size("walker")
    blocks = lax.axis_size("block")
    slots, share_width = green.shape
    vectors, occ_count, orb_count = chol.shape
    moves = move_slot.shape[1]
    keep = slots - moves
    share_rows = share_width // orb_count
    pad_rows = -(-slots * share_rows // 16) * 16
    table = jnp.concatenate([counts[None, :], move_slot.T, move_dest.T], axis=0)
    walker_index = lax.axis_index("walker").astype(jnp.int32).reshape(1)
    block_index = lax.axis_index("block").astype(jnp.int32).reshape(1)
    smem = pl.BlockSpec(memory_space=pltpu.SMEM)
    vmem = pl.BlockSpec(memory_space=pltpu.VMEM)
    limit = pltpu.CompilerParams(vmem_limit_bytes=32 * 1024 * 1024)

    spread = pltpu.VMEM((orb_count // LANES, share_rows * ROWS, LANES), jnp.float32)
    own_rows = pl.pallas_call(
        functools.partial(pack_kernel, (slots, share_rows, orb_count, pad_rows)),
        out_shape=jax.ShapeDtypeStruct((pad_rows, orb_count), jnp.bfloat16),
        in_specs=[vmem],
        out_specs=vmem,
        scratch_shapes=[spread],
        compiler_params=limit,
        name="pack",
    )(green)
    move_dims = (slots, share_rows, orb_count, walkers, moves, keep)
    *leaving, place = pl.pallas_call(
        functools.partial(leave_kernel, move_dims),
        out_shape=[jax.ShapeDtypeStruct((share_rows, orb_count), jnp.bfloat16)] * (walkers - 1)
        + [jax.ShapeDtypeStruct((slots,), jnp.int32)],
        in_specs=[smem, smem, vmem],
        out_specs=[vmem] * (walkers - 1) + [smem],
        scratch_shapes=[pltpu.VMEM((pad_rows, orb_count), jnp.float32)],
        compiler_params=limit,
        name="leave",
    )(walker_index, table, own_rows)
    coming = [
        lax.ppermute(
            leaving[shift - 1], "walker", [(z, (z + shift) % walkers) for z in range(walkers)]
        )
        for shift in range(1, walkers)
    ]

    group = 4
    groups = vectors // group
    chip_rows = 2 * share_rows
    weights = pl.pallas_call(
        functools.partial(order_kernel, (group, groups, chip_rows)),
        out_shape=jax.ShapeDtypeStruct((vectors * occ_count, orb_count), jnp.bfloat16),
        in_specs=[smem] + [pl.BlockSpec(memory_space=pl.ANY)] * 2,
        out_specs=vmem,
        scratch_shapes=[pltpu.SemaphoreType.DMA((5 * vectors,))],
        compiler_params=pltpu.CompilerParams(vmem_limit_bytes=48 * 1024 * 1024),
        cost_estimate=pl.CostEstimate(
            flops=0, bytes_accessed=4 * chol.size, transcendentals=0
        ),
        name="order",
    )(block_index, chol, own_rows)

    core, near_x, near_y = 1, 2, 4
    from_x = swap(own_rows, near_x, blocks)
    from_y = swap(own_rows, near_y, blocks)
    from_core = swap(own_rows, core, blocks)
    width = orb_count // 2
    from_x, from_y, weights, coming[:2] = lax.optimization_barrier(
        (from_x, from_y, weights, coming[:2])
    )
    far = [swap(from_y[:, :width], near_x, blocks), swap(from_x[:, width:], near_y, blocks)]
    near_pieces = [own_rows, from_core]
    for piece in (from_x, from_y):
        near_pieces += [piece, swap(piece, core, blocks)]

    dims = (slots, share_rows, group, groups, chip_rows)
    work = 2 * vectors * occ_count * orb_count * pad_rows
    near_sums, late = pl.pallas_call(
        functools.partial(near_kernel, dims),
        out_shape=[
            jax.ShapeDtypeStruct((slots * ROWS, LANES), jnp.float32),
            jax.ShapeDtypeStruct((slots * chip_rows, vectors * occ_count), jnp.float32),
        ],
        in_specs=[smem] + [vmem] * 7,
        out_specs=[vmem] * 2,
        scratch_shapes=[pltpu.VMEM((slots * 3 * chip_rows, group * occ_count), jnp.float32)]
        * groups,
        compiler_params=limit,
        cost_estimate=pl.CostEstimate(
            flops=6 * work, bytes_accessed=2 * chol.size, transcendentals=0
        ),
        name="near",
    )(block_index, weights, *near_pieces)
    far, near_sums = lax.optimization_barrier((far, near_sums))
    far_pieces = far + [swap(piece, core, blocks) for piece in far]
    all_sums = pl.pallas_call(
        functools.partial(far_kernel, dims),
        out_shape=jax.ShapeDtypeStruct((blocks * walkers, LANES), jnp.float32),
        in_specs=[smem] * 2 + [vmem] * 7,
        out_specs=vmem,
        scratch_shapes=[pltpu.VMEM((slots * chip_rows, group * occ_count), jnp.float32)] * groups,
        compiler_params=limit,
        cost_estimate=pl.CostEstimate(
            flops=2 * work, bytes_accessed=2 * chol.size, transcendentals=0
        ),
        name="far",
    )(block_index, place, weights, near_sums, late, *far_pieces)

    coming, _ = lax.optimization_barrier((coming, all_sums))
    new_green = pl.pallas_call(
        functools.partial(assemble_kernel, move_dims),
        out_shape=jax.ShapeDtypeStruct((keep, share_width), jnp.bfloat16),
        in_specs=[smem] * 2 + [vmem] * walkers,
        out_specs=vmem,
        scratch_shapes=[
            pltpu.VMEM((orb_count // LANES, share_rows * ROWS, LANES), jnp.float32),
            pltpu.VMEM(((slots + walkers - 1) * share_rows, orb_count), jnp.float32),
            pltpu.VMEM((orb_count // LANES, share_rows * ROWS, LANES), jnp.float32),
        ],
        compiler_params=limit,
        name="assemble",
    )(walker_index, table, green, *coming)

    energy_scale = 0.5 / (occ_count * math.sqrt(vectors * blocks))
    got = lax.all_to_all(
        all_sums, ("block", "walker"), split_axis=0, concat_axis=0, tiled=True
    )
    got_sums = jnp.sum(got, axis=0)
    own_sums = lax.dynamic_slice(got_sums, (walker_index[0] * keep,), (keep,))
    return (new_green, -energy_scale * own_sums)


def fits(mesh):
    blocks = mesh.shape["block"]
    walkers = mesh.shape["walker"]

    def check(green, chol, counts, move_slot, move_dest):
        vectors, occ_count, orb_count = chol.shape
        share_width = green.shape[1] // blocks
        moves = move_slot.shape[1]
        slots = green.shape[0] // walkers
        return (
            blocks == 8
            and walkers >= 2
            and walkers & (walkers - 1) == 0
            and (moves + walkers - 2) // (walkers - 1) == 1
            and slots <= ROWS
            and share_width % (orb_count * ROWS) == 0
            and orb_count % (2 * LANES) == 0
            and occ_count == blocks * (share_width // orb_count)
            and occ_count == LANES + LANES // 2
            and (vectors // blocks) % 4 == 0
            and walkers * (slots - moves) <= LANES
        )

    return check


def solution(mesh):
    in_specs = (P("walker", "block"), P("block", None, None), P(), P(), P())
    out_specs = (P("walker", "block"), P("walker"))
    check = fits(mesh)

    def run(*args):
        chosen = body if check(*args) else general_body
        return jax.shard_map(
            chosen, mesh=mesh, in_specs=in_specs, out_specs=out_specs, check_vma=False
        )(*args)

    return run
```

```python
import functools
import math

import jax
import jax.numpy as jnp
from jax import lax
from jax.experimental import pallas as pl
from jax.experimental.pallas import tpu as pltpu
from jax.sharding import PartitionSpec as P


def arrival_ranks(move_slot, move_dest):
    active = move_slot >= 0
    move_total = move_slot.shape[1]
    earlier = jnp.arange(move_total)[None, :] < jnp.arange(move_total)[:, None]
    same_target = (
        (move_dest[:, :, None] == move_dest[:, None, :]) & earlier[None, :, :] & active[:, None, :]
    )
    return (active, jnp.sum(same_target.astype(jnp.int32), axis=2))


def general_body(green, chol, counts, move_slot, move_dest):
    walker_total = lax.axis_size("walker")
    own_index = lax.axis_index("walker")
    slot_total = green.shape[0]
    share_width = green.shape[1]
    keep_total = slot_total - move_slot.shape[1]
    capacity = (move_slot.shape[1] + walker_total - 2) // (walker_total - 1)
    occ_count = chol.shape[1]
    orb_count = chol.shape[2]
    energy_scale = 0.5 / (occ_count * math.sqrt(chol.shape[0] * lax.axis_size("block")))
    active, move_rank = arrival_ranks(move_slot, move_dest)
    own_slots = move_slot[own_index]
    own_dests = move_dest[own_index]
    own_active = active[own_index]
    own_rank = move_rank[own_index]
    peer_ids = jnp.arange(walker_total)
    place_ids = jnp.arange(capacity)
    chosen = (
        (own_dests[None, None, :] == peer_ids[:, None, None])
        & (own_rank[None, None, :] == place_ids[None, :, None])
        & own_active[None, None, :]
    )
    send_slot = jnp.sum(jnp.where(chosen, own_slots[None, None, :], 0), axis=2).reshape(-1)
    present = jnp.any(chosen, axis=2).reshape(-1)
    arrive = jnp.any(
        (move_dest[:, None, :] == own_index)
        & (move_rank[:, None, :] == place_ids[None, :, None])
        & active[:, None, :],
        axis=2,
    ).reshape(-1)
    slot_ids = jnp.arange(slot_total)
    occupied = slot_ids < counts[own_index]
    leaving = jnp.any(own_slots[:, None] == slot_ids[None, :], axis=0)
    staying = occupied & jnp.logical_not(leaving)
    stay_rank = jnp.cumsum(staying.astype(jnp.int32)) - 1
    arrive_rank = jnp.cumsum(arrive.astype(jnp.int32)) - 1
    stay_total = jnp.sum(staying.astype(jnp.int32))
    targets = jnp.arange(keep_total)
    from_stay = jnp.sum(
        jnp.where(
            staying[None, :] & (stay_rank[None, :] == targets[:, None]), slot_ids[None, :], 0
        ),
        axis=1,
    )
    arrive_ids = jnp.arange(arrive.shape[0]) + slot_total
    from_arrive = jnp.sum(
        jnp.where(
            arrive[None, :] & (arrive_rank[None, :] == (targets - stay_total)[:, None]),
            arrive_ids[None, :],
            0,
        ),
        axis=1,
    )
    source_row = jnp.where(targets < stay_total, from_stay, from_arrive)
    outgoing = jnp.where(
        present[:, None], jnp.take(green, send_slot, axis=0), jnp.zeros((), jnp.bfloat16)
    )
    outgoing = outgoing.reshape(walker_total, capacity, share_width)

    def walker_energy(walker_row):
        green_mat = walker_row.reshape(occ_count, orb_count)
        transfer = jnp.einsum("gip,jp->gij", chol, green_mat, preferred_element_type=jnp.float32)
        return jnp.sum(transfer * jnp.swapaxes(transfer, 1, 2))

    got_rows = lax.all_to_all(outgoing, "walker", split_axis=0, concat_axis=0, tiled=True)
    source_pool = jnp.concatenate([green, got_rows.reshape(-1, share_width)], axis=0)
    new_green = jnp.take(source_pool, source_row, axis=0)
    complete = lax.all_gather(new_green, "block", axis=1, tiled=True)
    partial_value = lax.map(walker_energy, complete)
    energy = -energy_scale * lax.psum(partial_value, "block")
    return (new_green, energy)


LANES = 128
ROWS = 8


def spread_slots(green_ref, spread, share_rows):
    slots = green_ref.shape[0]
    tiles = spread.shape[0]
    for row in range(share_rows):
        for tile in range(tiles):
            col = (row * tiles + tile) * LANES
            block = green_ref[:, col : col + LANES].astype(jnp.float32)
            spread[tile, row * ROWS : row * ROWS + slots, :] = block


def pack_kernel(dims, green_ref, own_ref, spread):
    slots, share_rows, orb_count, pad_rows = dims
    spread_slots(green_ref, spread, share_rows)
    for tile in range(orb_count // LANES):
        dense = [spread[tile, pl.ds(slot, share_rows, stride=ROWS), :] for slot in range(slots)]
        if pad_rows > slots * share_rows:
            dense.append(jnp.zeros((pad_rows - slots * share_rows, LANES), jnp.float32))
        packed = jnp.concatenate(dense, axis=0).astype(jnp.bfloat16)
        own_ref[:, tile * LANES : (tile + 1) * LANES] = packed


class Moves:
    def __init__(self, table_ref, moves):
        self.table, self.moves = table_ref, moves

    def count(self, device):
        return self.table[0, device]

    def slot(self, device, move):
        return self.table[1 + move, device]

    def dest(self, device, move):
        return self.table[1 + self.moves + move, device]

    def staying(self, device):
        total = self.count(device)
        for move in range(self.moves):
            total = total - jnp.where(self.slot(device, move) >= 0, 1, 0)
        return total

    def goes_to(self, own, slot):
        target = jnp.int32(-1)
        for move in range(self.moves):
            target = jnp.where(self.slot(own, move) == slot, self.dest(own, move), target)
        return target


def assemble_kernel(dims, ident_ref, table_ref, green_ref, *refs):
    slots, share_rows, orb_count, walkers, moves, keep = dims
    table = Moves(table_ref, moves)
    come_refs = refs[: walkers - 1]
    new_ref, spread, pool, out = refs[walkers - 1 :]
    own = ident_ref[0]
    tiles = orb_count // LANES
    spread_slots(green_ref, spread, share_rows)
    for slot in range(slots):
        for tile in range(tiles):
            pool[
                slot * share_rows : (slot + 1) * share_rows, tile * LANES : (tile + 1) * LANES
            ] = spread[tile, pl.ds(slot, share_rows, stride=ROWS), :]
    for shift in range(1, walkers):
        start = (slots + shift - 1) * share_rows
        pool[start : start + share_rows, :] = come_refs[shift - 1][...].astype(jnp.float32)

    sources = [jnp.int32(0)] * keep
    rank = jnp.int32(0)
    for slot in range(slots):
        stays = (slot < table.count(own)) & (table.goes_to(own, slot) < 0)
        for target in range(keep):
            sources[target] = jnp.where(stays & (rank == target), slot, sources[target])
        rank = rank + jnp.where(stays, 1, 0)
    for device in range(walkers):
        comes = jnp.bool_(False)
        for move in range(moves):
            comes = comes | ((table.dest(device, move) == own) & (table.slot(device, move) >= 0))
        comes = comes & (device != own)
        shift = lax.rem(own - device + walkers, walkers)
        for target in range(keep):
            sources[target] = jnp.where(
                comes & (rank == target), slots + shift - 1, sources[target]
            )
        rank = rank + jnp.where(comes, 1, 0)
    for target in range(keep):
        start = pl.multiple_of(sources[target] * share_rows, ROWS)
        for tile in range(tiles):
            out[tile, pl.ds(target, share_rows, stride=ROWS), :] = pool[
                pl.ds(start, share_rows), tile * LANES : (tile + 1) * LANES
            ]
    for row in range(share_rows):
        for tile in range(tiles):
            col = (row * tiles + tile) * LANES
            new_ref[:, col : col + LANES] = out[
                tile, row * ROWS : row * ROWS + keep, :
            ].astype(jnp.bfloat16)


def times(left, right):
    return lax.dot_general(
        left, right, (((1,), (1,)), ((), ())), preferred_element_type=jnp.float32
    )


def find_places(dims, own, table, place_ref):
    slots, walkers, moves, keep = dims
    rank = jnp.int32(0)
    for slot in range(slots):
        live = slot < table.count(own)
        gone_to = table.goes_to(own, slot)
        stays = live & (gone_to < 0)
        there = jnp.maximum(gone_to, 0)
        ahead = table.staying(there)
        for device in range(walkers):
            for move in range(moves):
                hit = (
                    (device < own)
                    & (table.dest(device, move) == there)
                    & (table.slot(device, move) >= 0)
                )
                ahead = ahead + jnp.where(hit, 1, 0)
        place = jnp.where(stays, own * keep + rank, there * keep + ahead)
        place_ref[slot] = jnp.where(live, place, -1)
        rank = rank + jnp.where(stays, 1, 0)


def leave_kernel(dims, walker_ref, table_ref, own_ref, *refs):
    share_rows, walkers, moves = dims
    leave_refs, wide = refs[:-1], refs[-1]
    table = Moves(table_ref, moves)
    own = walker_ref[0]
    wide[...] = own_ref[...].astype(jnp.float32)
    for shift in range(1, walkers):
        target = lax.rem(own + shift, walkers)
        chosen = jnp.int32(0)
        for move in range(moves):
            hit = (table.dest(own, move) == target) & (table.slot(own, move) >= 0)
            chosen = jnp.where(hit, table.slot(own, move), chosen)
        start = pl.multiple_of(chosen * share_rows, ROWS)
        leave_refs[shift - 1][...] = wide[pl.ds(start, share_rows), :].astype(jnp.bfloat16)


def home_kernel(dims, ident_ref, walker_ref, table_ref, chol_ref, own_ref, core_ref, *refs):
    slots, share_rows, group, groups, chip_rows, walkers, moves, keep = dims
    weight_ref, home_ref, place_ref = refs[:3]
    sems = refs[3]
    chip, core = ident_ref[0] // 2, lax.rem(ident_ref[0], 2)
    edge = LANES - 2 * chip_rows
    rest = 2 * chip_rows - edge
    size = group * 4 * chip_rows
    copies = []

    def add(vec, distance, start, count, place):
        row = pl.multiple_of(jnp.bitwise_xor(chip, distance) * chip_rows + start, 16)
        copies.append(
            pltpu.make_async_copy(
                chol_ref.at[vec, pl.ds(row, count), :],
                weight_ref.at[pl.ds(place, count), :],
                sems.at[len(copies)],
            )
        )

    for index in range(groups):
        for item in range(group):
            vec = index * group + item
            place = index * size + item * LANES
            add(vec, 0, 0, chip_rows, place)
            add(vec, 1, 0, chip_rows, place + chip_rows)
            add(vec, 2, 0, edge, place + 2 * chip_rows)
            place = index * size + group * LANES + item * rest
            add(vec, 2, edge, chip_rows - edge, place)
            add(vec, 3, 0, chip_rows, place + chip_rows - edge)
    for copy in copies:
        copy.start()

    table = Moves(table_ref, moves)
    own = walker_ref[0]
    find_places((slots, walkers, moves, keep), own, table, place_ref)

    pad_rows = own_ref.shape[0]
    left = jnp.concatenate([own_ref[...], core_ref[...]], axis=0)
    per_group = len(copies) // groups
    for index in range(groups):
        for copy in copies[index * per_group : (index + 1) * per_group]:
            copy.wait()
        cols = slice(index * size, (index + 1) * size)
        result = times(left, weight_ref[cols, :])
        for piece in range(2):
            source = jnp.bitwise_xor(core, piece)
            for slot in range(slots):
                start = piece * pad_rows + slot * share_rows
                place = pl.multiple_of(slot * chip_rows + source * share_rows, ROWS)
                home_ref[pl.ds(place, share_rows), cols] = result[start : start + share_rows, :]


def near_kernel(dims, ident_ref, weight_ref, home_ref, *refs):
    slots, share_rows, group, groups, chip_rows = dims
    piece_refs = refs[:4]
    sum_ref, late_ref = refs[4:6]
    trans_refs = refs[6:]
    own = ident_ref[0]
    core = lax.rem(own, 2)
    pad_rows = piece_refs[0].shape[0]
    away = 2 * chip_rows
    size = 4 * chip_rows * group
    edge = 3 * chip_rows - LANES
    half = LANES // 2
    left = jnp.concatenate([ref[...] for ref in piece_refs], axis=0)
    lane = lax.broadcasted_iota(jnp.int32, (1, LANES), 1)
    low_half = lane < half
    in_edge = jnp.where(low_half, lane, lane - half) < edge
    sums = [jnp.zeros((ROWS, LANES), jnp.float32) for _ in range(slots)]

    def fold(value):
        return jnp.sum(value.reshape(-1, ROWS, LANES), axis=0)

    for index in range(groups):
        trans = trans_refs[index]
        result = times(left, weight_ref[index * size : (index + 1) * size, :])
        for piece in range(4):
            source = jnp.bitwise_xor(core, piece % 2)
            for slot in range(slots):
                start = piece * pad_rows + slot * share_rows
                place = slot * away + (piece // 2) * chip_rows + source * share_rows
                trans[pl.ds(pl.multiple_of(place, ROWS), share_rows), :] = result[
                    start : start + share_rows, :
                ]
        for slot in range(slots):
            late = slice(slot * chip_rows, (slot + 1) * chip_rows)

            def head(col):
                first = home_ref[late, index * size + col : index * size + col + LANES]
                second = trans[slot * away : slot * away + LANES - chip_rows, col : col + LANES]
                return jnp.concatenate([first, second], axis=0)

            def tail(col):
                base = (slot + 1) * away
                return trans[base - edge : base, col : col + LANES]

            acc = sums[slot]
            for pair in range(group // 2):
                col = (group + pair) * LANES
                top = head(col).T
                edge_rows = tail(col)
                gap = jnp.zeros((half - edge, LANES), jnp.float32)
                bottom = jnp.concatenate([edge_rows, gap, edge_rows, gap], axis=0).T
                for side in range(2):
                    vec = 2 * pair + side
                    high = head(vec * LANES)
                    acc = acc + fold(high * high.T)
                    across = tail(vec * LANES)
                    acc = acc + 2.0 * fold(across * top[side * half : side * half + edge, :])
                    late_ref[
                        late, (index * (group + group // 2) + vec) * LANES : (
                            index * (group + group // 2) + vec + 1
                        ) * LANES
                    ] = top[side * half + edge : (side + 1) * half, :]
                corner = jnp.where(low_half, bottom[:edge, :], bottom[half : half + edge, :])
                acc = acc + fold(jnp.where(in_edge, edge_rows * corner, 0.0))
                rest = jnp.where(low_half, bottom[edge:half, :], bottom[half + edge :, :])
                place = (index * (group + group // 2) + group + pair) * LANES
                late_ref[late, place : place + LANES] = jnp.where(in_edge, rest, 0.0)
            sums[slot] = acc
    sum_ref[...] = jnp.concatenate(sums, axis=0)


def far_kernel(dims, ident_ref, place_ref, weight_ref, near_sum_ref, late_ref, *refs):
    slots, share_rows, group, groups, chip_rows = dims
    piece_refs = refs[:4]
    sum_ref = refs[4]
    trans_refs = refs[5:]
    own = ident_ref[0]
    core = lax.rem(own, 2)
    pad_rows, width = piece_refs[0].shape
    half = LANES // 2
    edge = half - chip_rows
    size = 4 * chip_rows * group
    lane = lax.broadcasted_iota(jnp.int32, (1, LANES), 1)
    low_half = lane < half
    in_rest = jnp.where(low_half, lane, lane - half) >= edge
    lefts = [
        jnp.concatenate([piece_refs[part][...], piece_refs[2 + part][...]], axis=0)
        for part in range(2)
    ]
    twice = [jnp.zeros((ROWS, LANES), jnp.float32) for _ in range(slots)]
    once = [near_sum_ref[slot * ROWS : (slot + 1) * ROWS, :] for slot in range(slots)]

    def fold(value):
        return jnp.sum(value.reshape(-1, ROWS, LANES), axis=0)

    tiles = group + group // 2
    for index in range(groups):
        trans = trans_refs[index]
        rows = slice(index * size, (index + 1) * size)
        result = times(lefts[0], weight_ref[rows, :width])
        result = result + times(lefts[1], weight_ref[rows, width:])
        for piece in range(2):
            source = jnp.bitwise_xor(core, piece)
            for slot in range(slots):
                start = piece * pad_rows + slot * share_rows
                place = slot * chip_rows + source * share_rows
                trans[pl.ds(pl.multiple_of(place, ROWS), share_rows), :] = result[
                    start : start + share_rows, :
                ]
        for slot in range(slots):
            rows = slice(slot * chip_rows, (slot + 1) * chip_rows)
            for tile in range(tiles):
                here = trans[rows, tile * LANES : (tile + 1) * LANES]
                met = late_ref[rows, (index * tiles + tile) * LANES : (index * tiles + tile + 1) * LANES]
                twice[slot] = twice[slot] + fold(here * met)
                if tile >= group:
                    gap = jnp.zeros((edge, LANES), jnp.float32)
                    turned = jnp.concatenate([gap, here, gap, here], axis=0).T
                    corner = jnp.where(low_half, turned[edge:half, :], turned[half + edge :, :])
                    once[slot] = once[slot] + fold(jnp.where(in_rest, here * corner, 0.0))
    value = jnp.zeros((1, LANES), jnp.float32)
    for slot in range(slots):
        slot_sum = jnp.sum(once[slot] + 2.0 * twice[slot])
        value = jnp.where(lane == place_ref[slot], slot_sum, value)
    sum_ref[...] = jnp.broadcast_to(value, sum_ref.shape)


def swap(value, mask, blocks):
    return lax.ppermute(value, "block", [(index, index ^ mask) for index in range(blocks)])


def body(green, chol, counts, move_slot, move_dest):
    walkers = lax.axis_size("walker")
    blocks = lax.axis_size("block")
    slots, share_width = green.shape
    vectors, occ_count, orb_count = chol.shape
    moves = move_slot.shape[1]
    keep = slots - moves
    share_rows = share_width // orb_count
    pad_rows = -(-slots * share_rows // 16) * 16
    table = jnp.concatenate([counts[None, :], move_slot.T, move_dest.T], axis=0)
    walker_index = lax.axis_index("walker").astype(jnp.int32).reshape(1)
    block_index = lax.axis_index("block").astype(jnp.int32).reshape(1)
    smem = pl.BlockSpec(memory_space=pltpu.SMEM)
    vmem = pl.BlockSpec(memory_space=pltpu.VMEM)
    limit = pltpu.CompilerParams(vmem_limit_bytes=32 * 1024 * 1024)

    spread = pltpu.VMEM((orb_count // LANES, share_rows * ROWS, LANES), jnp.float32)
    own_rows = pl.pallas_call(
        functools.partial(pack_kernel, (slots, share_rows, orb_count, pad_rows)),
        out_shape=jax.ShapeDtypeStruct((pad_rows, orb_count), jnp.bfloat16),
        in_specs=[vmem],
        out_specs=vmem,
        scratch_shapes=[spread],
        compiler_params=limit,
        name="pack",
    )(green)
    leaving = pl.pallas_call(
        functools.partial(leave_kernel, (share_rows, walkers, moves)),
        out_shape=[jax.ShapeDtypeStruct((share_rows, orb_count), jnp.bfloat16)] * (walkers - 1),
        in_specs=[smem, smem, vmem],
        out_specs=[vmem] * (walkers - 1),
        scratch_shapes=[pltpu.VMEM((pad_rows, orb_count), jnp.float32)],
        compiler_params=limit,
        name="leave",
    )(walker_index, table, own_rows)
    core, near_x, near_y = 1, 2, 4
    from_x = swap(own_rows, near_x, blocks)
    from_y = swap(own_rows, near_y, blocks)
    from_core = swap(own_rows, core, blocks)
    group = 4
    groups = vectors // group
    chip_rows = 2 * share_rows
    anywhere = pl.BlockSpec(memory_space=pl.ANY)
    home_dims = (slots, share_rows, group, groups, chip_rows, walkers, moves, keep)
    weights, home, place = pl.pallas_call(
        functools.partial(home_kernel, home_dims),
        out_shape=[
            jax.ShapeDtypeStruct((vectors * occ_count, orb_count), jnp.bfloat16),
            jax.ShapeDtypeStruct((slots * chip_rows, vectors * occ_count), jnp.float32),
            jax.ShapeDtypeStruct((slots,), jnp.int32),
        ],
        in_specs=[smem] * 3 + [anywhere] + [vmem] * 2,
        out_specs=[vmem] * 2 + [smem],
        scratch_shapes=[pltpu.SemaphoreType.DMA((5 * vectors,))],
        compiler_params=pltpu.CompilerParams(vmem_limit_bytes=46 * 1024 * 1024),
        cost_estimate=pl.CostEstimate(
            flops=4 * vectors * occ_count * orb_count * pad_rows,
            bytes_accessed=4 * chol.size,
            transcendentals=0,
        ),
        name="home",
    )(block_index, walker_index, table, chol, own_rows, from_core)
    coming = [
        lax.ppermute(
            leaving[shift - 1], "walker", [(z, (z + shift) % walkers) for z in range(walkers)]
        )
        for shift in range(1, walkers)
    ]
    width = orb_count // 2
    from_x, from_y, weights, coming[:2] = lax.optimization_barrier(
        (from_x, from_y, weights, coming[:2])
    )
    far = [swap(from_y[:, :width], near_x, blocks), swap(from_x[:, width:], near_y, blocks)]
    near_pieces = []
    for piece in (from_x, from_y):
        near_pieces += [piece, swap(piece, core, blocks)]

    dims = (slots, share_rows, group, groups, chip_rows)
    work = 2 * vectors * occ_count * orb_count * pad_rows
    near_sums, late = pl.pallas_call(
        functools.partial(near_kernel, dims),
        out_shape=[
            jax.ShapeDtypeStruct((slots * ROWS, LANES), jnp.float32),
            jax.ShapeDtypeStruct((slots * chip_rows, vectors * occ_count), jnp.float32),
        ],
        in_specs=[smem] + [vmem] * 6,
        out_specs=[vmem] * 2,
        scratch_shapes=[pltpu.VMEM((slots * 2 * chip_rows, group * occ_count), jnp.float32)]
        * groups,
        compiler_params=limit,
        cost_estimate=pl.CostEstimate(
            flops=4 * work, bytes_accessed=2 * chol.size, transcendentals=0
        ),
        name="near",
    )(block_index, weights, home, *near_pieces)
    far, near_sums = lax.optimization_barrier((far, near_sums))
    far_pieces = far + [swap(piece, core, blocks) for piece in far]
    all_sums = pl.pallas_call(
        functools.partial(far_kernel, dims),
        out_shape=jax.ShapeDtypeStruct((blocks * walkers, LANES), jnp.float32),
        in_specs=[smem] * 2 + [vmem] * 7,
        out_specs=vmem,
        scratch_shapes=[pltpu.VMEM((slots * chip_rows, group * occ_count), jnp.float32)] * groups,
        compiler_params=limit,
        cost_estimate=pl.CostEstimate(
            flops=2 * work, bytes_accessed=2 * chol.size, transcendentals=0
        ),
        name="far",
    )(block_index, place, weights, near_sums, late, *far_pieces)

    coming, _ = lax.optimization_barrier((coming, all_sums))
    new_green = pl.pallas_call(
        functools.partial(
            assemble_kernel, (slots, share_rows, orb_count, walkers, moves, keep)
        ),
        out_shape=jax.ShapeDtypeStruct((keep, share_width), jnp.bfloat16),
        in_specs=[smem] * 2 + [vmem] * walkers,
        out_specs=vmem,
        scratch_shapes=[
            pltpu.VMEM((orb_count // LANES, share_rows * ROWS, LANES), jnp.float32),
            pltpu.VMEM(((slots + walkers - 1) * share_rows, orb_count), jnp.float32),
            pltpu.VMEM((orb_count // LANES, share_rows * ROWS, LANES), jnp.float32),
        ],
        compiler_params=limit,
        name="assemble",
    )(walker_index, table, green, *coming)

    energy_scale = 0.5 / (occ_count * math.sqrt(vectors * blocks))
    got = lax.all_to_all(
        all_sums, ("block", "walker"), split_axis=0, concat_axis=0, tiled=True
    )
    got_sums = jnp.sum(got, axis=0)
    own_sums = lax.dynamic_slice(got_sums, (walker_index[0] * keep,), (keep,))
    return (new_green, -energy_scale * own_sums)


def fits(mesh):
    blocks = mesh.shape["block"]
    walkers = mesh.shape["walker"]

    def check(green, chol, counts, move_slot, move_dest):
        vectors, occ_count, orb_count = chol.shape
        share_width = green.shape[1] // blocks
        moves = move_slot.shape[1]
        slots = green.shape[0] // walkers
        return (
            blocks == 8
            and walkers >= 2
            and walkers & (walkers - 1) == 0
            and (moves + walkers - 2) // (walkers - 1) == 1
            and slots <= ROWS
            and share_width % (orb_count * ROWS) == 0
            and orb_count % (2 * LANES) == 0
            and occ_count == blocks * (share_width // orb_count)
            and occ_count == LANES + LANES // 2
            and (vectors // blocks) % 4 == 0
            and walkers * (slots - moves) <= LANES
        )

    return check


def solution(mesh):
    in_specs = (P("walker", "block"), P("block", None, None), P(), P(), P())
    out_specs = (P("walker", "block"), P("walker"))
    check = fits(mesh)

    def run(*args):
        chosen = body if check(*args) else general_body
        return jax.shard_map(
            chosen, mesh=mesh, in_specs=in_specs, out_specs=out_specs, check_vma=False
        )(*args)

    return run
```

```python
import functools
import math

import jax
import jax.numpy as jnp
from jax import lax
from jax.experimental import pallas as pl
from jax.experimental.pallas import tpu as pltpu
from jax.sharding import PartitionSpec as P


def arrival_ranks(move_slot, move_dest):
    active = move_slot >= 0
    move_total = move_slot.shape[1]
    earlier = jnp.arange(move_total)[None, :] < jnp.arange(move_total)[:, None]
    same_target = (
        (move_dest[:, :, None] == move_dest[:, None, :]) & earlier[None, :, :] & active[:, None, :]
    )
    return (active, jnp.sum(same_target.astype(jnp.int32), axis=2))


def general_body(green, chol, counts, move_slot, move_dest):
    walker_total = lax.axis_size("walker")
    own_index = lax.axis_index("walker")
    slot_total = green.shape[0]
    share_width = green.shape[1]
    keep_total = slot_total - move_slot.shape[1]
    capacity = (move_slot.shape[1] + walker_total - 2) // (walker_total - 1)
    occ_count = chol.shape[1]
    orb_count = chol.shape[2]
    energy_scale = 0.5 / (occ_count * math.sqrt(chol.shape[0] * lax.axis_size("block")))
    active, move_rank = arrival_ranks(move_slot, move_dest)
    own_slots = move_slot[own_index]
    own_dests = move_dest[own_index]
    own_active = active[own_index]
    own_rank = move_rank[own_index]
    peer_ids = jnp.arange(walker_total)
    place_ids = jnp.arange(capacity)
    chosen = (
        (own_dests[None, None, :] == peer_ids[:, None, None])
        & (own_rank[None, None, :] == place_ids[None, :, None])
        & own_active[None, None, :]
    )
    send_slot = jnp.sum(jnp.where(chosen, own_slots[None, None, :], 0), axis=2).reshape(-1)
    present = jnp.any(chosen, axis=2).reshape(-1)
    arrive = jnp.any(
        (move_dest[:, None, :] == own_index)
        & (move_rank[:, None, :] == place_ids[None, :, None])
        & active[:, None, :],
        axis=2,
    ).reshape(-1)
    slot_ids = jnp.arange(slot_total)
    occupied = slot_ids < counts[own_index]
    leaving = jnp.any(own_slots[:, None] == slot_ids[None, :], axis=0)
    staying = occupied & jnp.logical_not(leaving)
    stay_rank = jnp.cumsum(staying.astype(jnp.int32)) - 1
    arrive_rank = jnp.cumsum(arrive.astype(jnp.int32)) - 1
    stay_total = jnp.sum(staying.astype(jnp.int32))
    targets = jnp.arange(keep_total)
    from_stay = jnp.sum(
        jnp.where(
            staying[None, :] & (stay_rank[None, :] == targets[:, None]), slot_ids[None, :], 0
        ),
        axis=1,
    )
    arrive_ids = jnp.arange(arrive.shape[0]) + slot_total
    from_arrive = jnp.sum(
        jnp.where(
            arrive[None, :] & (arrive_rank[None, :] == (targets - stay_total)[:, None]),
            arrive_ids[None, :],
            0,
        ),
        axis=1,
    )
    source_row = jnp.where(targets < stay_total, from_stay, from_arrive)
    outgoing = jnp.where(
        present[:, None], jnp.take(green, send_slot, axis=0), jnp.zeros((), jnp.bfloat16)
    )
    outgoing = outgoing.reshape(walker_total, capacity, share_width)

    def walker_energy(walker_row):
        green_mat = walker_row.reshape(occ_count, orb_count)
        transfer = jnp.einsum("gip,jp->gij", chol, green_mat, preferred_element_type=jnp.float32)
        return jnp.sum(transfer * jnp.swapaxes(transfer, 1, 2))

    got_rows = lax.all_to_all(outgoing, "walker", split_axis=0, concat_axis=0, tiled=True)
    source_pool = jnp.concatenate([green, got_rows.reshape(-1, share_width)], axis=0)
    new_green = jnp.take(source_pool, source_row, axis=0)
    complete = lax.all_gather(new_green, "block", axis=1, tiled=True)
    partial_value = lax.map(walker_energy, complete)
    energy = -energy_scale * lax.psum(partial_value, "block")
    return (new_green, energy)


LANES = 128
ROWS = 8


def spread_slots(green_ref, spread, share_rows):
    slots = green_ref.shape[0]
    tiles = spread.shape[0]
    for row in range(share_rows):
        for tile in range(tiles):
            col = (row * tiles + tile) * LANES
            block = green_ref[:, col : col + LANES].astype(jnp.float32)
            spread[tile, row * ROWS : row * ROWS + slots, :] = block


def pack_kernel(dims, green_ref, own_ref, spread):
    slots, share_rows, orb_count, pad_rows = dims
    spread_slots(green_ref, spread, share_rows)
    for tile in range(orb_count // LANES):
        dense = [spread[tile, pl.ds(slot, share_rows, stride=ROWS), :] for slot in range(slots)]
        if pad_rows > slots * share_rows:
            dense.append(jnp.zeros((pad_rows - slots * share_rows, LANES), jnp.float32))
        packed = jnp.concatenate(dense, axis=0).astype(jnp.bfloat16)
        own_ref[:, tile * LANES : (tile + 1) * LANES] = packed


class Moves:
    def __init__(self, table_ref, moves):
        self.table, self.moves = table_ref, moves

    def count(self, device):
        return self.table[0, device]

    def slot(self, device, move):
        return self.table[1 + move, device]

    def dest(self, device, move):
        return self.table[1 + self.moves + move, device]

    def staying(self, device):
        total = self.count(device)
        for move in range(self.moves):
            total = total - jnp.where(self.slot(device, move) >= 0, 1, 0)
        return total

    def goes_to(self, own, slot):
        target = jnp.int32(-1)
        for move in range(self.moves):
            target = jnp.where(self.slot(own, move) == slot, self.dest(own, move), target)
        return target


def assemble_kernel(dims, ident_ref, table_ref, green_ref, *refs):
    slots, share_rows, orb_count, walkers, moves, keep = dims
    table = Moves(table_ref, moves)
    come_refs = refs[: walkers - 1]
    new_ref, spread, pool, out = refs[walkers - 1 :]
    own = ident_ref[0]
    tiles = orb_count // LANES
    spread_slots(green_ref, spread, share_rows)
    for slot in range(slots):
        for tile in range(tiles):
            pool[
                slot * share_rows : (slot + 1) * share_rows, tile * LANES : (tile + 1) * LANES
            ] = spread[tile, pl.ds(slot, share_rows, stride=ROWS), :]
    for shift in range(1, walkers):
        start = (slots + shift - 1) * share_rows
        pool[start : start + share_rows, :] = come_refs[shift - 1][...].astype(jnp.float32)

    sources = [jnp.int32(0)] * keep
    rank = jnp.int32(0)
    for slot in range(slots):
        stays = (slot < table.count(own)) & (table.goes_to(own, slot) < 0)
        for target in range(keep):
            sources[target] = jnp.where(stays & (rank == target), slot, sources[target])
        rank = rank + jnp.where(stays, 1, 0)
    for device in range(walkers):
        comes = jnp.bool_(False)
        for move in range(moves):
            comes = comes | ((table.dest(device, move) == own) & (table.slot(device, move) >= 0))
        comes = comes & (device != own)
        shift = lax.rem(own - device + walkers, walkers)
        for target in range(keep):
            sources[target] = jnp.where(
                comes & (rank == target), slots + shift - 1, sources[target]
            )
        rank = rank + jnp.where(comes, 1, 0)
    for target in range(keep):
        start = pl.multiple_of(sources[target] * share_rows, ROWS)
        for tile in range(tiles):
            out[tile, pl.ds(target, share_rows, stride=ROWS), :] = pool[
                pl.ds(start, share_rows), tile * LANES : (tile + 1) * LANES
            ]
    for row in range(share_rows):
        for tile in range(tiles):
            col = (row * tiles + tile) * LANES
            new_ref[:, col : col + LANES] = out[
                tile, row * ROWS : row * ROWS + keep, :
            ].astype(jnp.bfloat16)


def times(left, right):
    return lax.dot_general(
        left, right, (((1,), (1,)), ((), ())), preferred_element_type=jnp.float32
    )


def find_places(dims, own, table, place_ref):
    slots, walkers, moves, keep = dims
    rank = jnp.int32(0)
    for slot in range(slots):
        live = slot < table.count(own)
        gone_to = table.goes_to(own, slot)
        stays = live & (gone_to < 0)
        there = jnp.maximum(gone_to, 0)
        ahead = table.staying(there)
        for device in range(walkers):
            for move in range(moves):
                hit = (
                    (device < own)
                    & (table.dest(device, move) == there)
                    & (table.slot(device, move) >= 0)
                )
                ahead = ahead + jnp.where(hit, 1, 0)
        place = jnp.where(stays, own * ROWS + rank, there * ROWS + ahead)
        place_ref[slot] = jnp.where(live, place, -1)
        rank = rank + jnp.where(stays, 1, 0)


def leave_kernel(dims, walker_ref, table_ref, own_ref, *refs):
    share_rows, walkers, moves = dims
    leave_refs, wide = refs[:-1], refs[-1]
    table = Moves(table_ref, moves)
    own = walker_ref[0]
    wide[...] = own_ref[...].astype(jnp.float32)
    for shift in range(1, walkers):
        target = lax.rem(own + shift, walkers)
        chosen = jnp.int32(0)
        for move in range(moves):
            hit = (table.dest(own, move) == target) & (table.slot(own, move) >= 0)
            chosen = jnp.where(hit, table.slot(own, move), chosen)
        start = pl.multiple_of(chosen * share_rows, ROWS)
        leave_refs[shift - 1][...] = wide[pl.ds(start, share_rows), :].astype(jnp.bfloat16)


def home_kernel(dims, ident_ref, walker_ref, table_ref, chol_ref, own_ref, core_ref, *refs):
    slots, share_rows, group, groups, chip_rows, walkers, moves, keep = dims
    weight_ref, home_ref, place_ref = refs
    chip, core = ident_ref[0] // 2, lax.rem(ident_ref[0], 2)
    edge = LANES - 2 * chip_rows
    rest = 2 * chip_rows - edge
    size = group * 4 * chip_rows

    def rows_of(vec, distance, start, count):
        row = pl.multiple_of(jnp.bitwise_xor(chip, distance) * chip_rows + start, 16)
        return chol_ref[vec, pl.ds(row, count), :]

    def put(place, value):
        weight_ref[place : place + value.shape[0], :] = value

    for index in range(groups):
        for item in range(group):
            vec = index * group + item
            place = index * size + item * LANES
            put(place, rows_of(vec, 0, 0, chip_rows))
            put(place + chip_rows, rows_of(vec, 1, 0, chip_rows))
            put(place + 2 * chip_rows, rows_of(vec, 2, 0, edge))
            place = index * size + group * LANES + item * rest
            put(place, rows_of(vec, 2, edge, chip_rows - edge))
            put(place + chip_rows - edge, rows_of(vec, 3, 0, chip_rows))

    table = Moves(table_ref, moves)
    own = walker_ref[0]
    find_places((slots, walkers, moves, keep), own, table, place_ref)

    pad_rows = own_ref.shape[0]
    left = jnp.concatenate([own_ref[...], core_ref[...]], axis=0)
    for index in range(groups):
        cols = slice(index * size, (index + 1) * size)
        result = times(left, weight_ref[cols, :])
        for piece in range(2):
            source = jnp.bitwise_xor(core, piece)
            for slot in range(slots):
                start = piece * pad_rows + slot * share_rows
                place = pl.multiple_of(slot * chip_rows + source * share_rows, ROWS)
                home_ref[pl.ds(place, share_rows), cols] = result[start : start + share_rows, :]


def near_kernel(dims, ident_ref, weight_ref, home_ref, *refs):
    slots, share_rows, group, groups, chip_rows = dims
    piece_refs = refs[:4]
    sum_ref, late_ref = refs[4:6]
    trans_refs = refs[6:]
    own = ident_ref[0]
    core = lax.rem(own, 2)
    pad_rows = piece_refs[0].shape[0]
    away = 2 * chip_rows
    size = 4 * chip_rows * group
    edge = 3 * chip_rows - LANES
    half = LANES // 2
    left = jnp.concatenate([ref[...] for ref in piece_refs], axis=0)
    lane = lax.broadcasted_iota(jnp.int32, (1, LANES), 1)
    low_half = lane < half
    in_edge = jnp.where(low_half, lane, lane - half) < edge
    sums = [jnp.zeros((ROWS, LANES), jnp.float32) for _ in range(slots)]

    def fold(value):
        return jnp.sum(value.reshape(-1, ROWS, LANES), axis=0)

    for index in range(groups):
        trans = trans_refs[index]
        result = times(left, weight_ref[index * size : (index + 1) * size, :])
        for piece in range(4):
            source = jnp.bitwise_xor(core, piece % 2)
            for slot in range(slots):
                start = piece * pad_rows + slot * share_rows
                place = slot * away + (piece // 2) * chip_rows + source * share_rows
                trans[pl.ds(pl.multiple_of(place, ROWS), share_rows), :] = result[
                    start : start + share_rows, :
                ]
        for slot in range(slots):
            late = slice(slot * chip_rows, (slot + 1) * chip_rows)

            def head(col):
                first = home_ref[late, index * size + col : index * size + col + LANES]
                second = trans[slot * away : slot * away + LANES - chip_rows, col : col + LANES]
                return jnp.concatenate([first, second], axis=0)

            def tail(col):
                base = (slot + 1) * away
                return trans[base - edge : base, col : col + LANES]

            acc = sums[slot]
            for pair in range(group // 2):
                col = (group + pair) * LANES
                top = head(col).T
                edge_rows = tail(col)
                gap = jnp.zeros((half - edge, LANES), jnp.float32)
                bottom = jnp.concatenate([edge_rows, gap, edge_rows, gap], axis=0).T
                for side in range(2):
                    vec = 2 * pair + side
                    high = head(vec * LANES)
                    acc = acc + fold(high * high.T)
                    across = tail(vec * LANES)
                    acc = acc + 2.0 * fold(across * top[side * half : side * half + edge, :])
                    late_ref[
                        late, (index * (group + group // 2) + vec) * LANES : (
                            index * (group + group // 2) + vec + 1
                        ) * LANES
                    ] = top[side * half + edge : (side + 1) * half, :]
                corner = jnp.where(low_half, bottom[:edge, :], bottom[half : half + edge, :])
                acc = acc + fold(jnp.where(in_edge, edge_rows * corner, 0.0))
                rest = jnp.where(low_half, bottom[edge:half, :], bottom[half + edge :, :])
                place = (index * (group + group // 2) + group + pair) * LANES
                late_ref[late, place : place + LANES] = jnp.where(in_edge, rest, 0.0)
            sums[slot] = acc
    sum_ref[...] = jnp.concatenate(sums, axis=0)


def far_kernel(dims, ident_ref, place_ref, weight_ref, near_sum_ref, late_ref, *refs):
    slots, share_rows, group, groups, chip_rows = dims
    piece_refs = refs[:4]
    sum_ref = refs[4]
    rows_ref, trans_refs = refs[5], refs[6:]
    own = ident_ref[0]
    core = lax.rem(own, 2)
    pad_rows, width = piece_refs[0].shape
    half = LANES // 2
    edge = half - chip_rows
    size = 4 * chip_rows * group
    lane = lax.broadcasted_iota(jnp.int32, (1, LANES), 1)
    low_half = lane < half
    in_rest = jnp.where(low_half, lane, lane - half) >= edge
    lefts = [
        jnp.concatenate([piece_refs[part][...], piece_refs[2 + part][...]], axis=0)
        for part in range(2)
    ]
    twice = [jnp.zeros((ROWS, LANES), jnp.float32) for _ in range(slots)]
    once = [near_sum_ref[slot * ROWS : (slot + 1) * ROWS, :] for slot in range(slots)]

    def fold(value):
        return jnp.sum(value.reshape(-1, ROWS, LANES), axis=0)

    tiles = group + group // 2
    for index in range(groups):
        trans = trans_refs[index]
        rows = slice(index * size, (index + 1) * size)
        result = times(lefts[0], weight_ref[rows, :width])
        result = result + times(lefts[1], weight_ref[rows, width:])
        for piece in range(2):
            source = jnp.bitwise_xor(core, piece)
            for slot in range(slots):
                start = piece * pad_rows + slot * share_rows
                place = slot * chip_rows + source * share_rows
                trans[pl.ds(pl.multiple_of(place, ROWS), share_rows), :] = result[
                    start : start + share_rows, :
                ]
        for slot in range(slots):
            rows = slice(slot * chip_rows, (slot + 1) * chip_rows)
            for tile in range(tiles):
                here = trans[rows, tile * LANES : (tile + 1) * LANES]
                met = late_ref[rows, (index * tiles + tile) * LANES : (index * tiles + tile + 1) * LANES]
                twice[slot] = twice[slot] + fold(here * met)
                if tile >= group:
                    gap = jnp.zeros((edge, LANES), jnp.float32)
                    turned = jnp.concatenate([gap, here, gap, here], axis=0).T
                    corner = jnp.where(low_half, turned[edge:half, :], turned[half + edge :, :])
                    once[slot] = once[slot] + fold(jnp.where(in_rest, here * corner, 0.0))
    rows_ref[...] = jnp.zeros_like(rows_ref)
    for slot in range(slots):
        slot_sum = jnp.sum(once[slot] + 2.0 * twice[slot], axis=0, keepdims=True)
        place = place_ref[slot]

        @pl.when(place >= 0)
        def _():
            rows_ref[pl.ds(place, 1), :] = slot_sum

    devices = sum_ref.shape[0]
    walkers = rows_ref.shape[0] // ROWS
    for device in range(devices):
        walker = device % walkers
        sum_ref[device] = rows_ref[walker * ROWS : (walker + 1) * ROWS, :]


def swap(value, mask, blocks):
    return lax.ppermute(value, "block", [(index, index ^ mask) for index in range(blocks)])


def body(green, chol, counts, move_slot, move_dest):
    walkers = lax.axis_size("walker")
    blocks = lax.axis_size("block")
    slots, share_width = green.shape
    vectors, occ_count, orb_count = chol.shape
    moves = move_slot.shape[1]
    keep = slots - moves
    share_rows = share_width // orb_count
    pad_rows = -(-slots * share_rows // 16) * 16
    table = jnp.concatenate([counts[None, :], move_slot.T, move_dest.T], axis=0)
    walker_index = lax.axis_index("walker").astype(jnp.int32).reshape(1)
    block_index = lax.axis_index("block").astype(jnp.int32).reshape(1)
    smem = pl.BlockSpec(memory_space=pltpu.SMEM)
    vmem = pl.BlockSpec(memory_space=pltpu.VMEM)
    limit = pltpu.CompilerParams(vmem_limit_bytes=32 * 1024 * 1024)

    spread = pltpu.VMEM((orb_count // LANES, share_rows * ROWS, LANES), jnp.float32)
    own_rows = pl.pallas_call(
        functools.partial(pack_kernel, (slots, share_rows, orb_count, pad_rows)),
        out_shape=jax.ShapeDtypeStruct((pad_rows, orb_count), jnp.bfloat16),
        in_specs=[vmem],
        out_specs=vmem,
        scratch_shapes=[spread],
        compiler_params=limit,
        cost_estimate=pl.CostEstimate(
            flops=3 * pad_rows * chol.size, bytes_accessed=4 * chol.size, transcendentals=0
        ),
        name="pack",
    )(green)
    leaving = pl.pallas_call(
        functools.partial(leave_kernel, (share_rows, walkers, moves)),
        out_shape=[jax.ShapeDtypeStruct((share_rows, orb_count), jnp.bfloat16)] * (walkers - 1),
        in_specs=[smem, smem, vmem],
        out_specs=[vmem] * (walkers - 1),
        scratch_shapes=[pltpu.VMEM((pad_rows, orb_count), jnp.float32)],
        compiler_params=limit,
        cost_estimate=pl.CostEstimate(
            flops=3 * pad_rows * chol.size, bytes_accessed=4 * chol.size, transcendentals=0
        ),
        name="leave",
    )(walker_index, table, own_rows)
    core, near_x, near_y = 1, 2, 4
    from_x = swap(own_rows, near_x, blocks)
    from_y = swap(own_rows, near_y, blocks)
    from_core = swap(own_rows, core, blocks)
    group = 4
    groups = vectors // group
    chip_rows = 2 * share_rows
    home_dims = (slots, share_rows, group, groups, chip_rows, walkers, moves, keep)
    weights, home, place = pl.pallas_call(
        functools.partial(home_kernel, home_dims),
        out_shape=[
            jax.ShapeDtypeStruct((vectors * occ_count, orb_count), jnp.bfloat16),
            jax.ShapeDtypeStruct((slots * chip_rows, vectors * occ_count), jnp.float32),
            jax.ShapeDtypeStruct((slots,), jnp.int32),
        ],
        in_specs=[smem] * 3 + [vmem] * 3,
        out_specs=[vmem] * 2 + [smem],
        compiler_params=limit,
        cost_estimate=pl.CostEstimate(
            flops=4 * vectors * occ_count * orb_count * pad_rows,
            bytes_accessed=4 * chol.size,
            transcendentals=0,
        ),
        name="home",
    )(block_index, walker_index, table, chol, own_rows, from_core)
    coming = [
        lax.ppermute(
            leaving[shift - 1], "walker", [(z, (z + shift) % walkers) for z in range(walkers)]
        )
        for shift in range(1, walkers)
    ]
    width = orb_count // 2
    from_x, from_y, weights, coming[:2] = lax.optimization_barrier(
        (from_x, from_y, weights, coming[:2])
    )
    far = [swap(from_y[:, :width], near_x, blocks), swap(from_x[:, width:], near_y, blocks)]
    near_pieces = []
    for piece in (from_x, from_y):
        near_pieces += [piece, swap(piece, core, blocks)]

    dims = (slots, share_rows, group, groups, chip_rows)
    work = 2 * vectors * occ_count * orb_count * pad_rows
    near_sums, late = pl.pallas_call(
        functools.partial(near_kernel, dims),
        out_shape=[
            jax.ShapeDtypeStruct((slots * ROWS, LANES), jnp.float32),
            jax.ShapeDtypeStruct((slots * chip_rows, vectors * occ_count), jnp.float32),
        ],
        in_specs=[smem] + [vmem] * 6,
        out_specs=[vmem] * 2,
        scratch_shapes=[pltpu.VMEM((slots * 2 * chip_rows, group * occ_count), jnp.float32)]
        * groups,
        compiler_params=limit,
        cost_estimate=pl.CostEstimate(
            flops=4 * work, bytes_accessed=2 * chol.size, transcendentals=0
        ),
        name="near",
    )(block_index, weights, home, *near_pieces)
    far, near_sums = lax.optimization_barrier((far, near_sums))
    far_pieces = far + [swap(piece, core, blocks) for piece in far]
    all_sums = pl.pallas_call(
        functools.partial(far_kernel, dims),
        out_shape=jax.ShapeDtypeStruct((blocks * walkers, ROWS, LANES), jnp.float32),
        in_specs=[smem] * 2 + [vmem] * 7,
        out_specs=vmem,
        scratch_shapes=[pltpu.VMEM((walkers * ROWS, LANES), jnp.float32)]
        + [pltpu.VMEM((slots * chip_rows, group * occ_count), jnp.float32)] * groups,
        compiler_params=limit,
        cost_estimate=pl.CostEstimate(
            flops=2 * work, bytes_accessed=2 * chol.size, transcendentals=0
        ),
        name="far",
    )(block_index, place, weights, near_sums, late, *far_pieces)

    coming, _ = lax.optimization_barrier((coming, all_sums))
    new_green = pl.pallas_call(
        functools.partial(
            assemble_kernel, (slots, share_rows, orb_count, walkers, moves, keep)
        ),
        out_shape=jax.ShapeDtypeStruct((keep, share_width), jnp.bfloat16),
        in_specs=[smem] * 2 + [vmem] * walkers,
        out_specs=vmem,
        scratch_shapes=[
            pltpu.VMEM((orb_count // LANES, share_rows * ROWS, LANES), jnp.float32),
            pltpu.VMEM(((slots + walkers - 1) * share_rows, orb_count), jnp.float32),
            pltpu.VMEM((orb_count // LANES, share_rows * ROWS, LANES), jnp.float32),
        ],
        compiler_params=limit,
        name="assemble",
    )(walker_index, table, green, *coming)

    energy_scale = 0.5 / (occ_count * math.sqrt(vectors * blocks))
    got = lax.all_to_all(
        all_sums, ("block", "walker"), split_axis=0, concat_axis=0, tiled=True
    )
    own_sums = jnp.sum(got, axis=(0, 2))[:keep]
    return (new_green, -energy_scale * own_sums)


def fits(mesh):
    blocks = mesh.shape["block"]
    walkers = mesh.shape["walker"]

    def check(green, chol, counts, move_slot, move_dest):
        vectors, occ_count, orb_count = chol.shape
        share_width = green.shape[1] // blocks
        moves = move_slot.shape[1]
        slots = green.shape[0] // walkers
        return (
            blocks == 8
            and walkers >= 2
            and walkers & (walkers - 1) == 0
            and (moves + walkers - 2) // (walkers - 1) == 1
            and slots <= ROWS
            and share_width % (orb_count * ROWS) == 0
            and orb_count % (2 * LANES) == 0
            and occ_count == blocks * (share_width // orb_count)
            and occ_count == LANES + LANES // 2
            and (vectors // blocks) % 4 == 0
        )

    return check


def solution(mesh):
    in_specs = (P("walker", "block"), P("block", None, None), P(), P(), P())
    out_specs = (P("walker", "block"), P("walker"))
    check = fits(mesh)

    def run(*args):
        chosen = body if check(*args) else general_body
        return jax.shard_map(
            chosen, mesh=mesh, in_specs=in_specs, out_specs=out_specs, check_vma=False
        )(*args)

    return run
```

```python
import functools
import math

import jax
import jax.numpy as jnp
from jax import lax
from jax.experimental import pallas as pl
from jax.experimental.pallas import tpu as pltpu
from jax.sharding import PartitionSpec as P


def arrival_ranks(move_slot, move_dest):
    active = move_slot >= 0
    move_total = move_slot.shape[1]
    earlier = jnp.arange(move_total)[None, :] < jnp.arange(move_total)[:, None]
    same_target = (
        (move_dest[:, :, None] == move_dest[:, None, :]) & earlier[None, :, :] & active[:, None, :]
    )
    return (active, jnp.sum(same_target.astype(jnp.int32), axis=2))


def general_body(green, chol, counts, move_slot, move_dest):
    walker_total = lax.axis_size("walker")
    own_index = lax.axis_index("walker")
    slot_total = green.shape[0]
    share_width = green.shape[1]
    keep_total = slot_total - move_slot.shape[1]
    capacity = (move_slot.shape[1] + walker_total - 2) // (walker_total - 1)
    occ_count = chol.shape[1]
    orb_count = chol.shape[2]
    energy_scale = 0.5 / (occ_count * math.sqrt(chol.shape[0] * lax.axis_size("block")))
    active, move_rank = arrival_ranks(move_slot, move_dest)
    own_slots = move_slot[own_index]
    own_dests = move_dest[own_index]
    own_active = active[own_index]
    own_rank = move_rank[own_index]
    peer_ids = jnp.arange(walker_total)
    place_ids = jnp.arange(capacity)
    chosen = (
        (own_dests[None, None, :] == peer_ids[:, None, None])
        & (own_rank[None, None, :] == place_ids[None, :, None])
        & own_active[None, None, :]
    )
    send_slot = jnp.sum(jnp.where(chosen, own_slots[None, None, :], 0), axis=2).reshape(-1)
    present = jnp.any(chosen, axis=2).reshape(-1)
    arrive = jnp.any(
        (move_dest[:, None, :] == own_index)
        & (move_rank[:, None, :] == place_ids[None, :, None])
        & active[:, None, :],
        axis=2,
    ).reshape(-1)
    slot_ids = jnp.arange(slot_total)
    occupied = slot_ids < counts[own_index]
    leaving = jnp.any(own_slots[:, None] == slot_ids[None, :], axis=0)
    staying = occupied & jnp.logical_not(leaving)
    stay_rank = jnp.cumsum(staying.astype(jnp.int32)) - 1
    arrive_rank = jnp.cumsum(arrive.astype(jnp.int32)) - 1
    stay_total = jnp.sum(staying.astype(jnp.int32))
    targets = jnp.arange(keep_total)
    from_stay = jnp.sum(
        jnp.where(
            staying[None, :] & (stay_rank[None, :] == targets[:, None]), slot_ids[None, :], 0
        ),
        axis=1,
    )
    arrive_ids = jnp.arange(arrive.shape[0]) + slot_total
    from_arrive = jnp.sum(
        jnp.where(
            arrive[None, :] & (arrive_rank[None, :] == (targets - stay_total)[:, None]),
            arrive_ids[None, :],
            0,
        ),
        axis=1,
    )
    source_row = jnp.where(targets < stay_total, from_stay, from_arrive)
    outgoing = jnp.where(
        present[:, None], jnp.take(green, send_slot, axis=0), jnp.zeros((), jnp.bfloat16)
    )
    outgoing = outgoing.reshape(walker_total, capacity, share_width)

    def walker_energy(walker_row):
        green_mat = walker_row.reshape(occ_count, orb_count)
        transfer = jnp.einsum("gip,jp->gij", chol, green_mat, preferred_element_type=jnp.float32)
        return jnp.sum(transfer * jnp.swapaxes(transfer, 1, 2))

    got_rows = lax.all_to_all(outgoing, "walker", split_axis=0, concat_axis=0, tiled=True)
    source_pool = jnp.concatenate([green, got_rows.reshape(-1, share_width)], axis=0)
    new_green = jnp.take(source_pool, source_row, axis=0)
    complete = lax.all_gather(new_green, "block", axis=1, tiled=True)
    partial_value = lax.map(walker_energy, complete)
    energy = -energy_scale * lax.psum(partial_value, "block")
    return (new_green, energy)


LANES = 128
ROWS = 8


def spread_slots(green_ref, spread, share_rows):
    slots = green_ref.shape[0]
    tiles = spread.shape[0]
    for row in range(share_rows):
        for tile in range(tiles):
            col = (row * tiles + tile) * LANES
            block = green_ref[:, col : col + LANES].astype(jnp.float32)
            spread[tile, row * ROWS : row * ROWS + slots, :] = block


def pack_kernel(dims, green_ref, own_ref, spread):
    slots, share_rows, orb_count, pad_rows = dims
    spread_slots(green_ref, spread, share_rows)
    for tile in range(orb_count // LANES):
        dense = [spread[tile, pl.ds(slot, share_rows, stride=ROWS), :] for slot in range(slots)]
        if pad_rows > slots * share_rows:
            dense.append(jnp.zeros((pad_rows - slots * share_rows, LANES), jnp.float32))
        packed = jnp.concatenate(dense, axis=0).astype(jnp.bfloat16)
        own_ref[:, tile * LANES : (tile + 1) * LANES] = packed


class Moves:
    def __init__(self, table_ref, moves):
        self.table, self.moves = table_ref, moves

    def count(self, device):
        return self.table[0, device]

    def slot(self, device, move):
        return self.table[1 + move, device]

    def dest(self, device, move):
        return self.table[1 + self.moves + move, device]

    def staying(self, device):
        total = self.count(device)
        for move in range(self.moves):
            total = total - jnp.where(self.slot(device, move) >= 0, 1, 0)
        return total

    def goes_to(self, own, slot):
        target = jnp.int32(-1)
        for move in range(self.moves):
            target = jnp.where(self.slot(own, move) == slot, self.dest(own, move), target)
        return target


def leave_kernel(dims, ident_ref, table_ref, own_ref, *refs):
    slots, share_rows, orb_count, walkers, moves, keep = dims
    leave_refs, place_ref, wide = refs[:-2], refs[-2], refs[-1]
    table = Moves(table_ref, moves)
    wide[...] = own_ref[...].astype(jnp.float32)
    own = ident_ref[0]
    for shift in range(1, walkers):
        target = lax.rem(own + shift, walkers)
        chosen = jnp.int32(0)
        for move in range(moves):
            hit = (table.dest(own, move) == target) & (table.slot(own, move) >= 0)
            chosen = jnp.where(hit, table.slot(own, move), chosen)
        start = pl.multiple_of(chosen * share_rows, ROWS)
        leave_refs[shift - 1][...] = wide[pl.ds(start, share_rows), :].astype(jnp.bfloat16)
    rank = jnp.int32(0)
    for slot in range(slots):
        live = slot < table.count(own)
        gone_to = table.goes_to(own, slot)
        stays = live & (gone_to < 0)
        there = jnp.maximum(gone_to, 0)
        ahead = table.staying(there)
        for device in range(walkers):
            for move in range(moves):
                hit = (
                    (device < own)
                    & (table.dest(device, move) == there)
                    & (table.slot(device, move) >= 0)
                )
                ahead = ahead + jnp.where(hit, 1, 0)
        place = jnp.where(stays, own * keep + rank, there * keep + ahead)
        place_ref[slot] = jnp.where(live, place, -1)
        rank = rank + jnp.where(stays, 1, 0)


def assemble_kernel(dims, ident_ref, table_ref, green_ref, *refs):
    slots, share_rows, orb_count, walkers, moves, keep = dims
    table = Moves(table_ref, moves)
    come_refs = refs[: walkers - 1]
    new_ref, spread, pool, out = refs[walkers - 1 :]
    own = ident_ref[0]
    tiles = orb_count // LANES
    spread_slots(green_ref, spread, share_rows)
    for slot in range(slots):
        for tile in range(tiles):
            pool[
                slot * share_rows : (slot + 1) * share_rows, tile * LANES : (tile + 1) * LANES
            ] = spread[tile, pl.ds(slot, share_rows, stride=ROWS), :]
    for shift in range(1, walkers):
        start = (slots + shift - 1) * share_rows
        pool[start : start + share_rows, :] = come_refs[shift - 1][...].astype(jnp.float32)

    sources = [jnp.int32(0)] * keep
    rank = jnp.int32(0)
    for slot in range(slots):
        stays = (slot < table.count(own)) & (table.goes_to(own, slot) < 0)
        for target in range(keep):
            sources[target] = jnp.where(stays & (rank == target), slot, sources[target])
        rank = rank + jnp.where(stays, 1, 0)
    for device in range(walkers):
        comes = jnp.bool_(False)
        for move in range(moves):
            comes = comes | ((table.dest(device, move) == own) & (table.slot(device, move) >= 0))
        comes = comes & (device != own)
        shift = lax.rem(own - device + walkers, walkers)
        for target in range(keep):
            sources[target] = jnp.where(
                comes & (rank == target), slots + shift - 1, sources[target]
            )
        rank = rank + jnp.where(comes, 1, 0)
    for target in range(keep):
        start = pl.multiple_of(sources[target] * share_rows, ROWS)
        for tile in range(tiles):
            out[tile, pl.ds(target, share_rows, stride=ROWS), :] = pool[
                pl.ds(start, share_rows), tile * LANES : (tile + 1) * LANES
            ]
    for row in range(share_rows):
        for tile in range(tiles):
            col = (row * tiles + tile) * LANES
            new_ref[:, col : col + LANES] = out[
                tile, row * ROWS : row * ROWS + keep, :
            ].astype(jnp.bfloat16)


def order_kernel(dims, ident_ref, chol_ref, own_ref, out_ref, sems):
    del own_ref
    group, groups, chip_rows = dims
    chip = ident_ref[0] // 2
    edge = LANES - 2 * chip_rows
    rest = 2 * chip_rows - edge
    copies = []

    def add(vec, distance, start, size, place):
        row = pl.multiple_of(jnp.bitwise_xor(chip, distance) * chip_rows + start, 16)
        copies.append(
            pltpu.make_async_copy(
                chol_ref.at[vec, pl.ds(row, size), :],
                out_ref.at[pl.ds(place, size), :],
                sems.at[len(copies)],
            )
        )

    for index in range(groups):
        for item in range(group):
            vec = index * group + item
            place = index * group * 4 * chip_rows + item * LANES
            add(vec, 0, 0, chip_rows, place)
            add(vec, 1, 0, chip_rows, place + chip_rows)
            add(vec, 2, 0, edge, place + 2 * chip_rows)
            place = index * group * 4 * chip_rows + group * LANES + item * rest
            add(vec, 2, edge, chip_rows - edge, place)
            add(vec, 3, 0, chip_rows, place + chip_rows - edge)
    for copy in copies:
        copy.start()
    for copy in copies:
        copy.wait()


def times(left, right):
    return lax.dot_general(
        left, right, (((1,), (1,)), ((), ())), preferred_element_type=jnp.float32
    )


def near_kernel(dims, ident_ref, weight_ref, *refs):
    slots, share_rows, group, groups, chip_rows = dims
    piece_refs = refs[:6]
    sum_ref, late_ref = refs[6:8]
    trans_refs = refs[8:]
    own = ident_ref[0]
    core = lax.rem(own, 2)
    pad_rows = piece_refs[0].shape[0]
    near = 3 * chip_rows
    size = 4 * chip_rows * group
    edge = near - LANES
    half = LANES // 2
    left = jnp.concatenate([ref[...] for ref in piece_refs], axis=0)
    lane = lax.broadcasted_iota(jnp.int32, (1, LANES), 1)
    low_half = lane < half
    in_edge = jnp.where(low_half, lane, lane - half) < edge
    sums = [jnp.zeros((ROWS, LANES), jnp.float32) for _ in range(slots)]

    def fold(value):
        return jnp.sum(value.reshape(-1, ROWS, LANES), axis=0)

    for index in range(groups):
        trans = trans_refs[index]
        result = times(left, weight_ref[index * size : (index + 1) * size, :])
        for piece in range(6):
            source = jnp.bitwise_xor(core, piece % 2)
            for slot in range(slots):
                start = piece * pad_rows + slot * share_rows
                place = slot * near + (piece // 2) * chip_rows + source * share_rows
                trans[pl.ds(pl.multiple_of(place, ROWS), share_rows), :] = result[
                    start : start + share_rows, :
                ]
        for slot in range(slots):
            base = slot * near
            late = slice(slot * chip_rows, (slot + 1) * chip_rows)
            acc = sums[slot]
            for pair in range(group // 2):
                col = (group + pair) * LANES
                top = trans[base : base + LANES, col : col + LANES].T
                edge_rows = trans[base + LANES : base + near, col : col + LANES]
                gap = jnp.zeros((half - edge, LANES), jnp.float32)
                bottom = jnp.concatenate([edge_rows, gap, edge_rows, gap], axis=0).T
                for side in range(2):
                    vec = 2 * pair + side
                    high = trans[base : base + LANES, vec * LANES : (vec + 1) * LANES]
                    acc = acc + fold(high * high.T)
                    across = trans[base + LANES : base + near, vec * LANES : (vec + 1) * LANES]
                    acc = acc + 2.0 * fold(across * top[side * half : side * half + edge, :])
                    late_ref[
                        late, (index * (group + group // 2) + vec) * LANES : (
                            index * (group + group // 2) + vec + 1
                        ) * LANES
                    ] = top[side * half + edge : (side + 1) * half, :]
                corner = jnp.where(low_half, bottom[:edge, :], bottom[half : half + edge, :])
                acc = acc + fold(jnp.where(in_edge, edge_rows * corner, 0.0))
                rest = jnp.where(low_half, bottom[edge:half, :], bottom[half + edge :, :])
                place = (index * (group + group // 2) + group + pair) * LANES
                late_ref[late, place : place + LANES] = jnp.where(in_edge, rest, 0.0)
            sums[slot] = acc
    sum_ref[...] = jnp.concatenate(sums, axis=0)


def far_kernel(dims, ident_ref, place_ref, weight_ref, near_sum_ref, late_ref, *refs):
    slots, share_rows, group, groups, chip_rows = dims
    piece_refs = refs[:4]
    sum_ref = refs[4]
    trans_refs = refs[5:]
    own = ident_ref[0]
    core = lax.rem(own, 2)
    pad_rows, width = piece_refs[0].shape
    half = LANES // 2
    edge = half - chip_rows
    size = 4 * chip_rows * group
    lane = lax.broadcasted_iota(jnp.int32, (1, LANES), 1)
    low_half = lane < half
    in_rest = jnp.where(low_half, lane, lane - half) >= edge
    lefts = [
        jnp.concatenate([piece_refs[part][...], piece_refs[2 + part][...]], axis=0)
        for part in range(2)
    ]
    twice = [jnp.zeros((ROWS, LANES), jnp.float32) for _ in range(slots)]
    once = [near_sum_ref[slot * ROWS : (slot + 1) * ROWS, :] for slot in range(slots)]

    def fold(value):
        return jnp.sum(value.reshape(-1, ROWS, LANES), axis=0)

    tiles = group + group // 2
    for index in range(groups):
        trans = trans_refs[index]
        rows = slice(index * size, (index + 1) * size)
        result = times(lefts[0], weight_ref[rows, :width])
        result = result + times(lefts[1], weight_ref[rows, width:])
        for piece in range(2):
            source = jnp.bitwise_xor(core, piece)
            for slot in range(slots):
                start = piece * pad_rows + slot * share_rows
                place = slot * chip_rows + source * share_rows
                trans[pl.ds(pl.multiple_of(place, ROWS), share_rows), :] = result[
                    start : start + share_rows, :
                ]
        for slot in range(slots):
            rows = slice(slot * chip_rows, (slot + 1) * chip_rows)
            for tile in range(tiles):
                here = trans[rows, tile * LANES : (tile + 1) * LANES]
                met = late_ref[rows, (index * tiles + tile) * LANES : (index * tiles + tile + 1) * LANES]
                twice[slot] = twice[slot] + fold(here * met)
                if tile >= group:
                    gap = jnp.zeros((edge, LANES), jnp.float32)
                    turned = jnp.concatenate([gap, here, gap, here], axis=0).T
                    corner = jnp.where(low_half, turned[edge:half, :], turned[half + edge :, :])
                    once[slot] = once[slot] + fold(jnp.where(in_rest, here * corner, 0.0))
    value = jnp.zeros((1, LANES), jnp.float32)
    for slot in range(slots):
        slot_sum = jnp.sum(once[slot] + 2.0 * twice[slot])
        value = jnp.where(lane == place_ref[slot], slot_sum, value)
    sum_ref[...] = jnp.broadcast_to(value, sum_ref.shape)


def swap(value, mask, blocks):
    return lax.ppermute(value, "block", [(index, index ^ mask) for index in range(blocks)])


def body(green, chol, counts, move_slot, move_dest):
    walkers = lax.axis_size("walker")
    blocks = lax.axis_size("block")
    slots, share_width = green.shape
    vectors, occ_count, orb_count = chol.shape
    moves = move_slot.shape[1]
    keep = slots - moves
    share_rows = share_width // orb_count
    pad_rows = -(-slots * share_rows // 16) * 16
    table = jnp.concatenate([counts[None, :], move_slot.T, move_dest.T], axis=0)
    walker_index = lax.axis_index("walker").astype(jnp.int32).reshape(1)
    block_index = lax.axis_index("block").astype(jnp.int32).reshape(1)
    smem = pl.BlockSpec(memory_space=pltpu.SMEM)
    vmem = pl.BlockSpec(memory_space=pltpu.VMEM)
    limit = pltpu.CompilerParams(vmem_limit_bytes=32 * 1024 * 1024)

    spread = pltpu.VMEM((orb_count // LANES, share_rows * ROWS, LANES), jnp.float32)
    own_rows = pl.pallas_call(
        functools.partial(pack_kernel, (slots, share_rows, orb_count, pad_rows)),
        out_shape=jax.ShapeDtypeStruct((pad_rows, orb_count), jnp.bfloat16),
        in_specs=[vmem],
        out_specs=vmem,
        scratch_shapes=[spread],
        compiler_params=limit,
        name="pack",
    )(green)
    move_dims = (slots, share_rows, orb_count, walkers, moves, keep)
    *leaving, place = pl.pallas_call(
        functools.partial(leave_kernel, move_dims),
        out_shape=[jax.ShapeDtypeStruct((share_rows, orb_count), jnp.bfloat16)] * (walkers - 1)
        + [jax.ShapeDtypeStruct((slots,), jnp.int32)],
        in_specs=[smem, smem, vmem],
        out_specs=[vmem] * (walkers - 1) + [smem],
        scratch_shapes=[pltpu.VMEM((pad_rows, orb_count), jnp.float32)],
        compiler_params=limit,
        name="leave",
    )(walker_index, table, own_rows)
    coming = [
        lax.ppermute(
            leaving[shift - 1], "walker", [(z, (z + shift) % walkers) for z in range(walkers)]
        )
        for shift in range(1, walkers)
    ]

    group = 4
    groups = vectors // group
    chip_rows = 2 * share_rows
    weights = pl.pallas_call(
        functools.partial(order_kernel, (group, groups, chip_rows)),
        out_shape=jax.ShapeDtypeStruct((vectors * occ_count, orb_count), jnp.bfloat16),
        in_specs=[smem] + [pl.BlockSpec(memory_space=pl.ANY)] * 2,
        out_specs=vmem,
        scratch_shapes=[pltpu.SemaphoreType.DMA((5 * vectors,))],
        compiler_params=pltpu.CompilerParams(vmem_limit_bytes=48 * 1024 * 1024),
        cost_estimate=pl.CostEstimate(
            flops=0, bytes_accessed=4 * chol.size, transcendentals=0
        ),
        name="order",
    )(block_index, chol, own_rows)

    core, near_x, near_y = 1, 2, 4
    from_x = swap(own_rows, near_x, blocks)
    from_y = swap(own_rows, near_y, blocks)
    from_core = swap(own_rows, core, blocks)
    width = orb_count // 2
    from_x, from_y, weights, coming[:2] = lax.optimization_barrier(
        (from_x, from_y, weights, coming[:2])
    )
    far = [swap(from_y[:, :width], near_x, blocks), swap(from_x[:, width:], near_y, blocks)]
    near_pieces = [own_rows, from_core]
    for piece in (from_x, from_y):
        near_pieces += [piece, swap(piece, core, blocks)]

    dims = (slots, share_rows, group, groups, chip_rows)
    work = 2 * vectors * occ_count * orb_count * pad_rows
    near_sums, late = pl.pallas_call(
        functools.partial(near_kernel, dims),
        out_shape=[
            jax.ShapeDtypeStruct((slots * ROWS, LANES), jnp.float32),
            jax.ShapeDtypeStruct((slots * chip_rows, vectors * occ_count), jnp.float32),
        ],
        in_specs=[smem] + [vmem] * 7,
        out_specs=[vmem] * 2,
        scratch_shapes=[pltpu.VMEM((slots * 3 * chip_rows, group * occ_count), jnp.float32)]
        * groups,
        compiler_params=limit,
        cost_estimate=pl.CostEstimate(
            flops=6 * work, bytes_accessed=2 * chol.size, transcendentals=0
        ),
        name="near",
    )(block_index, weights, *near_pieces)
    far, near_sums = lax.optimization_barrier((far, near_sums))
    far_pieces = far + [swap(piece, core, blocks) for piece in far]
    all_sums = pl.pallas_call(
        functools.partial(far_kernel, dims),
        out_shape=jax.ShapeDtypeStruct((blocks * walkers // 2, LANES), jnp.float32),
        in_specs=[smem] * 2 + [vmem] * 7,
        out_specs=vmem,
        scratch_shapes=[pltpu.VMEM((slots * chip_rows, group * occ_count), jnp.float32)] * groups,
        compiler_params=limit,
        cost_estimate=pl.CostEstimate(
            flops=2 * work, bytes_accessed=2 * chol.size, transcendentals=0
        ),
        name="far",
    )(block_index, place, weights, near_sums, late, *far_pieces)

    all_sums = all_sums + swap(all_sums, core, blocks)
    coming, _ = lax.optimization_barrier((coming, all_sums))
    new_green = pl.pallas_call(
        functools.partial(assemble_kernel, move_dims),
        out_shape=jax.ShapeDtypeStruct((keep, share_width), jnp.bfloat16),
        in_specs=[smem] * 2 + [vmem] * walkers,
        out_specs=vmem,
        scratch_shapes=[
            pltpu.VMEM((orb_count // LANES, share_rows * ROWS, LANES), jnp.float32),
            pltpu.VMEM(((slots + walkers - 1) * share_rows, orb_count), jnp.float32),
            pltpu.VMEM((orb_count // LANES, share_rows * ROWS, LANES), jnp.float32),
        ],
        compiler_params=limit,
        name="assemble",
    )(walker_index, table, green, *coming)

    energy_scale = 0.5 / (occ_count * math.sqrt(vectors * blocks))
    peers = [
        [block * walkers + walker for block in range(side, blocks, 2) for walker in range(walkers)]
        for side in range(2)
    ]
    got = lax.all_to_all(
        all_sums,
        ("block", "walker"),
        split_axis=0,
        concat_axis=0,
        axis_index_groups=peers,
        tiled=True,
    )
    got_sums = jnp.sum(got, axis=0)
    own_sums = lax.dynamic_slice(got_sums, (walker_index[0] * keep,), (keep,))
    return (new_green, -energy_scale * own_sums)


def fits(mesh):
    blocks = mesh.shape["block"]
    walkers = mesh.shape["walker"]

    def check(green, chol, counts, move_slot, move_dest):
        vectors, occ_count, orb_count = chol.shape
        share_width = green.shape[1] // blocks
        moves = move_slot.shape[1]
        slots = green.shape[0] // walkers
        return (
            blocks == 8
            and walkers >= 2
            and walkers & (walkers - 1) == 0
            and (moves + walkers - 2) // (walkers - 1) == 1
            and slots <= ROWS
            and share_width % (orb_count * ROWS) == 0
            and orb_count % (2 * LANES) == 0
            and occ_count == blocks * (share_width // orb_count)
            and occ_count == LANES + LANES // 2
            and (vectors // blocks) % 4 == 0
            and walkers * (slots - moves) <= LANES
        )

    return check


def solution(mesh):
    in_specs = (P("walker", "block"), P("block", None, None), P(), P(), P())
    out_specs = (P("walker", "block"), P("walker"))
    check = fits(mesh)

    def run(*args):
        chosen = body if check(*args) else general_body
        return jax.shard_map(
            chosen, mesh=mesh, in_specs=in_specs, out_specs=out_specs, check_vma=False
        )(*args)

    return run
```

```python
import functools
import math

import jax
import jax.numpy as jnp
from jax import lax
from jax.experimental import pallas as pl
from jax.experimental.pallas import tpu as pltpu
from jax.sharding import PartitionSpec as P


def arrival_ranks(move_slot, move_dest):
    active = move_slot >= 0
    move_total = move_slot.shape[1]
    earlier = jnp.arange(move_total)[None, :] < jnp.arange(move_total)[:, None]
    same_target = (
        (move_dest[:, :, None] == move_dest[:, None, :]) & earlier[None, :, :] & active[:, None, :]
    )
    return (active, jnp.sum(same_target.astype(jnp.int32), axis=2))


def general_body(green, chol, counts, move_slot, move_dest):
    walker_total = lax.axis_size("walker")
    own_index = lax.axis_index("walker")
    slot_total = green.shape[0]
    share_width = green.shape[1]
    keep_total = slot_total - move_slot.shape[1]
    capacity = (move_slot.shape[1] + walker_total - 2) // (walker_total - 1)
    occ_count = chol.shape[1]
    orb_count = chol.shape[2]
    energy_scale = 0.5 / (occ_count * math.sqrt(chol.shape[0] * lax.axis_size("block")))
    active, move_rank = arrival_ranks(move_slot, move_dest)
    own_slots = move_slot[own_index]
    own_dests = move_dest[own_index]
    own_active = active[own_index]
    own_rank = move_rank[own_index]
    peer_ids = jnp.arange(walker_total)
    place_ids = jnp.arange(capacity)
    chosen = (
        (own_dests[None, None, :] == peer_ids[:, None, None])
        & (own_rank[None, None, :] == place_ids[None, :, None])
        & own_active[None, None, :]
    )
    send_slot = jnp.sum(jnp.where(chosen, own_slots[None, None, :], 0), axis=2).reshape(-1)
    present = jnp.any(chosen, axis=2).reshape(-1)
    arrive = jnp.any(
        (move_dest[:, None, :] == own_index)
        & (move_rank[:, None, :] == place_ids[None, :, None])
        & active[:, None, :],
        axis=2,
    ).reshape(-1)
    slot_ids = jnp.arange(slot_total)
    occupied = slot_ids < counts[own_index]
    leaving = jnp.any(own_slots[:, None] == slot_ids[None, :], axis=0)
    staying = occupied & jnp.logical_not(leaving)
    stay_rank = jnp.cumsum(staying.astype(jnp.int32)) - 1
    arrive_rank = jnp.cumsum(arrive.astype(jnp.int32)) - 1
    stay_total = jnp.sum(staying.astype(jnp.int32))
    targets = jnp.arange(keep_total)
    from_stay = jnp.sum(
        jnp.where(
            staying[None, :] & (stay_rank[None, :] == targets[:, None]), slot_ids[None, :], 0
        ),
        axis=1,
    )
    arrive_ids = jnp.arange(arrive.shape[0]) + slot_total
    from_arrive = jnp.sum(
        jnp.where(
            arrive[None, :] & (arrive_rank[None, :] == (targets - stay_total)[:, None]),
            arrive_ids[None, :],
            0,
        ),
        axis=1,
    )
    source_row = jnp.where(targets < stay_total, from_stay, from_arrive)
    outgoing = jnp.where(
        present[:, None], jnp.take(green, send_slot, axis=0), jnp.zeros((), jnp.bfloat16)
    )
    outgoing = outgoing.reshape(walker_total, capacity, share_width)

    def walker_energy(walker_row):
        green_mat = walker_row.reshape(occ_count, orb_count)
        transfer = jnp.einsum("gip,jp->gij", chol, green_mat, preferred_element_type=jnp.float32)
        return jnp.sum(transfer * jnp.swapaxes(transfer, 1, 2))

    got_rows = lax.all_to_all(outgoing, "walker", split_axis=0, concat_axis=0, tiled=True)
    source_pool = jnp.concatenate([green, got_rows.reshape(-1, share_width)], axis=0)
    new_green = jnp.take(source_pool, source_row, axis=0)
    complete = lax.all_gather(new_green, "block", axis=1, tiled=True)
    partial_value = lax.map(walker_energy, complete)
    energy = -energy_scale * lax.psum(partial_value, "block")
    return (new_green, energy)


LANES = 128
ROWS = 8


def spread_slots(green_ref, spread, share_rows):
    slots = green_ref.shape[0]
    tiles = spread.shape[0]
    for row in range(share_rows):
        for tile in range(tiles):
            col = (row * tiles + tile) * LANES
            block = green_ref[:, col : col + LANES].astype(jnp.float32)
            spread[tile, row * ROWS : row * ROWS + slots, :] = block


def pack_kernel(dims, green_ref, own_ref, spread):
    slots, share_rows, orb_count, pad_rows = dims
    spread_slots(green_ref, spread, share_rows)
    for tile in range(orb_count // LANES):
        dense = [spread[tile, pl.ds(slot, share_rows, stride=ROWS), :] for slot in range(slots)]
        if pad_rows > slots * share_rows:
            dense.append(jnp.zeros((pad_rows - slots * share_rows, LANES), jnp.float32))
        packed = jnp.concatenate(dense, axis=0).astype(jnp.bfloat16)
        own_ref[:, tile * LANES : (tile + 1) * LANES] = packed


class Moves:
    def __init__(self, table_ref, moves):
        self.table, self.moves = table_ref, moves

    def count(self, device):
        return self.table[0, device]

    def slot(self, device, move):
        return self.table[1 + move, device]

    def dest(self, device, move):
        return self.table[1 + self.moves + move, device]

    def staying(self, device):
        total = self.count(device)
        for move in range(self.moves):
            total = total - jnp.where(self.slot(device, move) >= 0, 1, 0)
        return total

    def goes_to(self, own, slot):
        target = jnp.int32(-1)
        for move in range(self.moves):
            target = jnp.where(self.slot(own, move) == slot, self.dest(own, move), target)
        return target


def leave_kernel(dims, ident_ref, table_ref, own_ref, *refs):
    slots, share_rows, orb_count, walkers, moves, keep = dims
    leave_refs, place_ref, wide = refs[:-2], refs[-2], refs[-1]
    table = Moves(table_ref, moves)
    wide[...] = own_ref[...].astype(jnp.float32)
    own = ident_ref[0]
    for shift in range(1, walkers):
        target = lax.rem(own + shift, walkers)
        chosen = jnp.int32(0)
        for move in range(moves):
            hit = (table.dest(own, move) == target) & (table.slot(own, move) >= 0)
            chosen = jnp.where(hit, table.slot(own, move), chosen)
        start = pl.multiple_of(chosen * share_rows, ROWS)
        leave_refs[shift - 1][...] = wide[pl.ds(start, share_rows), :].astype(jnp.bfloat16)
    rank = jnp.int32(0)
    for slot in range(slots):
        live = slot < table.count(own)
        gone_to = table.goes_to(own, slot)
        stays = live & (gone_to < 0)
        there = jnp.maximum(gone_to, 0)
        ahead = table.staying(there)
        for device in range(walkers):
            for move in range(moves):
                hit = (
                    (device < own)
                    & (table.dest(device, move) == there)
                    & (table.slot(device, move) >= 0)
                )
                ahead = ahead + jnp.where(hit, 1, 0)
        place = jnp.where(stays, own * keep + rank, there * keep + ahead)
        place_ref[slot] = jnp.where(live, place, -1)
        rank = rank + jnp.where(stays, 1, 0)


def assemble_kernel(dims, ident_ref, table_ref, green_ref, *refs):
    slots, share_rows, orb_count, walkers, moves, keep = dims
    table = Moves(table_ref, moves)
    come_refs = refs[: walkers - 1]
    new_ref, spread, pool, out = refs[walkers - 1 :]
    own = ident_ref[0]
    tiles = orb_count // LANES
    spread_slots(green_ref, spread, share_rows)
    for slot in range(slots):
        for tile in range(tiles):
            pool[
                slot * share_rows : (slot + 1) * share_rows, tile * LANES : (tile + 1) * LANES
            ] = spread[tile, pl.ds(slot, share_rows, stride=ROWS), :]
    for shift in range(1, walkers):
        start = (slots + shift - 1) * share_rows
        pool[start : start + share_rows, :] = come_refs[shift - 1][...].astype(jnp.float32)

    sources = [jnp.int32(0)] * keep
    rank = jnp.int32(0)
    for slot in range(slots):
        stays = (slot < table.count(own)) & (table.goes_to(own, slot) < 0)
        for target in range(keep):
            sources[target] = jnp.where(stays & (rank == target), slot, sources[target])
        rank = rank + jnp.where(stays, 1, 0)
    for device in range(walkers):
        comes = jnp.bool_(False)
        for move in range(moves):
            comes = comes | ((table.dest(device, move) == own) & (table.slot(device, move) >= 0))
        comes = comes & (device != own)
        shift = lax.rem(own - device + walkers, walkers)
        for target in range(keep):
            sources[target] = jnp.where(
                comes & (rank == target), slots + shift - 1, sources[target]
            )
        rank = rank + jnp.where(comes, 1, 0)
    for target in range(keep):
        start = pl.multiple_of(sources[target] * share_rows, ROWS)
        for tile in range(tiles):
            out[tile, pl.ds(target, share_rows, stride=ROWS), :] = pool[
                pl.ds(start, share_rows), tile * LANES : (tile + 1) * LANES
            ]
    for row in range(share_rows):
        for tile in range(tiles):
            col = (row * tiles + tile) * LANES
            new_ref[:, col : col + LANES] = out[
                tile, row * ROWS : row * ROWS + keep, :
            ].astype(jnp.bfloat16)


def order_kernel(dims, ident_ref, chol_ref, own_ref, out_ref, sems):
    del own_ref
    group, groups, chip_rows = dims
    chip = ident_ref[0] // 2
    edge = LANES - 2 * chip_rows
    rest = 2 * chip_rows - edge
    copies = []

    def add(vec, distance, start, size, place):
        row = pl.multiple_of(jnp.bitwise_xor(chip, distance) * chip_rows + start, 16)
        copies.append(
            pltpu.make_async_copy(
                chol_ref.at[vec, pl.ds(row, size), :],
                out_ref.at[pl.ds(place, size), :],
                sems.at[len(copies)],
            )
        )

    for index in range(groups):
        for item in range(group):
            vec = index * group + item
            place = index * group * 4 * chip_rows + item * LANES
            add(vec, 0, 0, chip_rows, place)
            add(vec, 1, 0, chip_rows, place + chip_rows)
            add(vec, 2, 0, edge, place + 2 * chip_rows)
            place = index * group * 4 * chip_rows + group * LANES + item * rest
            add(vec, 2, edge, chip_rows - edge, place)
            add(vec, 3, 0, chip_rows, place + chip_rows - edge)
    for copy in copies:
        copy.start()
    for copy in copies:
        copy.wait()


def times(left, right):
    return lax.dot_general(
        left, right, (((1,), (1,)), ((), ())), preferred_element_type=jnp.float32
    )


def near_kernel(dims, ident_ref, weight_ref, *refs):
    slots, share_rows, group, groups, chip_rows = dims
    piece_refs = refs[:6]
    sum_ref, late_ref = refs[6:8]
    trans_refs = refs[8:]
    own = ident_ref[0]
    core = lax.rem(own, 2)
    pad_rows = piece_refs[0].shape[0]
    near = 3 * chip_rows
    size = 4 * chip_rows * group
    edge = near - LANES
    half = LANES // 2
    left = jnp.concatenate([ref[...] for ref in piece_refs], axis=0)
    lane = lax.broadcasted_iota(jnp.int32, (1, LANES), 1)
    low_half = lane < half
    in_edge = jnp.where(low_half, lane, lane - half) < edge
    sums = [jnp.zeros((ROWS, LANES), jnp.float32) for _ in range(slots)]

    def fold(value):
        return jnp.sum(value.reshape(-1, ROWS, LANES), axis=0)

    for index in range(groups):
        trans = trans_refs[index]
        result = times(left, weight_ref[index * size : (index + 1) * size, :])
        for piece in range(6):
            source = jnp.bitwise_xor(core, piece % 2)
            for slot in range(slots):
                start = piece * pad_rows + slot * share_rows
                place = slot * near + (piece // 2) * chip_rows + source * share_rows
                trans[pl.ds(pl.multiple_of(place, ROWS), share_rows), :] = result[
                    start : start + share_rows, :
                ]
        for slot in range(slots):
            base = slot * near
            late = slice(slot * chip_rows, (slot + 1) * chip_rows)
            acc = sums[slot]
            for pair in range(group // 2):
                col = (group + pair) * LANES
                top = trans[base : base + LANES, col : col + LANES].T
                edge_rows = trans[base + LANES : base + near, col : col + LANES]
                gap = jnp.zeros((half - edge, LANES), jnp.float32)
                bottom = jnp.concatenate([edge_rows, gap, edge_rows, gap], axis=0).T
                for side in range(2):
                    vec = 2 * pair + side
                    high = trans[base : base + LANES, vec * LANES : (vec + 1) * LANES]
                    acc = acc + fold(high * high.T)
                    across = trans[base + LANES : base + near, vec * LANES : (vec + 1) * LANES]
                    acc = acc + 2.0 * fold(across * top[side * half : side * half + edge, :])
                    late_ref[
                        late, (index * (group + group // 2) + vec) * LANES : (
                            index * (group + group // 2) + vec + 1
                        ) * LANES
                    ] = top[side * half + edge : (side + 1) * half, :]
                corner = jnp.where(low_half, bottom[:edge, :], bottom[half : half + edge, :])
                acc = acc + fold(jnp.where(in_edge, edge_rows * corner, 0.0))
                rest = jnp.where(low_half, bottom[edge:half, :], bottom[half + edge :, :])
                place = (index * (group + group // 2) + group + pair) * LANES
                late_ref[late, place : place + LANES] = jnp.where(in_edge, rest, 0.0)
            sums[slot] = acc
    sum_ref[...] = jnp.concatenate(sums, axis=0)


def far_kernel(dims, ident_ref, place_ref, weight_ref, near_sum_ref, late_ref, *refs):
    slots, share_rows, group, groups, chip_rows = dims
    piece_refs = refs[:4]
    sum_ref = refs[4]
    trans_refs = refs[5:]
    own = ident_ref[0]
    core = lax.rem(own, 2)
    pad_rows, width = piece_refs[0].shape
    half = LANES // 2
    edge = half - chip_rows
    size = 4 * chip_rows * group
    lane = lax.broadcasted_iota(jnp.int32, (1, LANES), 1)
    low_half = lane < half
    in_rest = jnp.where(low_half, lane, lane - half) >= edge
    lefts = [
        jnp.concatenate([piece_refs[part][...], piece_refs[2 + part][...]], axis=0)
        for part in range(2)
    ]
    twice = [jnp.zeros((ROWS, LANES), jnp.float32) for _ in range(slots)]
    once = [near_sum_ref[slot * ROWS : (slot + 1) * ROWS, :] for slot in range(slots)]

    def fold(value):
        return jnp.sum(value.reshape(-1, ROWS, LANES), axis=0)

    tiles = group + group // 2
    for index in range(groups):
        trans = trans_refs[index]
        rows = slice(index * size, (index + 1) * size)
        result = times(lefts[0], weight_ref[rows, :width])
        result = result + times(lefts[1], weight_ref[rows, width:])
        for piece in range(2):
            source = jnp.bitwise_xor(core, piece)
            for slot in range(slots):
                start = piece * pad_rows + slot * share_rows
                place = slot * chip_rows + source * share_rows
                trans[pl.ds(pl.multiple_of(place, ROWS), share_rows), :] = result[
                    start : start + share_rows, :
                ]
        for slot in range(slots):
            rows = slice(slot * chip_rows, (slot + 1) * chip_rows)
            for tile in range(tiles):
                here = trans[rows, tile * LANES : (tile + 1) * LANES]
                met = late_ref[rows, (index * tiles + tile) * LANES : (index * tiles + tile + 1) * LANES]
                twice[slot] = twice[slot] + fold(here * met)
                if tile >= group:
                    gap = jnp.zeros((edge, LANES), jnp.float32)
                    turned = jnp.concatenate([gap, here, gap, here], axis=0).T
                    corner = jnp.where(low_half, turned[edge:half, :], turned[half + edge :, :])
                    once[slot] = once[slot] + fold(jnp.where(in_rest, here * corner, 0.0))
    value = jnp.zeros((1, LANES), jnp.float32)
    for slot in range(slots):
        slot_sum = jnp.sum(once[slot] + 2.0 * twice[slot])
        value = jnp.where(lane == place_ref[slot], slot_sum, value)
    sum_ref[...] = value


def swap(value, mask, blocks):
    return lax.ppermute(value, "block", [(index, index ^ mask) for index in range(blocks)])


def turn(value, shift, walkers):
    pairs = [(index, (index + shift) % walkers) for index in range(walkers)]
    return lax.ppermute(value, "walker", pairs)


def body(green, chol, counts, move_slot, move_dest):
    walkers = lax.axis_size("walker")
    blocks = lax.axis_size("block")
    slots, share_width = green.shape
    vectors, occ_count, orb_count = chol.shape
    moves = move_slot.shape[1]
    keep = slots - moves
    share_rows = share_width // orb_count
    pad_rows = -(-slots * share_rows // 16) * 16
    table = jnp.concatenate([counts[None, :], move_slot.T, move_dest.T], axis=0)
    walker_index = lax.axis_index("walker").astype(jnp.int32).reshape(1)
    block_index = lax.axis_index("block").astype(jnp.int32).reshape(1)
    smem = pl.BlockSpec(memory_space=pltpu.SMEM)
    vmem = pl.BlockSpec(memory_space=pltpu.VMEM)
    limit = pltpu.CompilerParams(vmem_limit_bytes=32 * 1024 * 1024)

    spread = pltpu.VMEM((orb_count // LANES, share_rows * ROWS, LANES), jnp.float32)
    own_rows = pl.pallas_call(
        functools.partial(pack_kernel, (slots, share_rows, orb_count, pad_rows)),
        out_shape=jax.ShapeDtypeStruct((pad_rows, orb_count), jnp.bfloat16),
        in_specs=[vmem],
        out_specs=vmem,
        scratch_shapes=[spread],
        compiler_params=limit,
        name="pack",
    )(green)
    move_dims = (slots, share_rows, orb_count, walkers, moves, keep)
    *leaving, place = pl.pallas_call(
        functools.partial(leave_kernel, move_dims),
        out_shape=[jax.ShapeDtypeStruct((share_rows, orb_count), jnp.bfloat16)] * (walkers - 1)
        + [jax.ShapeDtypeStruct((slots,), jnp.int32)],
        in_specs=[smem, smem, vmem],
        out_specs=[vmem] * (walkers - 1) + [smem],
        scratch_shapes=[pltpu.VMEM((pad_rows, orb_count), jnp.float32)],
        compiler_params=limit,
        name="leave",
    )(walker_index, table, own_rows)
    coming = [turn(leaving[shift - 1], shift, walkers) for shift in range(1, walkers)]

    group = 4
    groups = vectors // group
    chip_rows = 2 * share_rows
    weights = pl.pallas_call(
        functools.partial(order_kernel, (group, groups, chip_rows)),
        out_shape=jax.ShapeDtypeStruct((vectors * occ_count, orb_count), jnp.bfloat16),
        in_specs=[smem] + [pl.BlockSpec(memory_space=pl.ANY)] * 2,
        out_specs=vmem,
        scratch_shapes=[pltpu.SemaphoreType.DMA((5 * vectors,))],
        compiler_params=pltpu.CompilerParams(vmem_limit_bytes=48 * 1024 * 1024),
        cost_estimate=pl.CostEstimate(
            flops=0, bytes_accessed=4 * chol.size, transcendentals=0
        ),
        name="order",
    )(block_index, chol, own_rows)

    core, near_x, near_y = 1, 2, 4
    from_x = swap(own_rows, near_x, blocks)
    from_y = swap(own_rows, near_y, blocks)
    from_core = swap(own_rows, core, blocks)
    width = orb_count // 2
    from_x, from_y, weights, coming[:2] = lax.optimization_barrier(
        (from_x, from_y, weights, coming[:2])
    )
    far = [swap(from_y[:, :width], near_x, blocks), swap(from_x[:, width:], near_y, blocks)]
    near_pieces = [own_rows, from_core]
    for piece in (from_x, from_y):
        near_pieces += [piece, swap(piece, core, blocks)]

    dims = (slots, share_rows, group, groups, chip_rows)
    work = 2 * vectors * occ_count * orb_count * pad_rows
    near_sums, late = pl.pallas_call(
        functools.partial(near_kernel, dims),
        out_shape=[
            jax.ShapeDtypeStruct((slots * ROWS, LANES), jnp.float32),
            jax.ShapeDtypeStruct((slots * chip_rows, vectors * occ_count), jnp.float32),
        ],
        in_specs=[smem] + [vmem] * 7,
        out_specs=[vmem] * 2,
        scratch_shapes=[pltpu.VMEM((slots * 3 * chip_rows, group * occ_count), jnp.float32)]
        * groups,
        compiler_params=limit,
        cost_estimate=pl.CostEstimate(
            flops=6 * work, bytes_accessed=2 * chol.size, transcendentals=0
        ),
        name="near",
    )(block_index, weights, *near_pieces)
    far, near_sums = lax.optimization_barrier((far, near_sums))
    far_pieces = far + [swap(piece, core, blocks) for piece in far]
    all_sums = pl.pallas_call(
        functools.partial(far_kernel, dims),
        out_shape=jax.ShapeDtypeStruct((1, LANES), jnp.float32),
        in_specs=[smem] * 2 + [vmem] * 7,
        out_specs=vmem,
        scratch_shapes=[pltpu.VMEM((slots * chip_rows, group * occ_count), jnp.float32)] * groups,
        compiler_params=limit,
        cost_estimate=pl.CostEstimate(
            flops=2 * work, bytes_accessed=2 * chol.size, transcendentals=0
        ),
        name="far",
    )(block_index, place, weights, near_sums, late, *far_pieces)

    coming, _ = lax.optimization_barrier((coming, all_sums))
    energy_scale = 0.5 / (occ_count * math.sqrt(vectors * blocks))
    all_sums = all_sums + swap(all_sums, core, blocks)
    all_sums, coming[2:] = lax.optimization_barrier((all_sums, coming[2:]))
    others = [swap(all_sums, mask, blocks) for mask in (near_x, near_y, near_x | near_y)]
    all_sums = (all_sums + others[0]) + (others[1] + others[2])
    others = [turn(all_sums, shift, walkers) for shift in range(1, walkers)]
    all_sums = functools.reduce(jnp.add, others, all_sums)
    own_sums = lax.dynamic_slice(all_sums[0], (walker_index[0] * keep,), (keep,))
    new_green = pl.pallas_call(
        functools.partial(assemble_kernel, move_dims),
        out_shape=jax.ShapeDtypeStruct((keep, share_width), jnp.bfloat16),
        in_specs=[smem] * 2 + [vmem] * walkers,
        out_specs=vmem,
        scratch_shapes=[
            pltpu.VMEM((orb_count // LANES, share_rows * ROWS, LANES), jnp.float32),
            pltpu.VMEM(((slots + walkers - 1) * share_rows, orb_count), jnp.float32),
            pltpu.VMEM((orb_count // LANES, share_rows * ROWS, LANES), jnp.float32),
        ],
        compiler_params=limit,
        name="assemble",
    )(walker_index, table, green, *coming)

    return (new_green, -energy_scale * own_sums)


def fits(mesh):
    blocks = mesh.shape["block"]
    walkers = mesh.shape["walker"]

    def check(green, chol, counts, move_slot, move_dest):
        vectors, occ_count, orb_count = chol.shape
        share_width = green.shape[1] // blocks
        moves = move_slot.shape[1]
        slots = green.shape[0] // walkers
        return (
            blocks == 8
            and walkers >= 2
            and walkers & (walkers - 1) == 0
            and (moves + walkers - 2) // (walkers - 1) == 1
            and slots <= ROWS
            and share_width % (orb_count * ROWS) == 0
            and orb_count % (2 * LANES) == 0
            and occ_count == blocks * (share_width // orb_count)
            and occ_count == LANES + LANES // 2
            and (vectors // blocks) % 4 == 0
            and walkers * (slots - moves) <= LANES
        )

    return check


def solution(mesh):
    in_specs = (P("walker", "block"), P("block", None, None), P(), P(), P())
    out_specs = (P("walker", "block"), P("walker"))
    check = fits(mesh)

    def run(*args):
        chosen = body if check(*args) else general_body
        return jax.shard_map(
            chosen, mesh=mesh, in_specs=in_specs, out_specs=out_specs, check_vma=False
        )(*args)

    return run
```

```python
import functools
import math

import jax
import jax.numpy as jnp
from jax import lax
from jax.experimental import pallas as pl
from jax.experimental.pallas import tpu as pltpu
from jax.sharding import PartitionSpec as P


def arrival_ranks(move_slot, move_dest):
    active = move_slot >= 0
    move_total = move_slot.shape[1]
    earlier = jnp.arange(move_total)[None, :] < jnp.arange(move_total)[:, None]
    same_target = (
        (move_dest[:, :, None] == move_dest[:, None, :]) & earlier[None, :, :] & active[:, None, :]
    )
    return (active, jnp.sum(same_target.astype(jnp.int32), axis=2))


def general_body(green, chol, counts, move_slot, move_dest):
    walker_total = lax.axis_size("walker")
    own_index = lax.axis_index("walker")
    slot_total = green.shape[0]
    share_width = green.shape[1]
    keep_total = slot_total - move_slot.shape[1]
    capacity = (move_slot.shape[1] + walker_total - 2) // (walker_total - 1)
    occ_count = chol.shape[1]
    orb_count = chol.shape[2]
    energy_scale = 0.5 / (occ_count * math.sqrt(chol.shape[0] * lax.axis_size("block")))
    active, move_rank = arrival_ranks(move_slot, move_dest)
    own_slots = move_slot[own_index]
    own_dests = move_dest[own_index]
    own_active = active[own_index]
    own_rank = move_rank[own_index]
    peer_ids = jnp.arange(walker_total)
    place_ids = jnp.arange(capacity)
    chosen = (
        (own_dests[None, None, :] == peer_ids[:, None, None])
        & (own_rank[None, None, :] == place_ids[None, :, None])
        & own_active[None, None, :]
    )
    send_slot = jnp.sum(jnp.where(chosen, own_slots[None, None, :], 0), axis=2).reshape(-1)
    present = jnp.any(chosen, axis=2).reshape(-1)
    arrive = jnp.any(
        (move_dest[:, None, :] == own_index)
        & (move_rank[:, None, :] == place_ids[None, :, None])
        & active[:, None, :],
        axis=2,
    ).reshape(-1)
    slot_ids = jnp.arange(slot_total)
    occupied = slot_ids < counts[own_index]
    leaving = jnp.any(own_slots[:, None] == slot_ids[None, :], axis=0)
    staying = occupied & jnp.logical_not(leaving)
    stay_rank = jnp.cumsum(staying.astype(jnp.int32)) - 1
    arrive_rank = jnp.cumsum(arrive.astype(jnp.int32)) - 1
    stay_total = jnp.sum(staying.astype(jnp.int32))
    targets = jnp.arange(keep_total)
    from_stay = jnp.sum(
        jnp.where(
            staying[None, :] & (stay_rank[None, :] == targets[:, None]), slot_ids[None, :], 0
        ),
        axis=1,
    )
    arrive_ids = jnp.arange(arrive.shape[0]) + slot_total
    from_arrive = jnp.sum(
        jnp.where(
            arrive[None, :] & (arrive_rank[None, :] == (targets - stay_total)[:, None]),
            arrive_ids[None, :],
            0,
        ),
        axis=1,
    )
    source_row = jnp.where(targets < stay_total, from_stay, from_arrive)
    outgoing = jnp.where(
        present[:, None], jnp.take(green, send_slot, axis=0), jnp.zeros((), jnp.bfloat16)
    )
    outgoing = outgoing.reshape(walker_total, capacity, share_width)

    def walker_energy(walker_row):
        green_mat = walker_row.reshape(occ_count, orb_count)
        transfer = jnp.einsum("gip,jp->gij", chol, green_mat, preferred_element_type=jnp.float32)
        return jnp.sum(transfer * jnp.swapaxes(transfer, 1, 2))

    got_rows = lax.all_to_all(outgoing, "walker", split_axis=0, concat_axis=0, tiled=True)
    source_pool = jnp.concatenate([green, got_rows.reshape(-1, share_width)], axis=0)
    new_green = jnp.take(source_pool, source_row, axis=0)
    complete = lax.all_gather(new_green, "block", axis=1, tiled=True)
    partial_value = lax.map(walker_energy, complete)
    energy = -energy_scale * lax.psum(partial_value, "block")
    return (new_green, energy)


LANES = 128
ROWS = 8


def spread_slots(green_ref, spread, share_rows):
    slots = green_ref.shape[0]
    tiles = spread.shape[0]
    for row in range(share_rows):
        for tile in range(tiles):
            col = (row * tiles + tile) * LANES
            block = green_ref[:, col : col + LANES].astype(jnp.float32)
            spread[tile, row * ROWS : row * ROWS + slots, :] = block


def pack_kernel(dims, green_ref, own_ref, spread):
    slots, share_rows, orb_count = dims
    spread_slots(green_ref, spread, share_rows)
    for tile in range(orb_count // LANES):
        dense = [spread[tile, pl.ds(slot, share_rows, stride=ROWS), :] for slot in range(slots)]
        packed = jnp.concatenate(dense, axis=0).astype(jnp.bfloat16)
        own_ref[:, tile * LANES : (tile + 1) * LANES] = packed


class Moves:
    def __init__(self, table_ref, moves):
        self.table, self.moves = table_ref, moves

    def count(self, device):
        return self.table[0, device]

    def slot(self, device, move):
        return self.table[1 + move, device]

    def dest(self, device, move):
        return self.table[1 + self.moves + move, device]

    def staying(self, device):
        total = self.count(device)
        for move in range(self.moves):
            total = total - jnp.where(self.slot(device, move) >= 0, 1, 0)
        return total

    def goes_to(self, own, slot):
        target = jnp.int32(-1)
        for move in range(self.moves):
            target = jnp.where(self.slot(own, move) == slot, self.dest(own, move), target)
        return target


def leave_kernel(dims, ident_ref, table_ref, own_ref, *refs):
    slots, share_rows, orb_count, walkers, moves, keep = dims
    leave_refs, place_ref, wide = refs[:-2], refs[-2], refs[-1]
    table = Moves(table_ref, moves)
    wide[...] = own_ref[...].astype(jnp.float32)
    own = ident_ref[0]
    for shift in range(1, walkers):
        target = lax.rem(own + shift, walkers)
        chosen = jnp.int32(0)
        for move in range(moves):
            hit = (table.dest(own, move) == target) & (table.slot(own, move) >= 0)
            chosen = jnp.where(hit, table.slot(own, move), chosen)
        start = pl.multiple_of(chosen * share_rows, ROWS)
        leave_refs[shift - 1][...] = wide[pl.ds(start, share_rows), :].astype(jnp.bfloat16)
    rank = jnp.int32(0)
    for slot in range(slots):
        live = slot < table.count(own)
        gone_to = table.goes_to(own, slot)
        stays = live & (gone_to < 0)
        there = jnp.maximum(gone_to, 0)
        ahead = table.staying(there)
        for device in range(walkers):
            for move in range(moves):
                hit = (
                    (device < own)
                    & (table.dest(device, move) == there)
                    & (table.slot(device, move) >= 0)
                )
                ahead = ahead + jnp.where(hit, 1, 0)
        place = jnp.where(stays, own * keep + rank, there * keep + ahead)
        place_ref[slot] = jnp.where(live, place, -1)
        rank = rank + jnp.where(stays, 1, 0)


def assemble_kernel(dims, ident_ref, table_ref, green_ref, *refs):
    slots, share_rows, orb_count, walkers, moves, keep = dims
    table = Moves(table_ref, moves)
    come_refs = refs[: walkers - 1]
    new_ref, spread, pool, out = refs[walkers - 1 :]
    own = ident_ref[0]
    tiles = orb_count // LANES
    spread_slots(green_ref, spread, share_rows)
    for slot in range(slots):
        for tile in range(tiles):
            pool[
                slot * share_rows : (slot + 1) * share_rows, tile * LANES : (tile + 1) * LANES
            ] = spread[tile, pl.ds(slot, share_rows, stride=ROWS), :]
    for shift in range(1, walkers):
        start = (slots + shift - 1) * share_rows
        pool[start : start + share_rows, :] = come_refs[shift - 1][...].astype(jnp.float32)

    sources = [jnp.int32(0)] * keep
    rank = jnp.int32(0)
    for slot in range(slots):
        stays = (slot < table.count(own)) & (table.goes_to(own, slot) < 0)
        for target in range(keep):
            sources[target] = jnp.where(stays & (rank == target), slot, sources[target])
        rank = rank + jnp.where(stays, 1, 0)
    for device in range(walkers):
        comes = jnp.bool_(False)
        for move in range(moves):
            comes = comes | ((table.dest(device, move) == own) & (table.slot(device, move) >= 0))
        comes = comes & (device != own)
        shift = lax.rem(own - device + walkers, walkers)
        for target in range(keep):
            sources[target] = jnp.where(
                comes & (rank == target), slots + shift - 1, sources[target]
            )
        rank = rank + jnp.where(comes, 1, 0)
    for target in range(keep):
        start = pl.multiple_of(sources[target] * share_rows, ROWS)
        for tile in range(tiles):
            out[tile, pl.ds(target, share_rows, stride=ROWS), :] = pool[
                pl.ds(start, share_rows), tile * LANES : (tile + 1) * LANES
            ]
    for row in range(share_rows):
        for tile in range(tiles):
            col = (row * tiles + tile) * LANES
            new_ref[:, col : col + LANES] = out[
                tile, row * ROWS : row * ROWS + keep, :
            ].astype(jnp.bfloat16)


def order_kernel(dims, ident_ref, chol_ref, own_ref, out_ref, sems):
    del own_ref
    group, groups, chip_rows = dims
    chip = ident_ref[0] // 2
    edge = LANES - 2 * chip_rows
    rest = 2 * chip_rows - edge
    copies = []

    def add(vec, distance, start, size, place):
        row = pl.multiple_of(jnp.bitwise_xor(chip, distance) * chip_rows + start, 16)
        copies.append(
            pltpu.make_async_copy(
                chol_ref.at[vec, pl.ds(row, size), :],
                out_ref.at[pl.ds(place, size), :],
                sems.at[len(copies)],
            )
        )

    for index in range(groups):
        for item in range(group):
            vec = index * group + item
            place = index * group * 4 * chip_rows + item * LANES
            add(vec, 0, 0, chip_rows, place)
            add(vec, 1, 0, chip_rows, place + chip_rows)
            add(vec, 2, 0, edge, place + 2 * chip_rows)
            place = index * group * 4 * chip_rows + group * LANES + item * rest
            add(vec, 2, edge, chip_rows - edge, place)
            add(vec, 3, 0, chip_rows, place + chip_rows - edge)
    for copy in copies:
        copy.start()
    for copy in copies:
        copy.wait()


def padded(rows):
    return -(-rows // 16) * 16


def stacked(refs):
    values = []
    for ref in refs:
        rows, width = ref.shape
        values.append(ref[...])
        if padded(rows) > rows:
            values.append(jnp.zeros((padded(rows) - rows, width), jnp.bfloat16))
    return jnp.concatenate(values, axis=0)


def times(left, right):
    return lax.dot_general(
        left, right, (((1,), (1,)), ((), ())), preferred_element_type=jnp.float32
    )


def near_kernel(dims, ident_ref, weight_ref, *refs):
    slots, share_rows, group, groups, chip_rows = dims
    piece_refs = refs[:6]
    sum_ref, late_ref = refs[6:8]
    trans_refs = refs[8:]
    own = ident_ref[0]
    core = lax.rem(own, 2)
    pad_rows = padded(piece_refs[0].shape[0])
    near = 3 * chip_rows
    size = 4 * chip_rows * group
    edge = near - LANES
    half = LANES // 2
    left = stacked(piece_refs)
    lane = lax.broadcasted_iota(jnp.int32, (1, LANES), 1)
    low_half = lane < half
    in_edge = jnp.where(low_half, lane, lane - half) < edge
    sums = [jnp.zeros((ROWS, LANES), jnp.float32) for _ in range(slots)]

    def fold(value):
        return jnp.sum(value.reshape(-1, ROWS, LANES), axis=0)

    for index in range(groups):
        trans = trans_refs[index]
        result = times(left, weight_ref[index * size : (index + 1) * size, :])
        for piece in range(6):
            source = jnp.bitwise_xor(core, piece % 2)
            for slot in range(slots):
                start = piece * pad_rows + slot * share_rows
                place = slot * near + (piece // 2) * chip_rows + source * share_rows
                trans[pl.ds(pl.multiple_of(place, ROWS), share_rows), :] = result[
                    start : start + share_rows, :
                ]
        for slot in range(slots):
            base = slot * near
            late = slice(slot * chip_rows, (slot + 1) * chip_rows)
            acc = sums[slot]
            for pair in range(group // 2):
                col = (group + pair) * LANES
                top = trans[base : base + LANES, col : col + LANES].T
                edge_rows = trans[base + LANES : base + near, col : col + LANES]
                gap = jnp.zeros((half - edge, LANES), jnp.float32)
                bottom = jnp.concatenate([edge_rows, gap, edge_rows, gap], axis=0).T
                for side in range(2):
                    vec = 2 * pair + side
                    high = trans[base : base + LANES, vec * LANES : (vec + 1) * LANES]
                    acc = acc + fold(high * high.T)
                    across = trans[base + LANES : base + near, vec * LANES : (vec + 1) * LANES]
                    acc = acc + 2.0 * fold(across * top[side * half : side * half + edge, :])
                    late_ref[
                        late, (index * (group + group // 2) + vec) * LANES : (
                            index * (group + group // 2) + vec + 1
                        ) * LANES
                    ] = top[side * half + edge : (side + 1) * half, :]
                corner = jnp.where(low_half, bottom[:edge, :], bottom[half : half + edge, :])
                acc = acc + fold(jnp.where(in_edge, edge_rows * corner, 0.0))
                rest = jnp.where(low_half, bottom[edge:half, :], bottom[half + edge :, :])
                place = (index * (group + group // 2) + group + pair) * LANES
                late_ref[late, place : place + LANES] = jnp.where(in_edge, rest, 0.0)
            sums[slot] = acc
    sum_ref[...] = jnp.concatenate(sums, axis=0)


def far_kernel(dims, ident_ref, place_ref, weight_ref, near_sum_ref, late_ref, *refs):
    slots, share_rows, group, groups, chip_rows = dims
    piece_refs = refs[:4]
    sum_ref = refs[4]
    trans_refs = refs[5:]
    own = ident_ref[0]
    core = lax.rem(own, 2)
    pack_rows, width = piece_refs[0].shape
    pad_rows = padded(pack_rows)
    half = LANES // 2
    edge = half - chip_rows
    size = 4 * chip_rows * group
    lane = lax.broadcasted_iota(jnp.int32, (1, LANES), 1)
    low_half = lane < half
    in_rest = jnp.where(low_half, lane, lane - half) >= edge
    lefts = [stacked(piece_refs[part::2]) for part in range(2)]
    twice = [jnp.zeros((ROWS, LANES), jnp.float32) for _ in range(slots)]
    once = [near_sum_ref[slot * ROWS : (slot + 1) * ROWS, :] for slot in range(slots)]

    def fold(value):
        return jnp.sum(value.reshape(-1, ROWS, LANES), axis=0)

    tiles = group + group // 2
    for index in range(groups):
        trans = trans_refs[index]
        rows = slice(index * size, (index + 1) * size)
        result = times(lefts[0], weight_ref[rows, :width])
        result = result + times(lefts[1], weight_ref[rows, width:])
        for piece in range(2):
            source = jnp.bitwise_xor(core, piece)
            for slot in range(slots):
                start = piece * pad_rows + slot * share_rows
                place = slot * chip_rows + source * share_rows
                trans[pl.ds(pl.multiple_of(place, ROWS), share_rows), :] = result[
                    start : start + share_rows, :
                ]
        for slot in range(slots):
            rows = slice(slot * chip_rows, (slot + 1) * chip_rows)
            for tile in range(tiles):
                here = trans[rows, tile * LANES : (tile + 1) * LANES]
                met = late_ref[rows, (index * tiles + tile) * LANES : (index * tiles + tile + 1) * LANES]
                twice[slot] = twice[slot] + fold(here * met)
                if tile >= group:
                    gap = jnp.zeros((edge, LANES), jnp.float32)
                    turned = jnp.concatenate([gap, here, gap, here], axis=0).T
                    corner = jnp.where(low_half, turned[edge:half, :], turned[half + edge :, :])
                    once[slot] = once[slot] + fold(jnp.where(in_rest, here * corner, 0.0))
    value = jnp.zeros((1, LANES), jnp.float32)
    for slot in range(slots):
        slot_sum = jnp.sum(once[slot] + 2.0 * twice[slot])
        value = jnp.where(lane == place_ref[slot], slot_sum, value)
    sum_ref[...] = jnp.broadcast_to(value, sum_ref.shape)


def swap(value, mask, blocks):
    return lax.ppermute(value, "block", [(index, index ^ mask) for index in range(blocks)])


def body(green, chol, counts, move_slot, move_dest):
    walkers = lax.axis_size("walker")
    blocks = lax.axis_size("block")
    slots, share_width = green.shape
    vectors, occ_count, orb_count = chol.shape
    moves = move_slot.shape[1]
    keep = slots - moves
    share_rows = share_width // orb_count
    pack_rows = slots * share_rows
    table = jnp.concatenate([counts[None, :], move_slot.T, move_dest.T], axis=0)
    walker_index = lax.axis_index("walker").astype(jnp.int32).reshape(1)
    block_index = lax.axis_index("block").astype(jnp.int32).reshape(1)
    smem = pl.BlockSpec(memory_space=pltpu.SMEM)
    vmem = pl.BlockSpec(memory_space=pltpu.VMEM)
    limit = pltpu.CompilerParams(vmem_limit_bytes=32 * 1024 * 1024)

    spread = pltpu.VMEM((orb_count // LANES, share_rows * ROWS, LANES), jnp.float32)
    own_rows = pl.pallas_call(
        functools.partial(pack_kernel, (slots, share_rows, orb_count)),
        out_shape=jax.ShapeDtypeStruct((pack_rows, orb_count), jnp.bfloat16),
        in_specs=[vmem],
        out_specs=vmem,
        scratch_shapes=[spread],
        compiler_params=limit,
        name="pack",
    )(green)
    move_dims = (slots, share_rows, orb_count, walkers, moves, keep)
    *leaving, place = pl.pallas_call(
        functools.partial(leave_kernel, move_dims),
        out_shape=[jax.ShapeDtypeStruct((share_rows, orb_count), jnp.bfloat16)] * (walkers - 1)
        + [jax.ShapeDtypeStruct((slots,), jnp.int32)],
        in_specs=[smem, smem, vmem],
        out_specs=[vmem] * (walkers - 1) + [smem],
        scratch_shapes=[pltpu.VMEM((pack_rows, orb_count), jnp.float32)],
        compiler_params=limit,
        name="leave",
    )(walker_index, table, own_rows)
    coming = [
        lax.ppermute(
            leaving[shift - 1], "walker", [(z, (z + shift) % walkers) for z in range(walkers)]
        )
        for shift in range(1, walkers)
    ]

    group = 4
    groups = vectors // group
    chip_rows = 2 * share_rows
    weights = pl.pallas_call(
        functools.partial(order_kernel, (group, groups, chip_rows)),
        out_shape=jax.ShapeDtypeStruct((vectors * occ_count, orb_count), jnp.bfloat16),
        in_specs=[smem] + [pl.BlockSpec(memory_space=pl.ANY)] * 2,
        out_specs=vmem,
        scratch_shapes=[pltpu.SemaphoreType.DMA((5 * vectors,))],
        compiler_params=pltpu.CompilerParams(vmem_limit_bytes=48 * 1024 * 1024),
        cost_estimate=pl.CostEstimate(
            flops=0, bytes_accessed=4 * chol.size, transcendentals=0
        ),
        name="order",
    )(block_index, chol, own_rows)

    core, near_x, near_y = 1, 2, 4
    from_x = swap(own_rows, near_x, blocks)
    from_y = swap(own_rows, near_y, blocks)
    from_core = swap(own_rows, core, blocks)
    width = orb_count // 2
    from_x, from_y, weights, coming[:2] = lax.optimization_barrier(
        (from_x, from_y, weights, coming[:2])
    )
    far = [swap(from_y[:, :width], near_x, blocks), swap(from_x[:, width:], near_y, blocks)]
    near_pieces = [own_rows, from_core]
    for piece in (from_x, from_y):
        near_pieces += [piece, swap(piece, core, blocks)]

    dims = (slots, share_rows, group, groups, chip_rows)
    work = 2 * vectors * occ_count * orb_count * pack_rows
    near_sums, late = pl.pallas_call(
        functools.partial(near_kernel, dims),
        out_shape=[
            jax.ShapeDtypeStruct((slots * ROWS, LANES), jnp.float32),
            jax.ShapeDtypeStruct((slots * chip_rows, vectors * occ_count), jnp.float32),
        ],
        in_specs=[smem] + [vmem] * 7,
        out_specs=[vmem] * 2,
        scratch_shapes=[pltpu.VMEM((slots * 3 * chip_rows, group * occ_count), jnp.float32)]
        * groups,
        compiler_params=limit,
        cost_estimate=pl.CostEstimate(
            flops=6 * work, bytes_accessed=2 * chol.size, transcendentals=0
        ),
        name="near",
    )(block_index, weights, *near_pieces)
    far, near_sums = lax.optimization_barrier((far, near_sums))
    far_pieces = far + [swap(piece, core, blocks) for piece in far]
    all_sums = pl.pallas_call(
        functools.partial(far_kernel, dims),
        out_shape=jax.ShapeDtypeStruct((blocks * walkers, LANES), jnp.float32),
        in_specs=[smem] * 2 + [vmem] * 7,
        out_specs=vmem,
        scratch_shapes=[pltpu.VMEM((slots * chip_rows, group * occ_count), jnp.float32)] * groups,
        compiler_params=limit,
        cost_estimate=pl.CostEstimate(
            flops=2 * work, bytes_accessed=2 * chol.size, transcendentals=0
        ),
        name="far",
    )(block_index, place, weights, near_sums, late, *far_pieces)

    coming, _ = lax.optimization_barrier((coming, all_sums))
    new_green = pl.pallas_call(
        functools.partial(assemble_kernel, move_dims),
        out_shape=jax.ShapeDtypeStruct((keep, share_width), jnp.bfloat16),
        in_specs=[smem] * 2 + [vmem] * walkers,
        out_specs=vmem,
        scratch_shapes=[
            pltpu.VMEM((orb_count // LANES, share_rows * ROWS, LANES), jnp.float32),
            pltpu.VMEM(((slots + walkers - 1) * share_rows, orb_count), jnp.float32),
            pltpu.VMEM((orb_count // LANES, share_rows * ROWS, LANES), jnp.float32),
        ],
        compiler_params=limit,
        name="assemble",
    )(walker_index, table, green, *coming)

    energy_scale = 0.5 / (occ_count * math.sqrt(vectors * blocks))
    got = lax.all_to_all(
        all_sums, ("block", "walker"), split_axis=0, concat_axis=0, tiled=True
    )
    got_sums = jnp.sum(got, axis=0)
    own_sums = lax.dynamic_slice(got_sums, (walker_index[0] * keep,), (keep,))
    return (new_green, -energy_scale * own_sums)


def fits(mesh):
    blocks = mesh.shape["block"]
    walkers = mesh.shape["walker"]

    def check(green, chol, counts, move_slot, move_dest):
        vectors, occ_count, orb_count = chol.shape
        share_width = green.shape[1] // blocks
        moves = move_slot.shape[1]
        slots = green.shape[0] // walkers
        return (
            blocks == 8
            and walkers >= 2
            and walkers & (walkers - 1) == 0
            and (moves + walkers - 2) // (walkers - 1) == 1
            and slots <= ROWS
            and share_width % (orb_count * ROWS) == 0
            and orb_count % (2 * LANES) == 0
            and occ_count == blocks * (share_width // orb_count)
            and occ_count == LANES + LANES // 2
            and (vectors // blocks) % 4 == 0
            and walkers * (slots - moves) <= LANES
        )

    return check


def solution(mesh):
    in_specs = (P("walker", "block"), P("block", None, None), P(), P(), P())
    out_specs = (P("walker", "block"), P("walker"))
    check = fits(mesh)

    def run(*args):
        chosen = body if check(*args) else general_body
        return jax.shard_map(
            chosen, mesh=mesh, in_specs=in_specs, out_specs=out_specs, check_vma=False
        )(*args)

    return run
```

```python
import functools
import math

import jax
import jax.numpy as jnp
from jax import lax
from jax.experimental import pallas as pl
from jax.experimental.pallas import tpu as pltpu
from jax.sharding import PartitionSpec as P


def arrival_ranks(move_slot, move_dest):
    active = move_slot >= 0
    move_total = move_slot.shape[1]
    earlier = jnp.arange(move_total)[None, :] < jnp.arange(move_total)[:, None]
    same_target = (
        (move_dest[:, :, None] == move_dest[:, None, :]) & earlier[None, :, :] & active[:, None, :]
    )
    return (active, jnp.sum(same_target.astype(jnp.int32), axis=2))


def general_body(green, chol, counts, move_slot, move_dest):
    walker_total = lax.axis_size("walker")
    own_index = lax.axis_index("walker")
    slot_total = green.shape[0]
    share_width = green.shape[1]
    keep_total = slot_total - move_slot.shape[1]
    capacity = (move_slot.shape[1] + walker_total - 2) // (walker_total - 1)
    occ_count = chol.shape[1]
    orb_count = chol.shape[2]
    energy_scale = 0.5 / (occ_count * math.sqrt(chol.shape[0] * lax.axis_size("block")))
    active, move_rank = arrival_ranks(move_slot, move_dest)
    own_slots = move_slot[own_index]
    own_dests = move_dest[own_index]
    own_active = active[own_index]
    own_rank = move_rank[own_index]
    peer_ids = jnp.arange(walker_total)
    place_ids = jnp.arange(capacity)
    chosen = (
        (own_dests[None, None, :] == peer_ids[:, None, None])
        & (own_rank[None, None, :] == place_ids[None, :, None])
        & own_active[None, None, :]
    )
    send_slot = jnp.sum(jnp.where(chosen, own_slots[None, None, :], 0), axis=2).reshape(-1)
    present = jnp.any(chosen, axis=2).reshape(-1)
    arrive = jnp.any(
        (move_dest[:, None, :] == own_index)
        & (move_rank[:, None, :] == place_ids[None, :, None])
        & active[:, None, :],
        axis=2,
    ).reshape(-1)
    slot_ids = jnp.arange(slot_total)
    occupied = slot_ids < counts[own_index]
    leaving = jnp.any(own_slots[:, None] == slot_ids[None, :], axis=0)
    staying = occupied & jnp.logical_not(leaving)
    stay_rank = jnp.cumsum(staying.astype(jnp.int32)) - 1
    arrive_rank = jnp.cumsum(arrive.astype(jnp.int32)) - 1
    stay_total = jnp.sum(staying.astype(jnp.int32))
    targets = jnp.arange(keep_total)
    from_stay = jnp.sum(
        jnp.where(
            staying[None, :] & (stay_rank[None, :] == targets[:, None]), slot_ids[None, :], 0
        ),
        axis=1,
    )
    arrive_ids = jnp.arange(arrive.shape[0]) + slot_total
    from_arrive = jnp.sum(
        jnp.where(
            arrive[None, :] & (arrive_rank[None, :] == (targets - stay_total)[:, None]),
            arrive_ids[None, :],
            0,
        ),
        axis=1,
    )
    source_row = jnp.where(targets < stay_total, from_stay, from_arrive)
    outgoing = jnp.where(
        present[:, None], jnp.take(green, send_slot, axis=0), jnp.zeros((), jnp.bfloat16)
    )
    outgoing = outgoing.reshape(walker_total, capacity, share_width)

    def walker_energy(walker_row):
        green_mat = walker_row.reshape(occ_count, orb_count)
        transfer = jnp.einsum("gip,jp->gij", chol, green_mat, preferred_element_type=jnp.float32)
        return jnp.sum(transfer * jnp.swapaxes(transfer, 1, 2))

    got_rows = lax.all_to_all(outgoing, "walker", split_axis=0, concat_axis=0, tiled=True)
    source_pool = jnp.concatenate([green, got_rows.reshape(-1, share_width)], axis=0)
    new_green = jnp.take(source_pool, source_row, axis=0)
    complete = lax.all_gather(new_green, "block", axis=1, tiled=True)
    partial_value = lax.map(walker_energy, complete)
    energy = -energy_scale * lax.psum(partial_value, "block")
    return (new_green, energy)


LANES = 128
ROWS = 8


def spread_slots(green_ref, spread, share_rows):
    slots = green_ref.shape[0]
    tiles = spread.shape[0]
    for row in range(share_rows):
        for tile in range(tiles):
            col = (row * tiles + tile) * LANES
            block = green_ref[:, col : col + LANES].astype(jnp.float32)
            spread[tile, row * ROWS : row * ROWS + slots, :] = block


def pack_kernel(dims, green_ref, own_ref, spread):
    slots, share_rows, orb_count = dims
    spread_slots(green_ref, spread, share_rows)
    for tile in range(orb_count // LANES):
        dense = [spread[tile, pl.ds(slot, share_rows, stride=ROWS), :] for slot in range(slots)]
        packed = jnp.concatenate(dense, axis=0).astype(jnp.bfloat16)
        own_ref[:, tile * LANES : (tile + 1) * LANES] = packed


class Moves:
    def __init__(self, table_ref, moves):
        self.table, self.moves = table_ref, moves

    def count(self, device):
        return self.table[0, device]

    def slot(self, device, move):
        return self.table[1 + move, device]

    def dest(self, device, move):
        return self.table[1 + self.moves + move, device]

    def staying(self, device):
        total = self.count(device)
        for move in range(self.moves):
            total = total - jnp.where(self.slot(device, move) >= 0, 1, 0)
        return total

    def goes_to(self, own, slot):
        target = jnp.int32(-1)
        for move in range(self.moves):
            target = jnp.where(self.slot(own, move) == slot, self.dest(own, move), target)
        return target


def leave_kernel(dims, ident_ref, table_ref, own_ref, *refs):
    slots, share_rows, orb_count, walkers, moves, keep = dims
    leave_refs, wide = refs[:-1], refs[-1]
    table = Moves(table_ref, moves)
    wide[...] = own_ref[...].astype(jnp.float32)
    own = ident_ref[0]
    for shift in range(1, walkers):
        target = lax.rem(own + shift, walkers)
        chosen = jnp.int32(0)
        for move in range(moves):
            hit = (table.dest(own, move) == target) & (table.slot(own, move) >= 0)
            chosen = jnp.where(hit, table.slot(own, move), chosen)
        start = pl.multiple_of(chosen * share_rows, ROWS)
        leave_refs[shift - 1][...] = wide[pl.ds(start, share_rows), :].astype(jnp.bfloat16)


def assemble_kernel(dims, ident_ref, table_ref, green_ref, *refs):
    slots, share_rows, orb_count, walkers, moves, keep = dims
    table = Moves(table_ref, moves)
    come_refs = refs[: walkers - 1]
    new_ref, spread, pool, out = refs[walkers - 1 :]
    own = ident_ref[0]
    tiles = orb_count // LANES
    spread_slots(green_ref, spread, share_rows)
    for slot in range(slots):
        for tile in range(tiles):
            pool[
                slot * share_rows : (slot + 1) * share_rows, tile * LANES : (tile + 1) * LANES
            ] = spread[tile, pl.ds(slot, share_rows, stride=ROWS), :]
    for shift in range(1, walkers):
        start = (slots + shift - 1) * share_rows
        pool[start : start + share_rows, :] = come_refs[shift - 1][...].astype(jnp.float32)

    sources = [jnp.int32(0)] * keep
    rank = jnp.int32(0)
    for slot in range(slots):
        stays = (slot < table.count(own)) & (table.goes_to(own, slot) < 0)
        for target in range(keep):
            sources[target] = jnp.where(stays & (rank == target), slot, sources[target])
        rank = rank + jnp.where(stays, 1, 0)
    for device in range(walkers):
        comes = jnp.bool_(False)
        for move in range(moves):
            comes = comes | ((table.dest(device, move) == own) & (table.slot(device, move) >= 0))
        comes = comes & (device != own)
        shift = lax.rem(own - device + walkers, walkers)
        for target in range(keep):
            sources[target] = jnp.where(
                comes & (rank == target), slots + shift - 1, sources[target]
            )
        rank = rank + jnp.where(comes, 1, 0)
    for target in range(keep):
        start = pl.multiple_of(sources[target] * share_rows, ROWS)
        for tile in range(tiles):
            out[tile, pl.ds(target, share_rows, stride=ROWS), :] = pool[
                pl.ds(start, share_rows), tile * LANES : (tile + 1) * LANES
            ]
    for row in range(share_rows):
        for tile in range(tiles):
            col = (row * tiles + tile) * LANES
            new_ref[:, col : col + LANES] = out[
                tile, row * ROWS : row * ROWS + keep, :
            ].astype(jnp.bfloat16)


def find_places(dims, own, table, place_ref):
    slots, walkers, moves, keep = dims
    rank = jnp.int32(0)
    for slot in range(slots):
        live = slot < table.count(own)
        gone_to = table.goes_to(own, slot)
        stays = live & (gone_to < 0)
        there = jnp.maximum(gone_to, 0)
        ahead = table.staying(there)
        for device in range(walkers):
            for move in range(moves):
                hit = (
                    (device < own)
                    & (table.dest(device, move) == there)
                    & (table.slot(device, move) >= 0)
                )
                ahead = ahead + jnp.where(hit, 1, 0)
        place = jnp.where(stays, own * keep + rank, there * keep + ahead)
        place_ref[slot] = jnp.where(live, place, -1)
        rank = rank + jnp.where(stays, 1, 0)


def order_kernel(
    dims, ident_ref, walker_ref, table_ref, chol_ref, core_ref, out_ref, place_ref, sems
):
    del core_ref
    group, groups, chip_rows, place_dims = dims
    chip = ident_ref[0] // 2
    edge = LANES - 2 * chip_rows
    rest = 2 * chip_rows - edge
    copies = []

    def add(vec, distance, start, size, place):
        row = pl.multiple_of(jnp.bitwise_xor(chip, distance) * chip_rows + start, 16)
        copies.append(
            pltpu.make_async_copy(
                chol_ref.at[vec, pl.ds(row, size), :],
                out_ref.at[pl.ds(place, size), :],
                sems.at[len(copies)],
            )
        )

    for index in range(groups):
        for item in range(group):
            vec = index * group + item
            place = index * group * 4 * chip_rows + item * LANES
            add(vec, 0, 0, chip_rows, place)
            add(vec, 1, 0, chip_rows, place + chip_rows)
            add(vec, 2, 0, edge, place + 2 * chip_rows)
            place = index * group * 4 * chip_rows + group * LANES + item * rest
            add(vec, 2, edge, chip_rows - edge, place)
            add(vec, 3, 0, chip_rows, place + chip_rows - edge)
    for copy in copies:
        copy.start()
    find_places(place_dims, walker_ref[0], Moves(table_ref, place_dims[2]), place_ref)
    for copy in copies:
        copy.wait()


def padded(rows):
    return -(-rows // 16) * 16


def stacked(refs):
    values = []
    for ref in refs:
        rows, width = ref.shape
        values.append(ref[...])
        if padded(rows) > rows:
            values.append(jnp.zeros((padded(rows) - rows, width), jnp.bfloat16))
    return jnp.concatenate(values, axis=0)


def times(left, right):
    return lax.dot_general(
        left, right, (((1,), (1,)), ((), ())), preferred_element_type=jnp.float32
    )


def near_kernel(dims, ident_ref, weight_ref, *refs):
    slots, share_rows, group, groups, chip_rows = dims
    piece_refs = refs[:6]
    sum_ref, late_ref = refs[6:8]
    trans_refs = refs[8:]
    own = ident_ref[0]
    core = lax.rem(own, 2)
    pad_rows = padded(piece_refs[0].shape[0])
    near = 3 * chip_rows
    size = 4 * chip_rows * group
    edge = near - LANES
    half = LANES // 2
    left = stacked(piece_refs)
    lane = lax.broadcasted_iota(jnp.int32, (1, LANES), 1)
    low_half = lane < half
    in_edge = jnp.where(low_half, lane, lane - half) < edge
    sums = [jnp.zeros((ROWS, LANES), jnp.float32) for _ in range(slots)]

    def fold(value):
        return jnp.sum(value.reshape(-1, ROWS, LANES), axis=0)

    for index in range(groups):
        trans = trans_refs[index]
        result = times(left, weight_ref[index * size : (index + 1) * size, :])
        for piece in range(6):
            source = jnp.bitwise_xor(core, piece % 2)
            for slot in range(slots):
                start = piece * pad_rows + slot * share_rows
                place = slot * near + (piece // 2) * chip_rows + source * share_rows
                trans[pl.ds(pl.multiple_of(place, ROWS), share_rows), :] = result[
                    start : start + share_rows, :
                ]
        for slot in range(slots):
            base = slot * near
            late = slice(slot * chip_rows, (slot + 1) * chip_rows)
            acc = sums[slot]
            for pair in range(group // 2):
                col = (group + pair) * LANES
                top = trans[base : base + LANES, col : col + LANES].T
                edge_rows = trans[base + LANES : base + near, col : col + LANES]
                gap = jnp.zeros((half - edge, LANES), jnp.float32)
                bottom = jnp.concatenate([edge_rows, gap, edge_rows, gap], axis=0).T
                for side in range(2):
                    vec = 2 * pair + side
                    high = trans[base : base + LANES, vec * LANES : (vec + 1) * LANES]
                    acc = acc + fold(high * high.T)
                    across = trans[base + LANES : base + near, vec * LANES : (vec + 1) * LANES]
                    acc = acc + 2.0 * fold(across * top[side * half : side * half + edge, :])
                    late_ref[
                        late, (index * (group + group // 2) + vec) * LANES : (
                            index * (group + group // 2) + vec + 1
                        ) * LANES
                    ] = top[side * half + edge : (side + 1) * half, :]
                corner = jnp.where(low_half, bottom[:edge, :], bottom[half : half + edge, :])
                acc = acc + fold(jnp.where(in_edge, edge_rows * corner, 0.0))
                rest = jnp.where(low_half, bottom[edge:half, :], bottom[half + edge :, :])
                place = (index * (group + group // 2) + group + pair) * LANES
                late_ref[late, place : place + LANES] = jnp.where(in_edge, rest, 0.0)
            sums[slot] = acc
    sum_ref[...] = jnp.concatenate(sums, axis=0)


def far_kernel(dims, ident_ref, place_ref, weight_ref, near_sum_ref, late_ref, *refs):
    slots, share_rows, group, groups, chip_rows = dims
    piece_refs = refs[:4]
    sum_ref = refs[4]
    trans_refs = refs[5:]
    own = ident_ref[0]
    core = lax.rem(own, 2)
    pack_rows, width = piece_refs[0].shape
    pad_rows = padded(pack_rows)
    half = LANES // 2
    edge = half - chip_rows
    size = 4 * chip_rows * group
    lane = lax.broadcasted_iota(jnp.int32, (1, LANES), 1)
    low_half = lane < half
    in_rest = jnp.where(low_half, lane, lane - half) >= edge
    lefts = [stacked(piece_refs[part::2]) for part in range(2)]
    twice = [jnp.zeros((ROWS, LANES), jnp.float32) for _ in range(slots)]
    once = [near_sum_ref[slot * ROWS : (slot + 1) * ROWS, :] for slot in range(slots)]

    def fold(value):
        return jnp.sum(value.reshape(-1, ROWS, LANES), axis=0)

    tiles = group + group // 2
    for index in range(groups):
        trans = trans_refs[index]
        rows = slice(index * size, (index + 1) * size)
        result = times(lefts[0], weight_ref[rows, :width])
        result = result + times(lefts[1], weight_ref[rows, width:])
        for piece in range(2):
            source = jnp.bitwise_xor(core, piece)
            for slot in range(slots):
                start = piece * pad_rows + slot * share_rows
                place = slot * chip_rows + source * share_rows
                trans[pl.ds(pl.multiple_of(place, ROWS), share_rows), :] = result[
                    start : start + share_rows, :
                ]
        for slot in range(slots):
            rows = slice(slot * chip_rows, (slot + 1) * chip_rows)
            for tile in range(tiles):
                here = trans[rows, tile * LANES : (tile + 1) * LANES]
                met = late_ref[rows, (index * tiles + tile) * LANES : (index * tiles + tile + 1) * LANES]
                twice[slot] = twice[slot] + fold(here * met)
                if tile >= group:
                    gap = jnp.zeros((edge, LANES), jnp.float32)
                    turned = jnp.concatenate([gap, here, gap, here], axis=0).T
                    corner = jnp.where(low_half, turned[edge:half, :], turned[half + edge :, :])
                    once[slot] = once[slot] + fold(jnp.where(in_rest, here * corner, 0.0))
    value = jnp.zeros((1, LANES), jnp.float32)
    for slot in range(slots):
        slot_sum = jnp.sum(once[slot] + 2.0 * twice[slot])
        value = jnp.where(lane == place_ref[slot], slot_sum, value)
    sum_ref[...] = jnp.broadcast_to(value, sum_ref.shape)


def swap(value, mask, blocks):
    return lax.ppermute(value, "block", [(index, index ^ mask) for index in range(blocks)])


def body(green, chol, counts, move_slot, move_dest):
    walkers = lax.axis_size("walker")
    blocks = lax.axis_size("block")
    slots, share_width = green.shape
    vectors, occ_count, orb_count = chol.shape
    moves = move_slot.shape[1]
    keep = slots - moves
    share_rows = share_width // orb_count
    pack_rows = slots * share_rows
    table = jnp.concatenate([counts[None, :], move_slot.T, move_dest.T], axis=0)
    walker_index = lax.axis_index("walker").astype(jnp.int32).reshape(1)
    block_index = lax.axis_index("block").astype(jnp.int32).reshape(1)
    smem = pl.BlockSpec(memory_space=pltpu.SMEM)
    vmem = pl.BlockSpec(memory_space=pltpu.VMEM)
    limit = pltpu.CompilerParams(vmem_limit_bytes=32 * 1024 * 1024)

    spread = pltpu.VMEM((orb_count // LANES, share_rows * ROWS, LANES), jnp.float32)
    own_rows = pl.pallas_call(
        functools.partial(pack_kernel, (slots, share_rows, orb_count)),
        out_shape=jax.ShapeDtypeStruct((pack_rows, orb_count), jnp.bfloat16),
        in_specs=[vmem],
        out_specs=vmem,
        scratch_shapes=[spread],
        compiler_params=limit,
        name="pack",
    )(green)
    move_dims = (slots, share_rows, orb_count, walkers, moves, keep)
    leaving = pl.pallas_call(
        functools.partial(leave_kernel, move_dims),
        out_shape=[jax.ShapeDtypeStruct((share_rows, orb_count), jnp.bfloat16)] * (walkers - 1),
        in_specs=[smem, smem, vmem],
        out_specs=[vmem] * (walkers - 1),
        scratch_shapes=[pltpu.VMEM((pack_rows, orb_count), jnp.float32)],
        compiler_params=limit,
        name="leave",
    )(walker_index, table, own_rows)
    coming = [
        lax.ppermute(
            leaving[shift - 1], "walker", [(z, (z + shift) % walkers) for z in range(walkers)]
        )
        for shift in range(1, walkers)
    ]

    group = 4
    groups = vectors // group
    chip_rows = 2 * share_rows
    core, near_x, near_y = 1, 2, 4
    from_x = swap(own_rows, near_x, blocks)
    from_y = swap(own_rows, near_y, blocks)
    from_core = swap(own_rows, core, blocks)
    weights, place = pl.pallas_call(
        functools.partial(
            order_kernel, (group, groups, chip_rows, (slots, walkers, moves, keep))
        ),
        out_shape=[
            jax.ShapeDtypeStruct((vectors * occ_count, orb_count), jnp.bfloat16),
            jax.ShapeDtypeStruct((slots,), jnp.int32),
        ],
        in_specs=[smem] * 3 + [pl.BlockSpec(memory_space=pl.ANY)] * 2,
        out_specs=[vmem, smem],
        scratch_shapes=[pltpu.SemaphoreType.DMA((5 * vectors,))],
        compiler_params=pltpu.CompilerParams(vmem_limit_bytes=48 * 1024 * 1024),
        cost_estimate=pl.CostEstimate(
            flops=0, bytes_accessed=4 * chol.size, transcendentals=0
        ),
        name="order",
    )(block_index, walker_index, table, chol, own_rows)
    width = orb_count // 2
    from_x, from_y, weights, coming[:2] = lax.optimization_barrier(
        (from_x, from_y, weights, coming[:2])
    )
    far = [swap(from_y[:, :width], near_x, blocks), swap(from_x[:, width:], near_y, blocks)]
    near_pieces = [own_rows, from_core]
    for piece in (from_x, from_y):
        near_pieces += [piece, swap(piece, core, blocks)]

    dims = (slots, share_rows, group, groups, chip_rows)
    work = 2 * vectors * occ_count * orb_count * pack_rows
    near_sums, late = pl.pallas_call(
        functools.partial(near_kernel, dims),
        out_shape=[
            jax.ShapeDtypeStruct((slots * ROWS, LANES), jnp.float32),
            jax.ShapeDtypeStruct((slots * chip_rows, vectors * occ_count), jnp.float32),
        ],
        in_specs=[smem] + [vmem] * 7,
        out_specs=[vmem] * 2,
        scratch_shapes=[pltpu.VMEM((slots * 3 * chip_rows, group * occ_count), jnp.float32)]
        * groups,
        compiler_params=limit,
        cost_estimate=pl.CostEstimate(
            flops=6 * work, bytes_accessed=2 * chol.size, transcendentals=0
        ),
        name="near",
    )(block_index, weights, *near_pieces)
    far, near_sums = lax.optimization_barrier((far, near_sums))
    far_pieces = far + [swap(piece, core, blocks) for piece in far]
    all_sums = pl.pallas_call(
        functools.partial(far_kernel, dims),
        out_shape=jax.ShapeDtypeStruct((blocks * walkers, LANES), jnp.float32),
        in_specs=[smem] * 2 + [vmem] * 7,
        out_specs=vmem,
        scratch_shapes=[pltpu.VMEM((slots * chip_rows, group * occ_count), jnp.float32)] * groups,
        compiler_params=limit,
        cost_estimate=pl.CostEstimate(
            flops=2 * work, bytes_accessed=2 * chol.size, transcendentals=0
        ),
        name="far",
    )(block_index, place, weights, near_sums, late, *far_pieces)

    coming, _ = lax.optimization_barrier((coming, all_sums))
    new_green = pl.pallas_call(
        functools.partial(assemble_kernel, move_dims),
        out_shape=jax.ShapeDtypeStruct((keep, share_width), jnp.bfloat16),
        in_specs=[smem] * 2 + [vmem] * walkers,
        out_specs=vmem,
        scratch_shapes=[
            pltpu.VMEM((orb_count // LANES, share_rows * ROWS, LANES), jnp.float32),
            pltpu.VMEM(((slots + walkers - 1) * share_rows, orb_count), jnp.float32),
            pltpu.VMEM((orb_count // LANES, share_rows * ROWS, LANES), jnp.float32),
        ],
        compiler_params=limit,
        name="assemble",
    )(walker_index, table, green, *coming)

    energy_scale = 0.5 / (occ_count * math.sqrt(vectors * blocks))
    got = lax.all_to_all(
        all_sums, ("block", "walker"), split_axis=0, concat_axis=0, tiled=True
    )
    got_sums = jnp.sum(got, axis=0)
    own_sums = lax.dynamic_slice(got_sums, (walker_index[0] * keep,), (keep,))
    return (new_green, -energy_scale * own_sums)


def fits(mesh):
    blocks = mesh.shape["block"]
    walkers = mesh.shape["walker"]

    def check(green, chol, counts, move_slot, move_dest):
        vectors, occ_count, orb_count = chol.shape
        share_width = green.shape[1] // blocks
        moves = move_slot.shape[1]
        slots = green.shape[0] // walkers
        return (
            blocks == 8
            and walkers >= 2
            and walkers & (walkers - 1) == 0
            and (moves + walkers - 2) // (walkers - 1) == 1
            and slots <= ROWS
            and share_width % (orb_count * ROWS) == 0
            and orb_count % (2 * LANES) == 0
            and occ_count == blocks * (share_width // orb_count)
            and occ_count == LANES + LANES // 2
            and (vectors // blocks) % 4 == 0
            and walkers * (slots - moves) <= LANES
        )

    return check


def solution(mesh):
    in_specs = (P("walker", "block"), P("block", None, None), P(), P(), P())
    out_specs = (P("walker", "block"), P("walker"))
    check = fits(mesh)

    def run(*args):
        chosen = body if check(*args) else general_body
        return jax.shard_map(
            chosen, mesh=mesh, in_specs=in_specs, out_specs=out_specs, check_vma=False
        )(*args)

    return run
```

```python
import functools
import math

import jax
import jax.numpy as jnp
from jax import lax
from jax.experimental import pallas as pl
from jax.experimental.pallas import tpu as pltpu
from jax.sharding import PartitionSpec as P


def arrival_ranks(move_slot, move_dest):
    active = move_slot >= 0
    move_total = move_slot.shape[1]
    earlier = jnp.arange(move_total)[None, :] < jnp.arange(move_total)[:, None]
    same_target = (
        (move_dest[:, :, None] == move_dest[:, None, :]) & earlier[None, :, :] & active[:, None, :]
    )
    return (active, jnp.sum(same_target.astype(jnp.int32), axis=2))


def general_body(green, chol, counts, move_slot, move_dest):
    walker_total = lax.axis_size("walker")
    own_index = lax.axis_index("walker")
    slot_total = green.shape[0]
    share_width = green.shape[1]
    keep_total = slot_total - move_slot.shape[1]
    capacity = (move_slot.shape[1] + walker_total - 2) // (walker_total - 1)
    occ_count = chol.shape[1]
    orb_count = chol.shape[2]
    energy_scale = 0.5 / (occ_count * math.sqrt(chol.shape[0] * lax.axis_size("block")))
    active, move_rank = arrival_ranks(move_slot, move_dest)
    own_slots = move_slot[own_index]
    own_dests = move_dest[own_index]
    own_active = active[own_index]
    own_rank = move_rank[own_index]
    peer_ids = jnp.arange(walker_total)
    place_ids = jnp.arange(capacity)
    chosen = (
        (own_dests[None, None, :] == peer_ids[:, None, None])
        & (own_rank[None, None, :] == place_ids[None, :, None])
        & own_active[None, None, :]
    )
    send_slot = jnp.sum(jnp.where(chosen, own_slots[None, None, :], 0), axis=2).reshape(-1)
    present = jnp.any(chosen, axis=2).reshape(-1)
    arrive = jnp.any(
        (move_dest[:, None, :] == own_index)
        & (move_rank[:, None, :] == place_ids[None, :, None])
        & active[:, None, :],
        axis=2,
    ).reshape(-1)
    slot_ids = jnp.arange(slot_total)
    occupied = slot_ids < counts[own_index]
    leaving = jnp.any(own_slots[:, None] == slot_ids[None, :], axis=0)
    staying = occupied & jnp.logical_not(leaving)
    stay_rank = jnp.cumsum(staying.astype(jnp.int32)) - 1
    arrive_rank = jnp.cumsum(arrive.astype(jnp.int32)) - 1
    stay_total = jnp.sum(staying.astype(jnp.int32))
    targets = jnp.arange(keep_total)
    from_stay = jnp.sum(
        jnp.where(
            staying[None, :] & (stay_rank[None, :] == targets[:, None]), slot_ids[None, :], 0
        ),
        axis=1,
    )
    arrive_ids = jnp.arange(arrive.shape[0]) + slot_total
    from_arrive = jnp.sum(
        jnp.where(
            arrive[None, :] & (arrive_rank[None, :] == (targets - stay_total)[:, None]),
            arrive_ids[None, :],
            0,
        ),
        axis=1,
    )
    source_row = jnp.where(targets < stay_total, from_stay, from_arrive)
    outgoing = jnp.where(
        present[:, None], jnp.take(green, send_slot, axis=0), jnp.zeros((), jnp.bfloat16)
    )
    outgoing = outgoing.reshape(walker_total, capacity, share_width)

    def walker_energy(walker_row):
        green_mat = walker_row.reshape(occ_count, orb_count)
        transfer = jnp.einsum("gip,jp->gij", chol, green_mat, preferred_element_type=jnp.float32)
        return jnp.sum(transfer * jnp.swapaxes(transfer, 1, 2))

    got_rows = lax.all_to_all(outgoing, "walker", split_axis=0, concat_axis=0, tiled=True)
    source_pool = jnp.concatenate([green, got_rows.reshape(-1, share_width)], axis=0)
    new_green = jnp.take(source_pool, source_row, axis=0)
    complete = lax.all_gather(new_green, "block", axis=1, tiled=True)
    partial_value = lax.map(walker_energy, complete)
    energy = -energy_scale * lax.psum(partial_value, "block")
    return (new_green, energy)


LANES = 128
ROWS = 8


def spread_slots(green_ref, spread, share_rows):
    slots = green_ref.shape[0]
    tiles = spread.shape[0]
    for row in range(share_rows):
        for tile in range(tiles):
            col = (row * tiles + tile) * LANES
            block = green_ref[:, col : col + LANES].astype(jnp.float32)
            spread[tile, row * ROWS : row * ROWS + slots, :] = block


def pack_kernel(dims, green_ref, own_ref, spread):
    slots, share_rows, orb_count = dims
    spread_slots(green_ref, spread, share_rows)
    for tile in range(orb_count // LANES):
        dense = [spread[tile, pl.ds(slot, share_rows, stride=ROWS), :] for slot in range(slots)]
        packed = jnp.concatenate(dense, axis=0).astype(jnp.bfloat16)
        own_ref[:, tile * LANES : (tile + 1) * LANES] = packed


class Moves:
    def __init__(self, table_ref, moves):
        self.table, self.moves = table_ref, moves

    def count(self, device):
        return self.table[0, device]

    def slot(self, device, move):
        return self.table[1 + move, device]

    def dest(self, device, move):
        return self.table[1 + self.moves + move, device]

    def staying(self, device):
        total = self.count(device)
        for move in range(self.moves):
            total = total - jnp.where(self.slot(device, move) >= 0, 1, 0)
        return total

    def goes_to(self, own, slot):
        target = jnp.int32(-1)
        for move in range(self.moves):
            target = jnp.where(self.slot(own, move) == slot, self.dest(own, move), target)
        return target


def leave_kernel(dims, ident_ref, table_ref, own_ref, *refs):
    slots, share_rows, orb_count, walkers, moves, keep = dims
    leave_refs, wide = refs[:-1], refs[-1]
    table = Moves(table_ref, moves)
    wide[...] = own_ref[...].astype(jnp.float32)
    own = ident_ref[0]
    for shift in range(1, walkers):
        target = lax.rem(own + shift, walkers)
        chosen = jnp.int32(0)
        for move in range(moves):
            hit = (table.dest(own, move) == target) & (table.slot(own, move) >= 0)
            chosen = jnp.where(hit, table.slot(own, move), chosen)
        start = pl.multiple_of(chosen * share_rows, ROWS)
        leave_refs[shift - 1][...] = wide[pl.ds(start, share_rows), :].astype(jnp.bfloat16)


def assemble_kernel(dims, ident_ref, table_ref, green_ref, *refs):
    slots, share_rows, orb_count, walkers, moves, keep = dims
    table = Moves(table_ref, moves)
    come_refs = refs[: walkers - 1]
    new_ref, spread, pool, out = refs[walkers - 1 :]
    own = ident_ref[0]
    tiles = orb_count // LANES
    spread_slots(green_ref, spread, share_rows)
    for slot in range(slots):
        for tile in range(tiles):
            pool[
                slot * share_rows : (slot + 1) * share_rows, tile * LANES : (tile + 1) * LANES
            ] = spread[tile, pl.ds(slot, share_rows, stride=ROWS), :]
    for shift in range(1, walkers):
        start = (slots + shift - 1) * share_rows
        pool[start : start + share_rows, :] = come_refs[shift - 1][...].astype(jnp.float32)

    sources = [jnp.int32(0)] * keep
    rank = jnp.int32(0)
    for slot in range(slots):
        stays = (slot < table.count(own)) & (table.goes_to(own, slot) < 0)
        for target in range(keep):
            sources[target] = jnp.where(stays & (rank == target), slot, sources[target])
        rank = rank + jnp.where(stays, 1, 0)
    for device in range(walkers):
        comes = jnp.bool_(False)
        for move in range(moves):
            comes = comes | ((table.dest(device, move) == own) & (table.slot(device, move) >= 0))
        comes = comes & (device != own)
        shift = lax.rem(own - device + walkers, walkers)
        for target in range(keep):
            sources[target] = jnp.where(
                comes & (rank == target), slots + shift - 1, sources[target]
            )
        rank = rank + jnp.where(comes, 1, 0)
    for target in range(keep):
        start = pl.multiple_of(sources[target] * share_rows, ROWS)
        for tile in range(tiles):
            out[tile, pl.ds(target, share_rows, stride=ROWS), :] = pool[
                pl.ds(start, share_rows), tile * LANES : (tile + 1) * LANES
            ]
    for row in range(share_rows):
        for tile in range(tiles):
            col = (row * tiles + tile) * LANES
            new_ref[:, col : col + LANES] = out[
                tile, row * ROWS : row * ROWS + keep, :
            ].astype(jnp.bfloat16)


def find_places(dims, own, table, place_ref):
    slots, walkers, moves, keep = dims
    rank = jnp.int32(0)
    for slot in range(slots):
        live = slot < table.count(own)
        gone_to = table.goes_to(own, slot)
        stays = live & (gone_to < 0)
        there = jnp.maximum(gone_to, 0)
        ahead = table.staying(there)
        for device in range(walkers):
            for move in range(moves):
                hit = (
                    (device < own)
                    & (table.dest(device, move) == there)
                    & (table.slot(device, move) >= 0)
                )
                ahead = ahead + jnp.where(hit, 1, 0)
        place = jnp.where(stays, own * keep + rank, there * keep + ahead)
        place_ref[slot] = jnp.where(live, place, -1)
        rank = rank + jnp.where(stays, 1, 0)


def order_kernel(
    dims, ident_ref, walker_ref, table_ref, chol_ref, core_ref, out_ref, place_ref, sems
):
    del core_ref
    group, groups, chip_rows, place_dims = dims
    chip = ident_ref[0] // 2
    edge = LANES - 2 * chip_rows
    rest = 2 * chip_rows - edge
    copies = []

    def add(vec, distance, start, size, place):
        row = pl.multiple_of(jnp.bitwise_xor(chip, distance) * chip_rows + start, 16)
        copies.append(
            pltpu.make_async_copy(
                chol_ref.at[vec, pl.ds(row, size), :],
                out_ref.at[pl.ds(place, size), :],
                sems.at[len(copies)],
            )
        )

    for index in range(groups):
        for item in range(group):
            vec = index * group + item
            place = index * group * 4 * chip_rows + item * LANES
            add(vec, 0, 0, chip_rows, place)
            add(vec, 1, 0, chip_rows, place + chip_rows)
            add(vec, 2, 0, edge, place + 2 * chip_rows)
            place = index * group * 4 * chip_rows + group * LANES + item * rest
            add(vec, 2, edge, chip_rows - edge, place)
            add(vec, 3, 0, chip_rows, place + chip_rows - edge)
    for copy in copies:
        copy.start()
    find_places(place_dims, walker_ref[0], Moves(table_ref, place_dims[2]), place_ref)
    for copy in copies:
        copy.wait()


def padded(rows):
    return -(-rows // 16) * 16


def stacked(refs):
    values = []
    for ref in refs:
        rows, width = ref.shape
        values.append(ref[...])
        if padded(rows) > rows:
            values.append(jnp.zeros((padded(rows) - rows, width), jnp.bfloat16))
    return jnp.concatenate(values, axis=0)


def times(left, right):
    return lax.dot_general(
        left, right, (((1,), (1,)), ((), ())), preferred_element_type=jnp.float32
    )


def near_kernel(dims, ident_ref, weight_ref, *refs):
    slots, share_rows, group, groups, chip_rows = dims
    own_ref, core_ref, x_ref, y_ref, turned_ref = refs[:5]
    piece_refs = [own_ref, core_ref, x_ref, turned_ref.at[0], y_ref, turned_ref.at[1]]
    sum_ref, late_ref = refs[5:7]
    trans_refs = refs[7:]
    own = ident_ref[0]
    core = lax.rem(own, 2)
    pad_rows = padded(piece_refs[0].shape[0])
    near = 3 * chip_rows
    size = 4 * chip_rows * group
    edge = near - LANES
    half = LANES // 2
    left = stacked(piece_refs)
    lane = lax.broadcasted_iota(jnp.int32, (1, LANES), 1)
    low_half = lane < half
    in_edge = jnp.where(low_half, lane, lane - half) < edge
    sums = [jnp.zeros((ROWS, LANES), jnp.float32) for _ in range(slots)]

    def fold(value):
        return jnp.sum(value.reshape(-1, ROWS, LANES), axis=0)

    for index in range(groups):
        trans = trans_refs[index]
        result = times(left, weight_ref[index * size : (index + 1) * size, :])
        for piece in range(6):
            source = jnp.bitwise_xor(core, piece % 2)
            for slot in range(slots):
                start = piece * pad_rows + slot * share_rows
                place = slot * near + (piece // 2) * chip_rows + source * share_rows
                trans[pl.ds(pl.multiple_of(place, ROWS), share_rows), :] = result[
                    start : start + share_rows, :
                ]
        for slot in range(slots):
            base = slot * near
            late = slice(slot * chip_rows, (slot + 1) * chip_rows)
            acc = sums[slot]
            for pair in range(group // 2):
                col = (group + pair) * LANES
                top = trans[base : base + LANES, col : col + LANES].T
                edge_rows = trans[base + LANES : base + near, col : col + LANES]
                gap = jnp.zeros((half - edge, LANES), jnp.float32)
                bottom = jnp.concatenate([edge_rows, gap, edge_rows, gap], axis=0).T
                for side in range(2):
                    vec = 2 * pair + side
                    high = trans[base : base + LANES, vec * LANES : (vec + 1) * LANES]
                    acc = acc + fold(high * high.T)
                    across = trans[base + LANES : base + near, vec * LANES : (vec + 1) * LANES]
                    acc = acc + 2.0 * fold(across * top[side * half : side * half + edge, :])
                    late_ref[
                        late, (index * (group + group // 2) + vec) * LANES : (
                            index * (group + group // 2) + vec + 1
                        ) * LANES
                    ] = top[side * half + edge : (side + 1) * half, :]
                corner = jnp.where(low_half, bottom[:edge, :], bottom[half : half + edge, :])
                acc = acc + fold(jnp.where(in_edge, edge_rows * corner, 0.0))
                rest = jnp.where(low_half, bottom[edge:half, :], bottom[half + edge :, :])
                place = (index * (group + group // 2) + group + pair) * LANES
                late_ref[late, place : place + LANES] = jnp.where(in_edge, rest, 0.0)
            sums[slot] = acc
    sum_ref[...] = jnp.concatenate(sums, axis=0)


def far_kernel(dims, ident_ref, place_ref, weight_ref, near_sum_ref, late_ref, *refs):
    slots, share_rows, group, groups, chip_rows = dims
    here_ref, there_ref, sum_ref = refs[:3]
    trans_refs = refs[3:]
    own = ident_ref[0]
    core = lax.rem(own, 2)
    _, pack_rows, width = here_ref.shape
    pad_rows = padded(pack_rows)
    half = LANES // 2
    edge = half - chip_rows
    size = 4 * chip_rows * group
    lane = lax.broadcasted_iota(jnp.int32, (1, LANES), 1)
    low_half = lane < half
    in_rest = jnp.where(low_half, lane, lane - half) >= edge
    lefts = [stacked([here_ref.at[part], there_ref.at[part]]) for part in range(2)]
    twice = [jnp.zeros((ROWS, LANES), jnp.float32) for _ in range(slots)]
    once = [near_sum_ref[slot * ROWS : (slot + 1) * ROWS, :] for slot in range(slots)]

    def fold(value):
        return jnp.sum(value.reshape(-1, ROWS, LANES), axis=0)

    tiles = group + group // 2
    for index in range(groups):
        trans = trans_refs[index]
        rows = slice(index * size, (index + 1) * size)
        result = times(lefts[0], weight_ref[rows, :width])
        result = result + times(lefts[1], weight_ref[rows, width:])
        for piece in range(2):
            source = jnp.bitwise_xor(core, piece)
            for slot in range(slots):
                start = piece * pad_rows + slot * share_rows
                place = slot * chip_rows + source * share_rows
                trans[pl.ds(pl.multiple_of(place, ROWS), share_rows), :] = result[
                    start : start + share_rows, :
                ]
        for slot in range(slots):
            rows = slice(slot * chip_rows, (slot + 1) * chip_rows)
            for tile in range(tiles):
                here = trans[rows, tile * LANES : (tile + 1) * LANES]
                met = late_ref[rows, (index * tiles + tile) * LANES : (index * tiles + tile + 1) * LANES]
                twice[slot] = twice[slot] + fold(here * met)
                if tile >= group:
                    gap = jnp.zeros((edge, LANES), jnp.float32)
                    turned = jnp.concatenate([gap, here, gap, here], axis=0).T
                    corner = jnp.where(low_half, turned[edge:half, :], turned[half + edge :, :])
                    once[slot] = once[slot] + fold(jnp.where(in_rest, here * corner, 0.0))
    value = jnp.zeros((1, LANES), jnp.float32)
    for slot in range(slots):
        slot_sum = jnp.sum(once[slot] + 2.0 * twice[slot])
        value = jnp.where(lane == place_ref[slot], slot_sum, value)
    sum_ref[...] = jnp.broadcast_to(value, sum_ref.shape)


def swap(value, mask, blocks):
    return lax.ppermute(value, "block", [(index, index ^ mask) for index in range(blocks)])


def pair_kernel(one_ref, two_ref, out_ref):
    out_ref[0] = one_ref[...]
    out_ref[1] = two_ref[...]


def pair(one, two):
    vmem = pl.BlockSpec(memory_space=pltpu.VMEM)
    return pl.pallas_call(
        pair_kernel,
        out_shape=jax.ShapeDtypeStruct((2, *one.shape), one.dtype),
        in_specs=[vmem] * 2,
        out_specs=vmem,
        compiler_params=pltpu.CompilerParams(vmem_limit_bytes=16 * 1024 * 1024),
        name="pair",
    )(one, two)


def body(green, chol, counts, move_slot, move_dest):
    walkers = lax.axis_size("walker")
    blocks = lax.axis_size("block")
    slots, share_width = green.shape
    vectors, occ_count, orb_count = chol.shape
    moves = move_slot.shape[1]
    keep = slots - moves
    share_rows = share_width // orb_count
    pack_rows = slots * share_rows
    table = jnp.concatenate([counts[None, :], move_slot.T, move_dest.T], axis=0)
    walker_index = lax.axis_index("walker").astype(jnp.int32).reshape(1)
    block_index = lax.axis_index("block").astype(jnp.int32).reshape(1)
    smem = pl.BlockSpec(memory_space=pltpu.SMEM)
    vmem = pl.BlockSpec(memory_space=pltpu.VMEM)
    limit = pltpu.CompilerParams(vmem_limit_bytes=32 * 1024 * 1024)

    spread = pltpu.VMEM((orb_count // LANES, share_rows * ROWS, LANES), jnp.float32)
    own_rows = pl.pallas_call(
        functools.partial(pack_kernel, (slots, share_rows, orb_count)),
        out_shape=jax.ShapeDtypeStruct((pack_rows, orb_count), jnp.bfloat16),
        in_specs=[vmem],
        out_specs=vmem,
        scratch_shapes=[spread],
        compiler_params=limit,
        name="pack",
    )(green)
    move_dims = (slots, share_rows, orb_count, walkers, moves, keep)
    leaving = pl.pallas_call(
        functools.partial(leave_kernel, move_dims),
        out_shape=[jax.ShapeDtypeStruct((share_rows, orb_count), jnp.bfloat16)] * (walkers - 1),
        in_specs=[smem, smem, vmem],
        out_specs=[vmem] * (walkers - 1),
        scratch_shapes=[pltpu.VMEM((pack_rows, orb_count), jnp.float32)],
        compiler_params=limit,
        name="leave",
    )(walker_index, table, own_rows)
    coming = [
        lax.ppermute(
            leaving[shift - 1], "walker", [(z, (z + shift) % walkers) for z in range(walkers)]
        )
        for shift in range(1, walkers)
    ]

    group = 4
    groups = vectors // group
    chip_rows = 2 * share_rows
    core, near_x, near_y = 1, 2, 4
    from_x = swap(own_rows, near_x, blocks)
    from_y = swap(own_rows, near_y, blocks)
    from_core = swap(own_rows, core, blocks)
    weights, place = pl.pallas_call(
        functools.partial(
            order_kernel, (group, groups, chip_rows, (slots, walkers, moves, keep))
        ),
        out_shape=[
            jax.ShapeDtypeStruct((vectors * occ_count, orb_count), jnp.bfloat16),
            jax.ShapeDtypeStruct((slots,), jnp.int32),
        ],
        in_specs=[smem] * 3 + [pl.BlockSpec(memory_space=pl.ANY)] * 2,
        out_specs=[vmem, smem],
        scratch_shapes=[pltpu.SemaphoreType.DMA((5 * vectors,))],
        compiler_params=pltpu.CompilerParams(vmem_limit_bytes=48 * 1024 * 1024),
        cost_estimate=pl.CostEstimate(
            flops=0, bytes_accessed=4 * chol.size, transcendentals=0
        ),
        name="order",
    )(block_index, walker_index, table, chol, own_rows)
    width = orb_count // 2
    from_x, from_y, from_core, weights, coming[:2] = lax.optimization_barrier(
        (from_x, from_y, from_core, weights, coming[:2])
    )
    far = [swap(from_y[:, :width], near_x, blocks), swap(from_x[:, width:], near_y, blocks)]
    turned = swap(pair(from_x, from_y), core, blocks)
    near_pieces = [own_rows, from_core, from_x, from_y, turned]

    dims = (slots, share_rows, group, groups, chip_rows)
    work = 2 * vectors * occ_count * orb_count * pack_rows
    near_sums, late = pl.pallas_call(
        functools.partial(near_kernel, dims),
        out_shape=[
            jax.ShapeDtypeStruct((slots * ROWS, LANES), jnp.float32),
            jax.ShapeDtypeStruct((slots * chip_rows, vectors * occ_count), jnp.float32),
        ],
        in_specs=[smem] + [vmem] * 6,
        out_specs=[vmem] * 2,
        scratch_shapes=[pltpu.VMEM((slots * 3 * chip_rows, group * occ_count), jnp.float32)]
        * groups,
        compiler_params=limit,
        cost_estimate=pl.CostEstimate(
            flops=6 * work, bytes_accessed=2 * chol.size, transcendentals=0
        ),
        name="near",
    )(block_index, weights, *near_pieces)
    far, near_sums = lax.optimization_barrier((far, near_sums))
    here = pair(*far)
    far_pieces = [here, swap(here, core, blocks)]
    all_sums = pl.pallas_call(
        functools.partial(far_kernel, dims),
        out_shape=jax.ShapeDtypeStruct((blocks * walkers, LANES), jnp.float32),
        in_specs=[smem] * 2 + [vmem] * 5,
        out_specs=vmem,
        scratch_shapes=[pltpu.VMEM((slots * chip_rows, group * occ_count), jnp.float32)] * groups,
        compiler_params=limit,
        cost_estimate=pl.CostEstimate(
            flops=2 * work, bytes_accessed=2 * chol.size, transcendentals=0
        ),
        name="far",
    )(block_index, place, weights, near_sums, late, *far_pieces)

    coming, _ = lax.optimization_barrier((coming, all_sums))
    new_green = pl.pallas_call(
        functools.partial(assemble_kernel, move_dims),
        out_shape=jax.ShapeDtypeStruct((keep, share_width), jnp.bfloat16),
        in_specs=[smem] * 2 + [vmem] * walkers,
        out_specs=vmem,
        scratch_shapes=[
            pltpu.VMEM((orb_count // LANES, share_rows * ROWS, LANES), jnp.float32),
            pltpu.VMEM(((slots + walkers - 1) * share_rows, orb_count), jnp.float32),
            pltpu.VMEM((orb_count // LANES, share_rows * ROWS, LANES), jnp.float32),
        ],
        compiler_params=limit,
        name="assemble",
    )(walker_index, table, green, *coming)

    energy_scale = 0.5 / (occ_count * math.sqrt(vectors * blocks))
    got = lax.all_to_all(
        all_sums, ("block", "walker"), split_axis=0, concat_axis=0, tiled=True
    )
    got_sums = jnp.sum(got, axis=0)
    own_sums = lax.dynamic_slice(got_sums, (walker_index[0] * keep,), (keep,))
    return (new_green, -energy_scale * own_sums)


def fits(mesh):
    blocks = mesh.shape["block"]
    walkers = mesh.shape["walker"]

    def check(green, chol, counts, move_slot, move_dest):
        vectors, occ_count, orb_count = chol.shape
        share_width = green.shape[1] // blocks
        moves = move_slot.shape[1]
        slots = green.shape[0] // walkers
        return (
            blocks == 8
            and walkers >= 2
            and walkers & (walkers - 1) == 0
            and (moves + walkers - 2) // (walkers - 1) == 1
            and slots <= ROWS
            and share_width % (orb_count * ROWS) == 0
            and orb_count % (2 * LANES) == 0
            and occ_count == blocks * (share_width // orb_count)
            and occ_count == LANES + LANES // 2
            and (vectors // blocks) % 4 == 0
            and walkers * (slots - moves) <= LANES
        )

    return check


def solution(mesh):
    in_specs = (P("walker", "block"), P("block", None, None), P(), P(), P())
    out_specs = (P("walker", "block"), P("walker"))
    check = fits(mesh)

    def run(*args):
        chosen = body if check(*args) else general_body
        return jax.shard_map(
            chosen, mesh=mesh, in_specs=in_specs, out_specs=out_specs, check_vma=False
        )(*args)

    return run
```

```python
import functools
import math

import jax
import jax.numpy as jnp
from jax import lax
from jax.experimental import pallas as pl
from jax.experimental.pallas import tpu as pltpu
from jax.sharding import PartitionSpec as P


def arrival_ranks(move_slot, move_dest):
    active = move_slot >= 0
    move_total = move_slot.shape[1]
    earlier = jnp.arange(move_total)[None, :] < jnp.arange(move_total)[:, None]
    same_target = (
        (move_dest[:, :, None] == move_dest[:, None, :]) & earlier[None, :, :] & active[:, None, :]
    )
    return (active, jnp.sum(same_target.astype(jnp.int32), axis=2))


def general_body(green, chol, counts, move_slot, move_dest):
    walker_total = lax.axis_size("walker")
    own_index = lax.axis_index("walker")
    slot_total = green.shape[0]
    share_width = green.shape[1]
    keep_total = slot_total - move_slot.shape[1]
    capacity = (move_slot.shape[1] + walker_total - 2) // (walker_total - 1)
    occ_count = chol.shape[1]
    orb_count = chol.shape[2]
    energy_scale = 0.5 / (occ_count * math.sqrt(chol.shape[0] * lax.axis_size("block")))
    active, move_rank = arrival_ranks(move_slot, move_dest)
    own_slots = move_slot[own_index]
    own_dests = move_dest[own_index]
    own_active = active[own_index]
    own_rank = move_rank[own_index]
    peer_ids = jnp.arange(walker_total)
    place_ids = jnp.arange(capacity)
    chosen = (
        (own_dests[None, None, :] == peer_ids[:, None, None])
        & (own_rank[None, None, :] == place_ids[None, :, None])
        & own_active[None, None, :]
    )
    send_slot = jnp.sum(jnp.where(chosen, own_slots[None, None, :], 0), axis=2).reshape(-1)
    present = jnp.any(chosen, axis=2).reshape(-1)
    arrive = jnp.any(
        (move_dest[:, None, :] == own_index)
        & (move_rank[:, None, :] == place_ids[None, :, None])
        & active[:, None, :],
        axis=2,
    ).reshape(-1)
    slot_ids = jnp.arange(slot_total)
    occupied = slot_ids < counts[own_index]
    leaving = jnp.any(own_slots[:, None] == slot_ids[None, :], axis=0)
    staying = occupied & jnp.logical_not(leaving)
    stay_rank = jnp.cumsum(staying.astype(jnp.int32)) - 1
    arrive_rank = jnp.cumsum(arrive.astype(jnp.int32)) - 1
    stay_total = jnp.sum(staying.astype(jnp.int32))
    targets = jnp.arange(keep_total)
    from_stay = jnp.sum(
        jnp.where(
            staying[None, :] & (stay_rank[None, :] == targets[:, None]), slot_ids[None, :], 0
        ),
        axis=1,
    )
    arrive_ids = jnp.arange(arrive.shape[0]) + slot_total
    from_arrive = jnp.sum(
        jnp.where(
            arrive[None, :] & (arrive_rank[None, :] == (targets - stay_total)[:, None]),
            arrive_ids[None, :],
            0,
        ),
        axis=1,
    )
    source_row = jnp.where(targets < stay_total, from_stay, from_arrive)
    outgoing = jnp.where(
        present[:, None], jnp.take(green, send_slot, axis=0), jnp.zeros((), jnp.bfloat16)
    )
    outgoing = outgoing.reshape(walker_total, capacity, share_width)

    def walker_energy(walker_row):
        green_mat = walker_row.reshape(occ_count, orb_count)
        transfer = jnp.einsum("gip,jp->gij", chol, green_mat, preferred_element_type=jnp.float32)
        return jnp.sum(transfer * jnp.swapaxes(transfer, 1, 2))

    got_rows = lax.all_to_all(outgoing, "walker", split_axis=0, concat_axis=0, tiled=True)
    source_pool = jnp.concatenate([green, got_rows.reshape(-1, share_width)], axis=0)
    new_green = jnp.take(source_pool, source_row, axis=0)
    complete = lax.all_gather(new_green, "block", axis=1, tiled=True)
    partial_value = lax.map(walker_energy, complete)
    energy = -energy_scale * lax.psum(partial_value, "block")
    return (new_green, energy)


LANES = 128
ROWS = 8


def spread_slots(green_ref, spread, share_rows):
    slots = green_ref.shape[0]
    tiles = spread.shape[0]
    for row in range(share_rows):
        for tile in range(tiles):
            col = (row * tiles + tile) * LANES
            block = green_ref[:, col : col + LANES].astype(jnp.float32)
            spread[tile, row * ROWS : row * ROWS + slots, :] = block


def pack_kernel(dims, green_ref, own_ref, spread):
    slots, share_rows, orb_count = dims
    spread_slots(green_ref, spread, share_rows)
    for tile in range(orb_count // LANES):
        dense = [spread[tile, pl.ds(slot, share_rows, stride=ROWS), :] for slot in range(slots)]
        packed = jnp.concatenate(dense, axis=0).astype(jnp.bfloat16)
        own_ref[:, tile * LANES : (tile + 1) * LANES] = packed


class Moves:
    def __init__(self, table_ref, moves):
        self.table, self.moves = table_ref, moves

    def count(self, device):
        return self.table[0, device]

    def slot(self, device, move):
        return self.table[1 + move, device]

    def dest(self, device, move):
        return self.table[1 + self.moves + move, device]

    def staying(self, device):
        total = self.count(device)
        for move in range(self.moves):
            total = total - jnp.where(self.slot(device, move) >= 0, 1, 0)
        return total

    def goes_to(self, own, slot):
        target = jnp.int32(-1)
        for move in range(self.moves):
            target = jnp.where(self.slot(own, move) == slot, self.dest(own, move), target)
        return target


def leave_kernel(dims, ident_ref, table_ref, own_ref, *refs):
    slots, share_rows, orb_count, walkers, moves, keep = dims
    leave_refs, place_ref, wide = refs[:-2], refs[-2], refs[-1]
    table = Moves(table_ref, moves)
    wide[...] = own_ref[...].astype(jnp.float32)
    own = ident_ref[0]
    for shift in range(1, walkers):
        target = lax.rem(own + shift, walkers)
        chosen = jnp.int32(0)
        for move in range(moves):
            hit = (table.dest(own, move) == target) & (table.slot(own, move) >= 0)
            chosen = jnp.where(hit, table.slot(own, move), chosen)
        start = pl.multiple_of(chosen * share_rows, ROWS)
        leave_refs[shift - 1][...] = wide[pl.ds(start, share_rows), :].astype(jnp.bfloat16)
    rank = jnp.int32(0)
    for slot in range(slots):
        live = slot < table.count(own)
        gone_to = table.goes_to(own, slot)
        stays = live & (gone_to < 0)
        there = jnp.maximum(gone_to, 0)
        ahead = table.staying(there)
        for device in range(walkers):
            for move in range(moves):
                hit = (
                    (device < own)
                    & (table.dest(device, move) == there)
                    & (table.slot(device, move) >= 0)
                )
                ahead = ahead + jnp.where(hit, 1, 0)
        place = jnp.where(stays, own * keep + rank, there * keep + ahead)
        place_ref[slot] = jnp.where(live, place, -1)
        rank = rank + jnp.where(stays, 1, 0)


def assemble_kernel(dims, ident_ref, table_ref, green_ref, *refs):
    slots, share_rows, orb_count, walkers, moves, keep = dims
    table = Moves(table_ref, moves)
    come_refs = refs[: walkers - 1]
    new_ref, spread, pool, out = refs[walkers - 1 :]
    own = ident_ref[0]
    tiles = orb_count // LANES
    spread_slots(green_ref, spread, share_rows)
    for slot in range(slots):
        for tile in range(tiles):
            pool[
                slot * share_rows : (slot + 1) * share_rows, tile * LANES : (tile + 1) * LANES
            ] = spread[tile, pl.ds(slot, share_rows, stride=ROWS), :]
    for shift in range(1, walkers):
        start = (slots + shift - 1) * share_rows
        pool[start : start + share_rows, :] = come_refs[shift - 1][...].astype(jnp.float32)

    sources = [jnp.int32(0)] * keep
    rank = jnp.int32(0)
    for slot in range(slots):
        stays = (slot < table.count(own)) & (table.goes_to(own, slot) < 0)
        for target in range(keep):
            sources[target] = jnp.where(stays & (rank == target), slot, sources[target])
        rank = rank + jnp.where(stays, 1, 0)
    for device in range(walkers):
        comes = jnp.bool_(False)
        for move in range(moves):
            comes = comes | ((table.dest(device, move) == own) & (table.slot(device, move) >= 0))
        comes = comes & (device != own)
        shift = lax.rem(own - device + walkers, walkers)
        for target in range(keep):
            sources[target] = jnp.where(
                comes & (rank == target), slots + shift - 1, sources[target]
            )
        rank = rank + jnp.where(comes, 1, 0)
    for target in range(keep):
        start = pl.multiple_of(sources[target] * share_rows, ROWS)
        for tile in range(tiles):
            out[tile, pl.ds(target, share_rows, stride=ROWS), :] = pool[
                pl.ds(start, share_rows), tile * LANES : (tile + 1) * LANES
            ]
    for row in range(share_rows):
        for tile in range(tiles):
            col = (row * tiles + tile) * LANES
            new_ref[:, col : col + LANES] = out[
                tile, row * ROWS : row * ROWS + keep, :
            ].astype(jnp.bfloat16)


def order_kernel(dims, ident_ref, chol_ref, own_ref, out_ref, sems):
    del own_ref
    group, groups, chip_rows = dims
    chip = ident_ref[0] // 2
    edge = LANES - 2 * chip_rows
    rest = 2 * chip_rows - edge
    copies = []

    def add(vec, distance, start, size, place):
        row = pl.multiple_of(jnp.bitwise_xor(chip, distance) * chip_rows + start, 16)
        copies.append(
            pltpu.make_async_copy(
                chol_ref.at[vec, pl.ds(row, size), :],
                out_ref.at[pl.ds(place, size), :],
                sems.at[len(copies)],
            )
        )

    for index in range(groups):
        for item in range(group):
            vec = index * group + item
            place = index * group * 4 * chip_rows + item * LANES
            add(vec, 0, 0, chip_rows, place)
            add(vec, 1, 0, chip_rows, place + chip_rows)
            add(vec, 2, 0, edge, place + 2 * chip_rows)
            place = index * group * 4 * chip_rows + group * LANES + item * rest
            add(vec, 2, edge, chip_rows - edge, place)
            add(vec, 3, 0, chip_rows, place + chip_rows - edge)
    for copy in copies:
        copy.start()
    for copy in copies:
        copy.wait()


def padded(rows):
    return -(-rows // 16) * 16


def stacked(refs):
    values = []
    for ref in refs:
        rows, width = ref.shape
        values.append(ref[...])
        if padded(rows) > rows:
            values.append(jnp.zeros((padded(rows) - rows, width), jnp.bfloat16))
    return jnp.concatenate(values, axis=0)


def times(left, right):
    return lax.dot_general(
        left, right, (((1,), (1,)), ((), ())), preferred_element_type=jnp.float32
    )


def near_kernel(dims, ident_ref, weight_ref, *refs):
    slots, share_rows, group, groups, chip_rows = dims
    own_ref, core_ref, x_ref, y_ref, turned_ref = refs[:5]
    piece_refs = [own_ref, core_ref, x_ref, turned_ref.at[0], y_ref, turned_ref.at[1]]
    sum_ref, late_ref = refs[5:7]
    trans_refs = refs[7:]
    own = ident_ref[0]
    core = lax.rem(own, 2)
    pad_rows = padded(piece_refs[0].shape[0])
    near = 3 * chip_rows
    size = 4 * chip_rows * group
    edge = near - LANES
    half = LANES // 2
    left = stacked(piece_refs)
    lane = lax.broadcasted_iota(jnp.int32, (1, LANES), 1)
    low_half = lane < half
    in_edge = jnp.where(low_half, lane, lane - half) < edge
    sums = [jnp.zeros((ROWS, LANES), jnp.float32) for _ in range(slots)]

    def fold(value):
        return jnp.sum(value.reshape(-1, ROWS, LANES), axis=0)

    for index in range(groups):
        trans = trans_refs[index]
        result = times(left, weight_ref[index * size : (index + 1) * size, :])
        for piece in range(6):
            source = jnp.bitwise_xor(core, piece % 2)
            for slot in range(slots):
                start = piece * pad_rows + slot * share_rows
                place = slot * near + (piece // 2) * chip_rows + source * share_rows
                trans[pl.ds(pl.multiple_of(place, ROWS), share_rows), :] = result[
                    start : start + share_rows, :
                ]
        for slot in range(slots):
            base = slot * near
            late = slice(slot * chip_rows, (slot + 1) * chip_rows)
            acc = sums[slot]
            for pair in range(group // 2):
                col = (group + pair) * LANES
                top = trans[base : base + LANES, col : col + LANES].T
                edge_rows = trans[base + LANES : base + near, col : col + LANES]
                gap = jnp.zeros((half - edge, LANES), jnp.float32)
                bottom = jnp.concatenate([edge_rows, gap, edge_rows, gap], axis=0).T
                for side in range(2):
                    vec = 2 * pair + side
                    high = trans[base : base + LANES, vec * LANES : (vec + 1) * LANES]
                    acc = acc + fold(high * high.T)
                    across = trans[base + LANES : base + near, vec * LANES : (vec + 1) * LANES]
                    acc = acc + 2.0 * fold(across * top[side * half : side * half + edge, :])
                    late_ref[
                        late, (index * (group + group // 2) + vec) * LANES : (
                            index * (group + group // 2) + vec + 1
                        ) * LANES
                    ] = top[side * half + edge : (side + 1) * half, :]
                corner = jnp.where(low_half, bottom[:edge, :], bottom[half : half + edge, :])
                acc = acc + fold(jnp.where(in_edge, edge_rows * corner, 0.0))
                rest = jnp.where(low_half, bottom[edge:half, :], bottom[half + edge :, :])
                place = (index * (group + group // 2) + group + pair) * LANES
                late_ref[late, place : place + LANES] = jnp.where(in_edge, rest, 0.0)
            sums[slot] = acc
    sum_ref[...] = jnp.concatenate(sums, axis=0)


def far_kernel(dims, ident_ref, place_ref, weight_ref, near_sum_ref, late_ref, *refs):
    slots, share_rows, group, groups, chip_rows = dims
    here_ref, there_ref, sum_ref = refs[:3]
    trans_refs = refs[3:]
    own = ident_ref[0]
    core = lax.rem(own, 2)
    _, pack_rows, width = here_ref.shape
    pad_rows = padded(pack_rows)
    half = LANES // 2
    edge = half - chip_rows
    size = 4 * chip_rows * group
    lane = lax.broadcasted_iota(jnp.int32, (1, LANES), 1)
    low_half = lane < half
    in_rest = jnp.where(low_half, lane, lane - half) >= edge
    lefts = [stacked([here_ref.at[part], there_ref.at[part]]) for part in range(2)]
    twice = [jnp.zeros((ROWS, LANES), jnp.float32) for _ in range(slots)]
    once = [near_sum_ref[slot * ROWS : (slot + 1) * ROWS, :] for slot in range(slots)]

    def fold(value):
        return jnp.sum(value.reshape(-1, ROWS, LANES), axis=0)

    tiles = group + group // 2
    for index in range(groups):
        trans = trans_refs[index]
        rows = slice(index * size, (index + 1) * size)
        result = times(lefts[0], weight_ref[rows, :width])
        result = result + times(lefts[1], weight_ref[rows, width:])
        for piece in range(2):
            source = jnp.bitwise_xor(core, piece)
            for slot in range(slots):
                start = piece * pad_rows + slot * share_rows
                place = slot * chip_rows + source * share_rows
                trans[pl.ds(pl.multiple_of(place, ROWS), share_rows), :] = result[
                    start : start + share_rows, :
                ]
        for slot in range(slots):
            rows = slice(slot * chip_rows, (slot + 1) * chip_rows)
            for tile in range(tiles):
                here = trans[rows, tile * LANES : (tile + 1) * LANES]
                met = late_ref[rows, (index * tiles + tile) * LANES : (index * tiles + tile + 1) * LANES]
                twice[slot] = twice[slot] + fold(here * met)
                if tile >= group:
                    gap = jnp.zeros((edge, LANES), jnp.float32)
                    turned = jnp.concatenate([gap, here, gap, here], axis=0).T
                    corner = jnp.where(low_half, turned[edge:half, :], turned[half + edge :, :])
                    once[slot] = once[slot] + fold(jnp.where(in_rest, here * corner, 0.0))
    value = jnp.zeros((1, LANES), jnp.float32)
    for slot in range(slots):
        slot_sum = jnp.sum(once[slot] + 2.0 * twice[slot])
        value = jnp.where(lane == place_ref[slot], slot_sum, value)
    sum_ref[...] = jnp.broadcast_to(value, sum_ref.shape)


def swap(value, mask, blocks):
    return lax.ppermute(value, "block", [(index, index ^ mask) for index in range(blocks)])


def pair_kernel(one_ref, two_ref, out_ref):
    out_ref[0] = one_ref[...]
    out_ref[1] = two_ref[...]


def pair(one, two):
    vmem = pl.BlockSpec(memory_space=pltpu.VMEM)
    return pl.pallas_call(
        pair_kernel,
        out_shape=jax.ShapeDtypeStruct((2, *one.shape), one.dtype),
        in_specs=[vmem] * 2,
        out_specs=vmem,
        compiler_params=pltpu.CompilerParams(vmem_limit_bytes=16 * 1024 * 1024),
        name="pair",
    )(one, two)


def body(green, chol, counts, move_slot, move_dest):
    walkers = lax.axis_size("walker")
    blocks = lax.axis_size("block")
    slots, share_width = green.shape
    vectors, occ_count, orb_count = chol.shape
    moves = move_slot.shape[1]
    keep = slots - moves
    share_rows = share_width // orb_count
    pack_rows = slots * share_rows
    table = jnp.concatenate([counts[None, :], move_slot.T, move_dest.T], axis=0)
    walker_index = lax.axis_index("walker").astype(jnp.int32).reshape(1)
    block_index = lax.axis_index("block").astype(jnp.int32).reshape(1)
    smem = pl.BlockSpec(memory_space=pltpu.SMEM)
    vmem = pl.BlockSpec(memory_space=pltpu.VMEM)
    limit = pltpu.CompilerParams(vmem_limit_bytes=32 * 1024 * 1024)

    spread = pltpu.VMEM((orb_count // LANES, share_rows * ROWS, LANES), jnp.float32)
    own_rows = pl.pallas_call(
        functools.partial(pack_kernel, (slots, share_rows, orb_count)),
        out_shape=jax.ShapeDtypeStruct((pack_rows, orb_count), jnp.bfloat16),
        in_specs=[vmem],
        out_specs=vmem,
        scratch_shapes=[spread],
        compiler_params=limit,
        name="pack",
    )(green)
    move_dims = (slots, share_rows, orb_count, walkers, moves, keep)
    *leaving, place = pl.pallas_call(
        functools.partial(leave_kernel, move_dims),
        out_shape=[jax.ShapeDtypeStruct((share_rows, orb_count), jnp.bfloat16)] * (walkers - 1)
        + [jax.ShapeDtypeStruct((slots,), jnp.int32)],
        in_specs=[smem, smem, vmem],
        out_specs=[vmem] * (walkers - 1) + [smem],
        scratch_shapes=[pltpu.VMEM((pack_rows, orb_count), jnp.float32)],
        compiler_params=limit,
        name="leave",
    )(walker_index, table, own_rows)
    coming = [
        lax.ppermute(
            leaving[shift - 1], "walker", [(z, (z + shift) % walkers) for z in range(walkers)]
        )
        for shift in range(1, walkers)
    ]

    group = 4
    groups = vectors // group
    chip_rows = 2 * share_rows
    weights = pl.pallas_call(
        functools.partial(order_kernel, (group, groups, chip_rows)),
        out_shape=jax.ShapeDtypeStruct((vectors * occ_count, orb_count), jnp.bfloat16),
        in_specs=[smem] + [pl.BlockSpec(memory_space=pl.ANY)] * 2,
        out_specs=vmem,
        scratch_shapes=[pltpu.SemaphoreType.DMA((5 * vectors,))],
        compiler_params=pltpu.CompilerParams(vmem_limit_bytes=48 * 1024 * 1024),
        cost_estimate=pl.CostEstimate(
            flops=0, bytes_accessed=4 * chol.size, transcendentals=0
        ),
        name="order",
    )(block_index, chol, own_rows)

    core, near_x, near_y = 1, 2, 4
    from_x = swap(own_rows, near_x, blocks)
    from_y = swap(own_rows, near_y, blocks)
    from_core = swap(own_rows, core, blocks)
    width = orb_count // 2
    from_x, from_y, from_core, weights, coming[:2] = lax.optimization_barrier(
        (from_x, from_y, from_core, weights, coming[:2])
    )
    far = [swap(from_y[:, :width], near_x, blocks), swap(from_x[:, width:], near_y, blocks)]
    turned = swap(pair(from_x, from_y), core, blocks)
    near_pieces = [own_rows, from_core, from_x, from_y, turned]

    dims = (slots, share_rows, group, groups, chip_rows)
    work = 2 * vectors * occ_count * orb_count * pack_rows
    near_sums, late = pl.pallas_call(
        functools.partial(near_kernel, dims),
        out_shape=[
            jax.ShapeDtypeStruct((slots * ROWS, LANES), jnp.float32),
            jax.ShapeDtypeStruct((slots * chip_rows, vectors * occ_count), jnp.float32),
        ],
        in_specs=[smem] + [vmem] * 6,
        out_specs=[vmem] * 2,
        scratch_shapes=[pltpu.VMEM((slots * 3 * chip_rows, group * occ_count), jnp.float32)]
        * groups,
        compiler_params=limit,
        cost_estimate=pl.CostEstimate(
            flops=6 * work, bytes_accessed=2 * chol.size, transcendentals=0
        ),
        name="near",
    )(block_index, weights, *near_pieces)
    far, near_sums = lax.optimization_barrier((far, near_sums))
    here = pair(*far)
    far_pieces = [here, swap(here, core, blocks)]
    all_sums = pl.pallas_call(
        functools.partial(far_kernel, dims),
        out_shape=jax.ShapeDtypeStruct((blocks * walkers, LANES), jnp.float32),
        in_specs=[smem] * 2 + [vmem] * 5,
        out_specs=vmem,
        scratch_shapes=[pltpu.VMEM((slots * chip_rows, group * occ_count), jnp.float32)] * groups,
        compiler_params=limit,
        cost_estimate=pl.CostEstimate(
            flops=2 * work, bytes_accessed=2 * chol.size, transcendentals=0
        ),
        name="far",
    )(block_index, place, weights, near_sums, late, *far_pieces)

    coming, _ = lax.optimization_barrier((coming, all_sums))
    new_green = pl.pallas_call(
        functools.partial(assemble_kernel, move_dims),
        out_shape=jax.ShapeDtypeStruct((keep, share_width), jnp.bfloat16),
        in_specs=[smem] * 2 + [vmem] * walkers,
        out_specs=vmem,
        scratch_shapes=[
            pltpu.VMEM((orb_count // LANES, share_rows * ROWS, LANES), jnp.float32),
            pltpu.VMEM(((slots + walkers - 1) * share_rows, orb_count), jnp.float32),
            pltpu.VMEM((orb_count // LANES, share_rows * ROWS, LANES), jnp.float32),
        ],
        compiler_params=limit,
        name="assemble",
    )(walker_index, table, green, *coming)

    energy_scale = 0.5 / (occ_count * math.sqrt(vectors * blocks))
    got = lax.all_to_all(
        all_sums, ("block", "walker"), split_axis=0, concat_axis=0, tiled=True
    )
    got_sums = jnp.sum(got, axis=0)
    own_sums = lax.dynamic_slice(got_sums, (walker_index[0] * keep,), (keep,))
    return (new_green, -energy_scale * own_sums)


def fits(mesh):
    blocks = mesh.shape["block"]
    walkers = mesh.shape["walker"]

    def check(green, chol, counts, move_slot, move_dest):
        vectors, occ_count, orb_count = chol.shape
        share_width = green.shape[1] // blocks
        moves = move_slot.shape[1]
        slots = green.shape[0] // walkers
        return (
            blocks == 8
            and walkers >= 2
            and walkers & (walkers - 1) == 0
            and (moves + walkers - 2) // (walkers - 1) == 1
            and slots <= ROWS
            and share_width % (orb_count * ROWS) == 0
            and orb_count % (2 * LANES) == 0
            and occ_count == blocks * (share_width // orb_count)
            and occ_count == LANES + LANES // 2
            and (vectors // blocks) % 4 == 0
            and walkers * (slots - moves) <= LANES
        )

    return check


def solution(mesh):
    in_specs = (P("walker", "block"), P("block", None, None), P(), P(), P())
    out_specs = (P("walker", "block"), P("walker"))
    check = fits(mesh)

    def run(*args):
        chosen = body if check(*args) else general_body
        return jax.shard_map(
            chosen, mesh=mesh, in_specs=in_specs, out_specs=out_specs, check_vma=False
        )(*args)

    return run
```

```python
import functools
import math

import jax
import jax.numpy as jnp
from jax import lax
from jax.experimental import pallas as pl
from jax.experimental.pallas import tpu as pltpu
from jax.sharding import PartitionSpec as P


def arrival_ranks(move_slot, move_dest):
    active = move_slot >= 0
    move_total = move_slot.shape[1]
    earlier = jnp.arange(move_total)[None, :] < jnp.arange(move_total)[:, None]
    same_target = (
        (move_dest[:, :, None] == move_dest[:, None, :]) & earlier[None, :, :] & active[:, None, :]
    )
    return (active, jnp.sum(same_target.astype(jnp.int32), axis=2))


def general_body(green, chol, counts, move_slot, move_dest):
    walker_total = lax.axis_size("walker")
    own_index = lax.axis_index("walker")
    slot_total = green.shape[0]
    share_width = green.shape[1]
    keep_total = slot_total - move_slot.shape[1]
    capacity = (move_slot.shape[1] + walker_total - 2) // (walker_total - 1)
    occ_count = chol.shape[1]
    orb_count = chol.shape[2]
    energy_scale = 0.5 / (occ_count * math.sqrt(chol.shape[0] * lax.axis_size("block")))
    active, move_rank = arrival_ranks(move_slot, move_dest)
    own_slots = move_slot[own_index]
    own_dests = move_dest[own_index]
    own_active = active[own_index]
    own_rank = move_rank[own_index]
    peer_ids = jnp.arange(walker_total)
    place_ids = jnp.arange(capacity)
    chosen = (
        (own_dests[None, None, :] == peer_ids[:, None, None])
        & (own_rank[None, None, :] == place_ids[None, :, None])
        & own_active[None, None, :]
    )
    send_slot = jnp.sum(jnp.where(chosen, own_slots[None, None, :], 0), axis=2).reshape(-1)
    present = jnp.any(chosen, axis=2).reshape(-1)
    arrive = jnp.any(
        (move_dest[:, None, :] == own_index)
        & (move_rank[:, None, :] == place_ids[None, :, None])
        & active[:, None, :],
        axis=2,
    ).reshape(-1)
    slot_ids = jnp.arange(slot_total)
    occupied = slot_ids < counts[own_index]
    leaving = jnp.any(own_slots[:, None] == slot_ids[None, :], axis=0)
    staying = occupied & jnp.logical_not(leaving)
    stay_rank = jnp.cumsum(staying.astype(jnp.int32)) - 1
    arrive_rank = jnp.cumsum(arrive.astype(jnp.int32)) - 1
    stay_total = jnp.sum(staying.astype(jnp.int32))
    targets = jnp.arange(keep_total)
    from_stay = jnp.sum(
        jnp.where(
            staying[None, :] & (stay_rank[None, :] == targets[:, None]), slot_ids[None, :], 0
        ),
        axis=1,
    )
    arrive_ids = jnp.arange(arrive.shape[0]) + slot_total
    from_arrive = jnp.sum(
        jnp.where(
            arrive[None, :] & (arrive_rank[None, :] == (targets - stay_total)[:, None]),
            arrive_ids[None, :],
            0,
        ),
        axis=1,
    )
    source_row = jnp.where(targets < stay_total, from_stay, from_arrive)
    outgoing = jnp.where(
        present[:, None], jnp.take(green, send_slot, axis=0), jnp.zeros((), jnp.bfloat16)
    )
    outgoing = outgoing.reshape(walker_total, capacity, share_width)

    def walker_energy(walker_row):
        green_mat = walker_row.reshape(occ_count, orb_count)
        transfer = jnp.einsum("gip,jp->gij", chol, green_mat, preferred_element_type=jnp.float32)
        return jnp.sum(transfer * jnp.swapaxes(transfer, 1, 2))

    got_rows = lax.all_to_all(outgoing, "walker", split_axis=0, concat_axis=0, tiled=True)
    source_pool = jnp.concatenate([green, got_rows.reshape(-1, share_width)], axis=0)
    new_green = jnp.take(source_pool, source_row, axis=0)
    complete = lax.all_gather(new_green, "block", axis=1, tiled=True)
    partial_value = lax.map(walker_energy, complete)
    energy = -energy_scale * lax.psum(partial_value, "block")
    return (new_green, energy)


LANES = 128
ROWS = 8


def spread_slots(green_ref, spread, share_rows):
    slots = green_ref.shape[0]
    tiles = spread.shape[0]
    for row in range(share_rows):
        for tile in range(tiles):
            col = (row * tiles + tile) * LANES
            block = green_ref[:, col : col + LANES].astype(jnp.float32)
            spread[tile, row * ROWS : row * ROWS + slots, :] = block


def pack_kernel(dims, green_ref, own_ref, spread):
    slots, share_rows, orb_count = dims
    spread_slots(green_ref, spread, share_rows)
    for tile in range(orb_count // LANES):
        dense = [spread[tile, pl.ds(slot, share_rows, stride=ROWS), :] for slot in range(slots)]
        packed = jnp.concatenate(dense, axis=0).astype(jnp.bfloat16)
        own_ref[:, tile * LANES : (tile + 1) * LANES] = packed


class Moves:
    def __init__(self, table_ref, moves):
        self.table, self.moves = table_ref, moves

    def count(self, device):
        return self.table[0, device]

    def slot(self, device, move):
        return self.table[1 + move, device]

    def dest(self, device, move):
        return self.table[1 + self.moves + move, device]

    def staying(self, device):
        total = self.count(device)
        for move in range(self.moves):
            total = total - jnp.where(self.slot(device, move) >= 0, 1, 0)
        return total

    def goes_to(self, own, slot):
        target = jnp.int32(-1)
        for move in range(self.moves):
            target = jnp.where(self.slot(own, move) == slot, self.dest(own, move), target)
        return target


def leave_kernel(dims, ident_ref, table_ref, own_ref, *refs):
    slots, share_rows, orb_count, walkers, moves, keep = dims
    leave_refs, place_ref, wide = refs[:-2], refs[-2], refs[-1]
    table = Moves(table_ref, moves)
    wide[...] = own_ref[...].astype(jnp.float32)
    own = ident_ref[0]
    for shift in range(1, walkers):
        target = lax.rem(own + shift, walkers)
        chosen = jnp.int32(0)
        for move in range(moves):
            hit = (table.dest(own, move) == target) & (table.slot(own, move) >= 0)
            chosen = jnp.where(hit, table.slot(own, move), chosen)
        start = pl.multiple_of(chosen * share_rows, ROWS)
        leave_refs[shift - 1][...] = wide[pl.ds(start, share_rows), :].astype(jnp.bfloat16)
    rank = jnp.int32(0)
    for slot in range(slots):
        live = slot < table.count(own)
        gone_to = table.goes_to(own, slot)
        stays = live & (gone_to < 0)
        there = jnp.maximum(gone_to, 0)
        ahead = table.staying(there)
        for device in range(walkers):
            for move in range(moves):
                hit = (
                    (device < own)
                    & (table.dest(device, move) == there)
                    & (table.slot(device, move) >= 0)
                )
                ahead = ahead + jnp.where(hit, 1, 0)
        place = jnp.where(stays, own * keep + rank, there * keep + ahead)
        place_ref[slot] = jnp.where(live, place, -1)
        rank = rank + jnp.where(stays, 1, 0)


def assemble_kernel(dims, ident_ref, table_ref, green_ref, *refs):
    slots, share_rows, orb_count, walkers, moves, keep = dims
    table = Moves(table_ref, moves)
    come_refs = refs[: walkers - 1]
    new_ref, spread, pool, out = refs[walkers - 1 :]
    own = ident_ref[0]
    tiles = orb_count // LANES
    spread_slots(green_ref, spread, share_rows)
    for slot in range(slots):
        for tile in range(tiles):
            pool[
                slot * share_rows : (slot + 1) * share_rows, tile * LANES : (tile + 1) * LANES
            ] = spread[tile, pl.ds(slot, share_rows, stride=ROWS), :]
    for shift in range(1, walkers):
        start = (slots + shift - 1) * share_rows
        pool[start : start + share_rows, :] = come_refs[shift - 1][...].astype(jnp.float32)

    sources = [jnp.int32(0)] * keep
    rank = jnp.int32(0)
    for slot in range(slots):
        stays = (slot < table.count(own)) & (table.goes_to(own, slot) < 0)
        for target in range(keep):
            sources[target] = jnp.where(stays & (rank == target), slot, sources[target])
        rank = rank + jnp.where(stays, 1, 0)
    for device in range(walkers):
        comes = jnp.bool_(False)
        for move in range(moves):
            comes = comes | ((table.dest(device, move) == own) & (table.slot(device, move) >= 0))
        comes = comes & (device != own)
        shift = lax.rem(own - device + walkers, walkers)
        for target in range(keep):
            sources[target] = jnp.where(
                comes & (rank == target), slots + shift - 1, sources[target]
            )
        rank = rank + jnp.where(comes, 1, 0)
    for target in range(keep):
        start = pl.multiple_of(sources[target] * share_rows, ROWS)
        for tile in range(tiles):
            out[tile, pl.ds(target, share_rows, stride=ROWS), :] = pool[
                pl.ds(start, share_rows), tile * LANES : (tile + 1) * LANES
            ]
    for row in range(share_rows):
        for tile in range(tiles):
            col = (row * tiles + tile) * LANES
            new_ref[:, col : col + LANES] = out[
                tile, row * ROWS : row * ROWS + keep, :
            ].astype(jnp.bfloat16)


def order_kernel(dims, ident_ref, chol_ref, own_ref, out_ref, sems):
    del own_ref
    group, groups, chip_rows = dims
    chip = ident_ref[0] // 2
    edge = LANES - 2 * chip_rows
    rest = 2 * chip_rows - edge
    copies = []

    def add(vec, distance, start, size, place):
        row = pl.multiple_of(jnp.bitwise_xor(chip, distance) * chip_rows + start, 16)
        copies.append(
            pltpu.make_async_copy(
                chol_ref.at[vec, pl.ds(row, size), :],
                out_ref.at[pl.ds(place, size), :],
                sems.at[len(copies)],
            )
        )

    for index in range(groups):
        for item in range(group):
            vec = index * group + item
            place = index * group * 4 * chip_rows + item * LANES
            add(vec, 0, 0, chip_rows, place)
            add(vec, 1, 0, chip_rows, place + chip_rows)
            add(vec, 2, 0, edge, place + 2 * chip_rows)
            place = index * group * 4 * chip_rows + group * LANES + item * rest
            add(vec, 2, edge, chip_rows - edge, place)
            add(vec, 3, 0, chip_rows, place + chip_rows - edge)
    for copy in copies:
        copy.start()
    for copy in copies:
        copy.wait()


def padded(rows):
    return -(-rows // 16) * 16


def stacked(refs):
    values = []
    for ref in refs:
        rows, width = ref.shape
        values.append(ref[...])
        if padded(rows) > rows:
            values.append(jnp.zeros((padded(rows) - rows, width), jnp.bfloat16))
    return jnp.concatenate(values, axis=0)


def times(left, right):
    return lax.dot_general(
        left, right, (((1,), (1,)), ((), ())), preferred_element_type=jnp.float32
    )


def near_kernel(dims, ident_ref, weight_ref, *refs):
    slots, share_rows, group, groups, chip_rows = dims
    own_ref, core_ref, x_ref, y_ref, turned_ref = refs[:5]
    piece_refs = [own_ref, core_ref, x_ref, turned_ref.at[0], y_ref, turned_ref.at[1]]
    sum_ref, late_ref = refs[5:7]
    trans_refs = refs[7:]
    own = ident_ref[0]
    core = lax.rem(own, 2)
    pad_rows = padded(piece_refs[0].shape[0])
    near = 3 * chip_rows
    size = 4 * chip_rows * group
    edge = near - LANES
    half = LANES // 2
    left = stacked(piece_refs)
    lane = lax.broadcasted_iota(jnp.int32, (1, LANES), 1)
    low_half = lane < half
    in_edge = jnp.where(low_half, lane, lane - half) < edge
    sums = [jnp.zeros((ROWS, LANES), jnp.float32) for _ in range(slots)]

    def fold(value):
        return jnp.sum(value.reshape(-1, ROWS, LANES), axis=0)

    for index in range(groups):
        trans = trans_refs[index]
        result = times(left, weight_ref[index * size : (index + 1) * size, :])
        for piece in range(6):
            source = jnp.bitwise_xor(core, piece % 2)
            for slot in range(slots):
                start = piece * pad_rows + slot * share_rows
                place = slot * near + (piece // 2) * chip_rows + source * share_rows
                trans[pl.ds(pl.multiple_of(place, ROWS), share_rows), :] = result[
                    start : start + share_rows, :
                ]
        for slot in range(slots):
            base = slot * near
            late = slice(slot * chip_rows, (slot + 1) * chip_rows)
            acc = sums[slot]
            for pair in range(group // 2):
                col = (group + pair) * LANES
                top = trans[base : base + LANES, col : col + LANES].T
                edge_rows = trans[base + LANES : base + near, col : col + LANES]
                gap = jnp.zeros((half - edge, LANES), jnp.float32)
                bottom = jnp.concatenate([edge_rows, gap, edge_rows, gap], axis=0).T
                for side in range(2):
                    vec = 2 * pair + side
                    high = trans[base : base + LANES, vec * LANES : (vec + 1) * LANES]
                    acc = acc + fold(high * high.T)
                    across = trans[base + LANES : base + near, vec * LANES : (vec + 1) * LANES]
                    acc = acc + 2.0 * fold(across * top[side * half : side * half + edge, :])
                    late_ref[
                        late, (index * (group + group // 2) + vec) * LANES : (
                            index * (group + group // 2) + vec + 1
                        ) * LANES
                    ] = top[side * half + edge : (side + 1) * half, :]
                corner = jnp.where(low_half, bottom[:edge, :], bottom[half : half + edge, :])
                acc = acc + fold(jnp.where(in_edge, edge_rows * corner, 0.0))
                rest = jnp.where(low_half, bottom[edge:half, :], bottom[half + edge :, :])
                place = (index * (group + group // 2) + group + pair) * LANES
                late_ref[late, place : place + LANES] = jnp.where(in_edge, rest, 0.0)
            sums[slot] = acc
    sum_ref[...] = jnp.concatenate(sums, axis=0)


def far_kernel(dims, ident_ref, place_ref, weight_ref, near_sum_ref, late_ref, *refs):
    slots, share_rows, group, groups, chip_rows = dims
    here_ref, there_ref, sum_ref = refs[:3]
    trans_refs = refs[3:]
    own = ident_ref[0]
    core = lax.rem(own, 2)
    _, pack_rows, width = here_ref.shape
    pad_rows = padded(pack_rows)
    half = LANES // 2
    edge = half - chip_rows
    size = 4 * chip_rows * group
    lane = lax.broadcasted_iota(jnp.int32, (1, LANES), 1)
    low_half = lane < half
    in_rest = jnp.where(low_half, lane, lane - half) >= edge
    lefts = [stacked([here_ref.at[part], there_ref.at[part]]) for part in range(2)]
    twice = [jnp.zeros((ROWS, LANES), jnp.float32) for _ in range(slots)]
    once = [near_sum_ref[slot * ROWS : (slot + 1) * ROWS, :] for slot in range(slots)]

    def fold(value):
        return jnp.sum(value.reshape(-1, ROWS, LANES), axis=0)

    tiles = group + group // 2
    for index in range(groups):
        trans = trans_refs[index]
        rows = slice(index * size, (index + 1) * size)
        result = times(lefts[0], weight_ref[rows, :width])
        result = result + times(lefts[1], weight_ref[rows, width:])
        for piece in range(2):
            source = jnp.bitwise_xor(core, piece)
            for slot in range(slots):
                start = piece * pad_rows + slot * share_rows
                place = slot * chip_rows + source * share_rows
                trans[pl.ds(pl.multiple_of(place, ROWS), share_rows), :] = result[
                    start : start + share_rows, :
                ]
        for slot in range(slots):
            rows = slice(slot * chip_rows, (slot + 1) * chip_rows)
            for tile in range(tiles):
                here = trans[rows, tile * LANES : (tile + 1) * LANES]
                met = late_ref[rows, (index * tiles + tile) * LANES : (index * tiles + tile + 1) * LANES]
                twice[slot] = twice[slot] + fold(here * met)
                if tile >= group:
                    gap = jnp.zeros((edge, LANES), jnp.float32)
                    turned = jnp.concatenate([gap, here, gap, here], axis=0).T
                    corner = jnp.where(low_half, turned[edge:half, :], turned[half + edge :, :])
                    once[slot] = once[slot] + fold(jnp.where(in_rest, here * corner, 0.0))
    value = jnp.zeros((1, LANES), jnp.float32)
    for slot in range(slots):
        slot_sum = jnp.sum(once[slot] + 2.0 * twice[slot])
        value = jnp.where(lane == place_ref[slot], slot_sum, value)
    sum_ref[...] = jnp.broadcast_to(value, sum_ref.shape)


def swap(value, mask, blocks):
    return lax.ppermute(value, "block", [(index, index ^ mask) for index in range(blocks)])


def pair_kernel(one_ref, two_ref, out_ref):
    out_ref[0] = one_ref[...]
    out_ref[1] = two_ref[...]


def pair(one, two):
    vmem = pl.BlockSpec(memory_space=pltpu.VMEM)
    return pl.pallas_call(
        pair_kernel,
        out_shape=jax.ShapeDtypeStruct((2, *one.shape), one.dtype),
        in_specs=[vmem] * 2,
        out_specs=vmem,
        compiler_params=pltpu.CompilerParams(vmem_limit_bytes=16 * 1024 * 1024),
        name="pair",
    )(one, two)


def body(green, chol, counts, move_slot, move_dest):
    walkers = lax.axis_size("walker")
    blocks = lax.axis_size("block")
    slots, share_width = green.shape
    vectors, occ_count, orb_count = chol.shape
    moves = move_slot.shape[1]
    keep = slots - moves
    share_rows = share_width // orb_count
    pack_rows = slots * share_rows
    table = jnp.concatenate([counts[None, :], move_slot.T, move_dest.T], axis=0)
    walker_index = lax.axis_index("walker").astype(jnp.int32).reshape(1)
    block_index = lax.axis_index("block").astype(jnp.int32).reshape(1)
    smem = pl.BlockSpec(memory_space=pltpu.SMEM)
    vmem = pl.BlockSpec(memory_space=pltpu.VMEM)
    limit = pltpu.CompilerParams(vmem_limit_bytes=32 * 1024 * 1024)

    spread = pltpu.VMEM((orb_count // LANES, share_rows * ROWS, LANES), jnp.float32)
    own_rows = pl.pallas_call(
        functools.partial(pack_kernel, (slots, share_rows, orb_count)),
        out_shape=jax.ShapeDtypeStruct((pack_rows, orb_count), jnp.bfloat16),
        in_specs=[vmem],
        out_specs=vmem,
        scratch_shapes=[spread],
        compiler_params=limit,
        name="pack",
    )(green)
    move_dims = (slots, share_rows, orb_count, walkers, moves, keep)
    *leaving, place = pl.pallas_call(
        functools.partial(leave_kernel, move_dims),
        out_shape=[jax.ShapeDtypeStruct((share_rows, orb_count), jnp.bfloat16)] * (walkers - 1)
        + [jax.ShapeDtypeStruct((slots,), jnp.int32)],
        in_specs=[smem, smem, vmem],
        out_specs=[vmem] * (walkers - 1) + [smem],
        scratch_shapes=[pltpu.VMEM((pack_rows, orb_count), jnp.float32)],
        compiler_params=limit,
        name="leave",
    )(walker_index, table, own_rows)
    coming = [
        lax.ppermute(
            leaving[shift - 1], "walker", [(z, (z + shift) % walkers) for z in range(walkers)]
        )
        for shift in range(1, walkers)
    ]

    group = 4
    groups = vectors // group
    chip_rows = 2 * share_rows
    weights = pl.pallas_call(
        functools.partial(order_kernel, (group, groups, chip_rows)),
        out_shape=jax.ShapeDtypeStruct((vectors * occ_count, orb_count), jnp.bfloat16),
        in_specs=[smem] + [pl.BlockSpec(memory_space=pl.ANY)] * 2,
        out_specs=vmem,
        scratch_shapes=[pltpu.SemaphoreType.DMA((5 * vectors,))],
        compiler_params=pltpu.CompilerParams(vmem_limit_bytes=48 * 1024 * 1024),
        cost_estimate=pl.CostEstimate(
            flops=0, bytes_accessed=4 * chol.size, transcendentals=0
        ),
        name="order",
    )(block_index, chol, own_rows)

    core, near_x, near_y = 1, 2, 4
    from_x = swap(own_rows, near_x, blocks)
    from_y = swap(own_rows, near_y, blocks)
    from_core = swap(own_rows, core, blocks)
    width = orb_count // 2
    from_x, from_y, from_core, weights, coming[:1] = lax.optimization_barrier(
        (from_x, from_y, from_core, weights, coming[:1])
    )
    far = [swap(from_y[:, :width], near_x, blocks), swap(from_x[:, width:], near_y, blocks)]
    turned = swap(pair(from_x, from_y), core, blocks)
    near_pieces = [own_rows, from_core, from_x, from_y, turned]

    dims = (slots, share_rows, group, groups, chip_rows)
    work = 2 * vectors * occ_count * orb_count * pack_rows
    near_sums, late = pl.pallas_call(
        functools.partial(near_kernel, dims),
        out_shape=[
            jax.ShapeDtypeStruct((slots * ROWS, LANES), jnp.float32),
            jax.ShapeDtypeStruct((slots * chip_rows, vectors * occ_count), jnp.float32),
        ],
        in_specs=[smem] + [vmem] * 6,
        out_specs=[vmem] * 2,
        scratch_shapes=[pltpu.VMEM((slots * 3 * chip_rows, group * occ_count), jnp.float32)]
        * groups,
        compiler_params=limit,
        cost_estimate=pl.CostEstimate(
            flops=6 * work, bytes_accessed=2 * chol.size, transcendentals=0
        ),
        name="near",
    )(block_index, weights, *near_pieces)
    far, near_sums = lax.optimization_barrier((far, near_sums))
    here = pair(*far)
    far_pieces = [here, swap(here, core, blocks)]
    all_sums = pl.pallas_call(
        functools.partial(far_kernel, dims),
        out_shape=jax.ShapeDtypeStruct((blocks * walkers, LANES), jnp.float32),
        in_specs=[smem] * 2 + [vmem] * 5,
        out_specs=vmem,
        scratch_shapes=[pltpu.VMEM((slots * chip_rows, group * occ_count), jnp.float32)] * groups,
        compiler_params=limit,
        cost_estimate=pl.CostEstimate(
            flops=2 * work, bytes_accessed=2 * chol.size, transcendentals=0
        ),
        name="far",
    )(block_index, place, weights, near_sums, late, *far_pieces)

    coming, _ = lax.optimization_barrier((coming, all_sums))
    new_green = pl.pallas_call(
        functools.partial(assemble_kernel, move_dims),
        out_shape=jax.ShapeDtypeStruct((keep, share_width), jnp.bfloat16),
        in_specs=[smem] * 2 + [vmem] * walkers,
        out_specs=vmem,
        scratch_shapes=[
            pltpu.VMEM((orb_count // LANES, share_rows * ROWS, LANES), jnp.float32),
            pltpu.VMEM(((slots + walkers - 1) * share_rows, orb_count), jnp.float32),
            pltpu.VMEM((orb_count // LANES, share_rows * ROWS, LANES), jnp.float32),
        ],
        compiler_params=limit,
        name="assemble",
    )(walker_index, table, green, *coming)

    energy_scale = 0.5 / (occ_count * math.sqrt(vectors * blocks))
    got = lax.all_to_all(
        all_sums, ("block", "walker"), split_axis=0, concat_axis=0, tiled=True
    )
    got_sums = jnp.sum(got, axis=0)
    own_sums = lax.dynamic_slice(got_sums, (walker_index[0] * keep,), (keep,))
    return (new_green, -energy_scale * own_sums)


def fits(mesh):
    blocks = mesh.shape["block"]
    walkers = mesh.shape["walker"]

    def check(green, chol, counts, move_slot, move_dest):
        vectors, occ_count, orb_count = chol.shape
        share_width = green.shape[1] // blocks
        moves = move_slot.shape[1]
        slots = green.shape[0] // walkers
        return (
            blocks == 8
            and walkers >= 2
            and walkers & (walkers - 1) == 0
            and (moves + walkers - 2) // (walkers - 1) == 1
            and slots <= ROWS
            and share_width % (orb_count * ROWS) == 0
            and orb_count % (2 * LANES) == 0
            and occ_count == blocks * (share_width // orb_count)
            and occ_count == LANES + LANES // 2
            and (vectors // blocks) % 4 == 0
            and walkers * (slots - moves) <= LANES
        )

    return check


def solution(mesh):
    in_specs = (P("walker", "block"), P("block", None, None), P(), P(), P())
    out_specs = (P("walker", "block"), P("walker"))
    check = fits(mesh)

    def run(*args):
        chosen = body if check(*args) else general_body
        return jax.shard_map(
            chosen, mesh=mesh, in_specs=in_specs, out_specs=out_specs, check_vma=False
        )(*args)

    return run
```

```python
import functools
import math

import jax
import jax.numpy as jnp
from jax import lax
from jax.experimental import pallas as pl
from jax.experimental.pallas import tpu as pltpu
from jax.sharding import PartitionSpec as P


def arrival_ranks(move_slot, move_dest):
    active = move_slot >= 0
    move_total = move_slot.shape[1]
    earlier = jnp.arange(move_total)[None, :] < jnp.arange(move_total)[:, None]
    same_target = (
        (move_dest[:, :, None] == move_dest[:, None, :]) & earlier[None, :, :] & active[:, None, :]
    )
    return (active, jnp.sum(same_target.astype(jnp.int32), axis=2))


def general_body(green, chol, counts, move_slot, move_dest):
    walker_total = lax.axis_size("walker")
    own_index = lax.axis_index("walker")
    slot_total = green.shape[0]
    share_width = green.shape[1]
    keep_total = slot_total - move_slot.shape[1]
    capacity = (move_slot.shape[1] + walker_total - 2) // (walker_total - 1)
    occ_count = chol.shape[1]
    orb_count = chol.shape[2]
    energy_scale = 0.5 / (occ_count * math.sqrt(chol.shape[0] * lax.axis_size("block")))
    active, move_rank = arrival_ranks(move_slot, move_dest)
    own_slots = move_slot[own_index]
    own_dests = move_dest[own_index]
    own_active = active[own_index]
    own_rank = move_rank[own_index]
    peer_ids = jnp.arange(walker_total)
    place_ids = jnp.arange(capacity)
    chosen = (
        (own_dests[None, None, :] == peer_ids[:, None, None])
        & (own_rank[None, None, :] == place_ids[None, :, None])
        & own_active[None, None, :]
    )
    send_slot = jnp.sum(jnp.where(chosen, own_slots[None, None, :], 0), axis=2).reshape(-1)
    present = jnp.any(chosen, axis=2).reshape(-1)
    arrive = jnp.any(
        (move_dest[:, None, :] == own_index)
        & (move_rank[:, None, :] == place_ids[None, :, None])
        & active[:, None, :],
        axis=2,
    ).reshape(-1)
    slot_ids = jnp.arange(slot_total)
    occupied = slot_ids < counts[own_index]
    leaving = jnp.any(own_slots[:, None] == slot_ids[None, :], axis=0)
    staying = occupied & jnp.logical_not(leaving)
    stay_rank = jnp.cumsum(staying.astype(jnp.int32)) - 1
    arrive_rank = jnp.cumsum(arrive.astype(jnp.int32)) - 1
    stay_total = jnp.sum(staying.astype(jnp.int32))
    targets = jnp.arange(keep_total)
    from_stay = jnp.sum(
        jnp.where(
            staying[None, :] & (stay_rank[None, :] == targets[:, None]), slot_ids[None, :], 0
        ),
        axis=1,
    )
    arrive_ids = jnp.arange(arrive.shape[0]) + slot_total
    from_arrive = jnp.sum(
        jnp.where(
            arrive[None, :] & (arrive_rank[None, :] == (targets - stay_total)[:, None]),
            arrive_ids[None, :],
            0,
        ),
        axis=1,
    )
    source_row = jnp.where(targets < stay_total, from_stay, from_arrive)
    outgoing = jnp.where(
        present[:, None], jnp.take(green, send_slot, axis=0), jnp.zeros((), jnp.bfloat16)
    )
    outgoing = outgoing.reshape(walker_total, capacity, share_width)

    def walker_energy(walker_row):
        green_mat = walker_row.reshape(occ_count, orb_count)
        transfer = jnp.einsum("gip,jp->gij", chol, green_mat, preferred_element_type=jnp.float32)
        return jnp.sum(transfer * jnp.swapaxes(transfer, 1, 2))

    got_rows = lax.all_to_all(outgoing, "walker", split_axis=0, concat_axis=0, tiled=True)
    source_pool = jnp.concatenate([green, got_rows.reshape(-1, share_width)], axis=0)
    new_green = jnp.take(source_pool, source_row, axis=0)
    complete = lax.all_gather(new_green, "block", axis=1, tiled=True)
    partial_value = lax.map(walker_energy, complete)
    energy = -energy_scale * lax.psum(partial_value, "block")
    return (new_green, energy)


LANES = 128
ROWS = 8


def spread_slots(green_ref, spread, share_rows):
    slots = green_ref.shape[0]
    tiles = spread.shape[0]
    for row in range(share_rows):
        for tile in range(tiles):
            col = (row * tiles + tile) * LANES
            block = green_ref[:, col : col + LANES].astype(jnp.float32)
            spread[tile, row * ROWS : row * ROWS + slots, :] = block


def pack_kernel(dims, green_ref, own_ref, spread):
    slots, share_rows, orb_count = dims
    spread_slots(green_ref, spread, share_rows)
    for tile in range(orb_count // LANES):
        dense = [spread[tile, pl.ds(slot, share_rows, stride=ROWS), :] for slot in range(slots)]
        packed = jnp.concatenate(dense, axis=0).astype(jnp.bfloat16)
        own_ref[:, tile * LANES : (tile + 1) * LANES] = packed


class Moves:
    def __init__(self, table_ref, moves):
        self.table, self.moves = table_ref, moves

    def count(self, device):
        return self.table[0, device]

    def slot(self, device, move):
        return self.table[1 + move, device]

    def dest(self, device, move):
        return self.table[1 + self.moves + move, device]

    def staying(self, device):
        total = self.count(device)
        for move in range(self.moves):
            total = total - jnp.where(self.slot(device, move) >= 0, 1, 0)
        return total

    def goes_to(self, own, slot):
        target = jnp.int32(-1)
        for move in range(self.moves):
            target = jnp.where(self.slot(own, move) == slot, self.dest(own, move), target)
        return target


def leave_kernel(dims, ident_ref, table_ref, own_ref, *refs):
    slots, share_rows, orb_count, walkers, moves, keep = dims
    leave_refs, wide = refs[:-1], refs[-1]
    table = Moves(table_ref, moves)
    wide[...] = own_ref[...].astype(jnp.float32)
    own = ident_ref[0]
    for shift in range(1, walkers):
        target = lax.rem(own + shift, walkers)
        chosen = jnp.int32(0)
        for move in range(moves):
            hit = (table.dest(own, move) == target) & (table.slot(own, move) >= 0)
            chosen = jnp.where(hit, table.slot(own, move), chosen)
        start = pl.multiple_of(chosen * share_rows, ROWS)
        leave_refs[shift - 1][...] = wide[pl.ds(start, share_rows), :].astype(jnp.bfloat16)


def assemble_kernel(dims, ident_ref, table_ref, green_ref, *refs):
    slots, share_rows, orb_count, walkers, moves, keep = dims
    table = Moves(table_ref, moves)
    come_refs = refs[: walkers - 1]
    new_ref, spread, pool, out = refs[walkers - 1 :]
    own = ident_ref[0]
    tiles = orb_count // LANES
    spread_slots(green_ref, spread, share_rows)
    for slot in range(slots):
        for tile in range(tiles):
            pool[
                slot * share_rows : (slot + 1) * share_rows, tile * LANES : (tile + 1) * LANES
            ] = spread[tile, pl.ds(slot, share_rows, stride=ROWS), :]
    for shift in range(1, walkers):
        start = (slots + shift - 1) * share_rows
        pool[start : start + share_rows, :] = come_refs[shift - 1][...].astype(jnp.float32)

    sources = [jnp.int32(0)] * keep
    rank = jnp.int32(0)
    for slot in range(slots):
        stays = (slot < table.count(own)) & (table.goes_to(own, slot) < 0)
        for target in range(keep):
            sources[target] = jnp.where(stays & (rank == target), slot, sources[target])
        rank = rank + jnp.where(stays, 1, 0)
    for device in range(walkers):
        comes = jnp.bool_(False)
        for move in range(moves):
            comes = comes | ((table.dest(device, move) == own) & (table.slot(device, move) >= 0))
        comes = comes & (device != own)
        shift = lax.rem(own - device + walkers, walkers)
        for target in range(keep):
            sources[target] = jnp.where(
                comes & (rank == target), slots + shift - 1, sources[target]
            )
        rank = rank + jnp.where(comes, 1, 0)
    for target in range(keep):
        start = pl.multiple_of(sources[target] * share_rows, ROWS)
        for tile in range(tiles):
            out[tile, pl.ds(target, share_rows, stride=ROWS), :] = pool[
                pl.ds(start, share_rows), tile * LANES : (tile + 1) * LANES
            ]
    for row in range(share_rows):
        for tile in range(tiles):
            col = (row * tiles + tile) * LANES
            new_ref[:, col : col + LANES] = out[
                tile, row * ROWS : row * ROWS + keep, :
            ].astype(jnp.bfloat16)


def find_places(dims, own, table, place_ref):
    slots, walkers, moves, keep = dims
    rank = jnp.int32(0)
    for slot in range(slots):
        live = slot < table.count(own)
        gone_to = table.goes_to(own, slot)
        stays = live & (gone_to < 0)
        there = jnp.maximum(gone_to, 0)
        ahead = table.staying(there)
        for device in range(walkers):
            for move in range(moves):
                hit = (
                    (device < own)
                    & (table.dest(device, move) == there)
                    & (table.slot(device, move) >= 0)
                )
                ahead = ahead + jnp.where(hit, 1, 0)
        place = jnp.where(stays, own * keep + rank, there * keep + ahead)
        place_ref[slot] = jnp.where(live, place, -1)
        rank = rank + jnp.where(stays, 1, 0)


def order_kernel(dims, ident_ref, chol_ref, own_ref, out_ref, sems):
    del own_ref
    group, groups, chip_rows = dims
    chip = ident_ref[0] // 2
    edge = LANES - 2 * chip_rows
    rest = 2 * chip_rows - edge
    copies = []

    def add(vec, distance, start, size, place):
        row = pl.multiple_of(jnp.bitwise_xor(chip, distance) * chip_rows + start, 16)
        copies.append(
            pltpu.make_async_copy(
                chol_ref.at[vec, pl.ds(row, size), :],
                out_ref.at[pl.ds(place, size), :],
                sems.at[len(copies)],
            )
        )

    for index in range(groups):
        for item in range(group):
            vec = index * group + item
            place = index * group * 4 * chip_rows + item * LANES
            add(vec, 0, 0, chip_rows, place)
            add(vec, 1, 0, chip_rows, place + chip_rows)
            add(vec, 2, 0, edge, place + 2 * chip_rows)
            place = index * group * 4 * chip_rows + group * LANES + item * rest
            add(vec, 2, edge, chip_rows - edge, place)
            add(vec, 3, 0, chip_rows, place + chip_rows - edge)
    for copy in copies:
        copy.start()
    for copy in copies:
        copy.wait()


def padded(rows):
    return -(-rows // 16) * 16


def stacked(refs):
    values = []
    for ref in refs:
        rows, width = ref.shape
        values.append(ref[...])
        if padded(rows) > rows:
            values.append(jnp.zeros((padded(rows) - rows, width), jnp.bfloat16))
    return jnp.concatenate(values, axis=0)


def times(left, right):
    return lax.dot_general(
        left, right, (((1,), (1,)), ((), ())), preferred_element_type=jnp.float32
    )


def near_kernel(dims, place_dims, ident_ref, walker_ref, table_ref, weight_ref, *refs):
    slots, share_rows, group, groups, chip_rows = dims
    piece_refs = refs[:6]
    sum_ref, late_ref, place_ref = refs[6:9]
    trans_refs = refs[9:]
    find_places(place_dims, walker_ref[0], Moves(table_ref, place_dims[2]), place_ref)
    own = ident_ref[0]
    core = lax.rem(own, 2)
    pad_rows = padded(piece_refs[0].shape[0])
    near = 3 * chip_rows
    size = 4 * chip_rows * group
    edge = near - LANES
    half = LANES // 2
    left = stacked(piece_refs)
    lane = lax.broadcasted_iota(jnp.int32, (1, LANES), 1)
    low_half = lane < half
    in_edge = jnp.where(low_half, lane, lane - half) < edge
    sums = [jnp.zeros((ROWS, LANES), jnp.float32) for _ in range(slots)]

    def fold(value):
        return jnp.sum(value.reshape(-1, ROWS, LANES), axis=0)

    for index in range(groups):
        trans = trans_refs[index]
        result = times(left, weight_ref[index * size : (index + 1) * size, :])
        for piece in range(6):
            source = jnp.bitwise_xor(core, piece % 2)
            for slot in range(slots):
                start = piece * pad_rows + slot * share_rows
                place = slot * near + (piece // 2) * chip_rows + source * share_rows
                trans[pl.ds(pl.multiple_of(place, ROWS), share_rows), :] = result[
                    start : start + share_rows, :
                ]
        for slot in range(slots):
            base = slot * near
            late = slice(slot * chip_rows, (slot + 1) * chip_rows)
            acc = sums[slot]
            for pair in range(group // 2):
                col = (group + pair) * LANES
                top = trans[base : base + LANES, col : col + LANES].T
                edge_rows = trans[base + LANES : base + near, col : col + LANES]
                gap = jnp.zeros((half - edge, LANES), jnp.float32)
                bottom = jnp.concatenate([edge_rows, gap, edge_rows, gap], axis=0).T
                for side in range(2):
                    vec = 2 * pair + side
                    high = trans[base : base + LANES, vec * LANES : (vec + 1) * LANES]
                    acc = acc + fold(high * high.T)
                    across = trans[base + LANES : base + near, vec * LANES : (vec + 1) * LANES]
                    acc = acc + 2.0 * fold(across * top[side * half : side * half + edge, :])
                    late_ref[
                        late, (index * (group + group // 2) + vec) * LANES : (
                            index * (group + group // 2) + vec + 1
                        ) * LANES
                    ] = top[side * half + edge : (side + 1) * half, :]
                corner = jnp.where(low_half, bottom[:edge, :], bottom[half : half + edge, :])
                acc = acc + fold(jnp.where(in_edge, edge_rows * corner, 0.0))
                rest = jnp.where(low_half, bottom[edge:half, :], bottom[half + edge :, :])
                place = (index * (group + group // 2) + group + pair) * LANES
                late_ref[late, place : place + LANES] = jnp.where(in_edge, rest, 0.0)
            sums[slot] = acc
    sum_ref[...] = jnp.concatenate(sums, axis=0)


def far_kernel(dims, ident_ref, place_ref, weight_ref, near_sum_ref, late_ref, *refs):
    slots, share_rows, group, groups, chip_rows = dims
    piece_refs = refs[:4]
    sum_ref = refs[4]
    trans_refs = refs[5:]
    own = ident_ref[0]
    core = lax.rem(own, 2)
    pack_rows, width = piece_refs[0].shape
    pad_rows = padded(pack_rows)
    half = LANES // 2
    edge = half - chip_rows
    size = 4 * chip_rows * group
    lane = lax.broadcasted_iota(jnp.int32, (1, LANES), 1)
    low_half = lane < half
    in_rest = jnp.where(low_half, lane, lane - half) >= edge
    lefts = [stacked(piece_refs[part::2]) for part in range(2)]
    twice = [jnp.zeros((ROWS, LANES), jnp.float32) for _ in range(slots)]
    once = [near_sum_ref[slot * ROWS : (slot + 1) * ROWS, :] for slot in range(slots)]

    def fold(value):
        return jnp.sum(value.reshape(-1, ROWS, LANES), axis=0)

    tiles = group + group // 2
    for index in range(groups):
        trans = trans_refs[index]
        rows = slice(index * size, (index + 1) * size)
        result = times(lefts[0], weight_ref[rows, :width])
        result = result + times(lefts[1], weight_ref[rows, width:])
        for piece in range(2):
            source = jnp.bitwise_xor(core, piece)
            for slot in range(slots):
                start = piece * pad_rows + slot * share_rows
                place = slot * chip_rows + source * share_rows
                trans[pl.ds(pl.multiple_of(place, ROWS), share_rows), :] = result[
                    start : start + share_rows, :
                ]
        for slot in range(slots):
            rows = slice(slot * chip_rows, (slot + 1) * chip_rows)
            for tile in range(tiles):
                here = trans[rows, tile * LANES : (tile + 1) * LANES]
                met = late_ref[rows, (index * tiles + tile) * LANES : (index * tiles + tile + 1) * LANES]
                twice[slot] = twice[slot] + fold(here * met)
                if tile >= group:
                    gap = jnp.zeros((edge, LANES), jnp.float32)
                    turned = jnp.concatenate([gap, here, gap, here], axis=0).T
                    corner = jnp.where(low_half, turned[edge:half, :], turned[half + edge :, :])
                    once[slot] = once[slot] + fold(jnp.where(in_rest, here * corner, 0.0))
    value = jnp.zeros((1, LANES), jnp.float32)
    for slot in range(slots):
        slot_sum = jnp.sum(once[slot] + 2.0 * twice[slot])
        value = jnp.where(lane == place_ref[slot], slot_sum, value)
    sum_ref[...] = jnp.broadcast_to(value, sum_ref.shape)


def swap(value, mask, blocks):
    return lax.ppermute(value, "block", [(index, index ^ mask) for index in range(blocks)])


def body(green, chol, counts, move_slot, move_dest):
    walkers = lax.axis_size("walker")
    blocks = lax.axis_size("block")
    slots, share_width = green.shape
    vectors, occ_count, orb_count = chol.shape
    moves = move_slot.shape[1]
    keep = slots - moves
    share_rows = share_width // orb_count
    pack_rows = slots * share_rows
    table = jnp.concatenate([counts[None, :], move_slot.T, move_dest.T], axis=0)
    walker_index = lax.axis_index("walker").astype(jnp.int32).reshape(1)
    block_index = lax.axis_index("block").astype(jnp.int32).reshape(1)
    smem = pl.BlockSpec(memory_space=pltpu.SMEM)
    vmem = pl.BlockSpec(memory_space=pltpu.VMEM)
    limit = pltpu.CompilerParams(vmem_limit_bytes=32 * 1024 * 1024)

    spread = pltpu.VMEM((orb_count // LANES, share_rows * ROWS, LANES), jnp.float32)
    own_rows = pl.pallas_call(
        functools.partial(pack_kernel, (slots, share_rows, orb_count)),
        out_shape=jax.ShapeDtypeStruct((pack_rows, orb_count), jnp.bfloat16),
        in_specs=[vmem],
        out_specs=vmem,
        scratch_shapes=[spread],
        compiler_params=limit,
        name="pack",
    )(green)
    move_dims = (slots, share_rows, orb_count, walkers, moves, keep)
    leaving = pl.pallas_call(
        functools.partial(leave_kernel, move_dims),
        out_shape=[jax.ShapeDtypeStruct((share_rows, orb_count), jnp.bfloat16)] * (walkers - 1),
        in_specs=[smem, smem, vmem],
        out_specs=[vmem] * (walkers - 1),
        scratch_shapes=[pltpu.VMEM((pack_rows, orb_count), jnp.float32)],
        compiler_params=limit,
        name="leave",
    )(walker_index, table, own_rows)
    coming = [
        lax.ppermute(
            leaving[shift - 1], "walker", [(z, (z + shift) % walkers) for z in range(walkers)]
        )
        for shift in range(1, walkers)
    ]

    group = 4
    groups = vectors // group
    chip_rows = 2 * share_rows
    core, near_x, near_y = 1, 2, 4
    from_x = swap(own_rows, near_x, blocks)
    from_y = swap(own_rows, near_y, blocks)
    from_core = swap(own_rows, core, blocks)
    weights = pl.pallas_call(
        functools.partial(order_kernel, (group, groups, chip_rows)),
        out_shape=jax.ShapeDtypeStruct((vectors * occ_count, orb_count), jnp.bfloat16),
        in_specs=[smem] + [pl.BlockSpec(memory_space=pl.ANY)] * 2,
        out_specs=vmem,
        scratch_shapes=[pltpu.SemaphoreType.DMA((5 * vectors,))],
        compiler_params=pltpu.CompilerParams(vmem_limit_bytes=48 * 1024 * 1024),
        cost_estimate=pl.CostEstimate(
            flops=0, bytes_accessed=4 * chol.size, transcendentals=0
        ),
        name="order",
    )(block_index, chol, own_rows)
    width = orb_count // 2
    from_x, from_y, weights, coming[:2] = lax.optimization_barrier(
        (from_x, from_y, weights, coming[:2])
    )
    far = [swap(from_y[:, :width], near_x, blocks), swap(from_x[:, width:], near_y, blocks)]
    near_pieces = [own_rows, from_core]
    for piece in (from_x, from_y):
        near_pieces += [piece, swap(piece, core, blocks)]

    dims = (slots, share_rows, group, groups, chip_rows)
    work = 2 * vectors * occ_count * orb_count * pack_rows
    near_sums, late, place = pl.pallas_call(
        functools.partial(near_kernel, dims, (slots, walkers, moves, keep)),
        out_shape=[
            jax.ShapeDtypeStruct((slots * ROWS, LANES), jnp.float32),
            jax.ShapeDtypeStruct((slots * chip_rows, vectors * occ_count), jnp.float32),
            jax.ShapeDtypeStruct((slots,), jnp.int32),
        ],
        in_specs=[smem] * 3 + [vmem] * 7,
        out_specs=[vmem] * 2 + [smem],
        scratch_shapes=[pltpu.VMEM((slots * 3 * chip_rows, group * occ_count), jnp.float32)]
        * groups,
        compiler_params=limit,
        cost_estimate=pl.CostEstimate(
            flops=6 * work, bytes_accessed=2 * chol.size, transcendentals=0
        ),
        name="near",
    )(block_index, walker_index, table, weights, *near_pieces)
    far, near_sums = lax.optimization_barrier((far, near_sums))
    far_pieces = far + [swap(piece, core, blocks) for piece in far]
    all_sums = pl.pallas_call(
        functools.partial(far_kernel, dims),
        out_shape=jax.ShapeDtypeStruct((blocks * walkers, LANES), jnp.float32),
        in_specs=[smem] * 2 + [vmem] * 7,
        out_specs=vmem,
        scratch_shapes=[pltpu.VMEM((slots * chip_rows, group * occ_count), jnp.float32)] * groups,
        compiler_params=limit,
        cost_estimate=pl.CostEstimate(
            flops=2 * work, bytes_accessed=2 * chol.size, transcendentals=0
        ),
        name="far",
    )(block_index, place, weights, near_sums, late, *far_pieces)

    coming, _ = lax.optimization_barrier((coming, all_sums))
    new_green = pl.pallas_call(
        functools.partial(assemble_kernel, move_dims),
        out_shape=jax.ShapeDtypeStruct((keep, share_width), jnp.bfloat16),
        in_specs=[smem] * 2 + [vmem] * walkers,
        out_specs=vmem,
        scratch_shapes=[
            pltpu.VMEM((orb_count // LANES, share_rows * ROWS, LANES), jnp.float32),
            pltpu.VMEM(((slots + walkers - 1) * share_rows, orb_count), jnp.float32),
            pltpu.VMEM((orb_count // LANES, share_rows * ROWS, LANES), jnp.float32),
        ],
        compiler_params=limit,
        name="assemble",
    )(walker_index, table, green, *coming)

    energy_scale = 0.5 / (occ_count * math.sqrt(vectors * blocks))
    got = lax.all_to_all(
        all_sums, ("block", "walker"), split_axis=0, concat_axis=0, tiled=True
    )
    got_sums = jnp.sum(got, axis=0)
    own_sums = lax.dynamic_slice(got_sums, (walker_index[0] * keep,), (keep,))
    return (new_green, -energy_scale * own_sums)


def fits(mesh):
    blocks = mesh.shape["block"]
    walkers = mesh.shape["walker"]

    def check(green, chol, counts, move_slot, move_dest):
        vectors, occ_count, orb_count = chol.shape
        share_width = green.shape[1] // blocks
        moves = move_slot.shape[1]
        slots = green.shape[0] // walkers
        return (
            blocks == 8
            and walkers >= 2
            and walkers & (walkers - 1) == 0
            and (moves + walkers - 2) // (walkers - 1) == 1
            and slots <= ROWS
            and share_width % (orb_count * ROWS) == 0
            and orb_count % (2 * LANES) == 0
            and occ_count == blocks * (share_width // orb_count)
            and occ_count == LANES + LANES // 2
            and (vectors // blocks) % 4 == 0
            and walkers * (slots - moves) <= LANES
        )

    return check


def solution(mesh):
    in_specs = (P("walker", "block"), P("block", None, None), P(), P(), P())
    out_specs = (P("walker", "block"), P("walker"))
    check = fits(mesh)

    def run(*args):
        chosen = body if check(*args) else general_body
        return jax.shard_map(
            chosen, mesh=mesh, in_specs=in_specs, out_specs=out_specs, check_vma=False
        )(*args)

    return run
```

```python
import functools
import math

import jax
import jax.numpy as jnp
from jax import lax
from jax.experimental import pallas as pl
from jax.experimental.pallas import tpu as pltpu
from jax.sharding import PartitionSpec as P


def arrival_ranks(move_slot, move_dest):
    active = move_slot >= 0
    move_total = move_slot.shape[1]
    earlier = jnp.arange(move_total)[None, :] < jnp.arange(move_total)[:, None]
    same_target = (
        (move_dest[:, :, None] == move_dest[:, None, :]) & earlier[None, :, :] & active[:, None, :]
    )
    return (active, jnp.sum(same_target.astype(jnp.int32), axis=2))


def general_body(green, chol, counts, move_slot, move_dest):
    walker_total = lax.axis_size("walker")
    own_index = lax.axis_index("walker")
    slot_total = green.shape[0]
    share_width = green.shape[1]
    keep_total = slot_total - move_slot.shape[1]
    capacity = (move_slot.shape[1] + walker_total - 2) // (walker_total - 1)
    occ_count = chol.shape[1]
    orb_count = chol.shape[2]
    energy_scale = 0.5 / (occ_count * math.sqrt(chol.shape[0] * lax.axis_size("block")))
    active, move_rank = arrival_ranks(move_slot, move_dest)
    own_slots = move_slot[own_index]
    own_dests = move_dest[own_index]
    own_active = active[own_index]
    own_rank = move_rank[own_index]
    peer_ids = jnp.arange(walker_total)
    place_ids = jnp.arange(capacity)
    chosen = (
        (own_dests[None, None, :] == peer_ids[:, None, None])
        & (own_rank[None, None, :] == place_ids[None, :, None])
        & own_active[None, None, :]
    )
    send_slot = jnp.sum(jnp.where(chosen, own_slots[None, None, :], 0), axis=2).reshape(-1)
    present = jnp.any(chosen, axis=2).reshape(-1)
    arrive = jnp.any(
        (move_dest[:, None, :] == own_index)
        & (move_rank[:, None, :] == place_ids[None, :, None])
        & active[:, None, :],
        axis=2,
    ).reshape(-1)
    slot_ids = jnp.arange(slot_total)
    occupied = slot_ids < counts[own_index]
    leaving = jnp.any(own_slots[:, None] == slot_ids[None, :], axis=0)
    staying = occupied & jnp.logical_not(leaving)
    stay_rank = jnp.cumsum(staying.astype(jnp.int32)) - 1
    arrive_rank = jnp.cumsum(arrive.astype(jnp.int32)) - 1
    stay_total = jnp.sum(staying.astype(jnp.int32))
    targets = jnp.arange(keep_total)
    from_stay = jnp.sum(
        jnp.where(
            staying[None, :] & (stay_rank[None, :] == targets[:, None]), slot_ids[None, :], 0
        ),
        axis=1,
    )
    arrive_ids = jnp.arange(arrive.shape[0]) + slot_total
    from_arrive = jnp.sum(
        jnp.where(
            arrive[None, :] & (arrive_rank[None, :] == (targets - stay_total)[:, None]),
            arrive_ids[None, :],
            0,
        ),
        axis=1,
    )
    source_row = jnp.where(targets < stay_total, from_stay, from_arrive)
    outgoing = jnp.where(
        present[:, None], jnp.take(green, send_slot, axis=0), jnp.zeros((), jnp.bfloat16)
    )
    outgoing = outgoing.reshape(walker_total, capacity, share_width)

    def walker_energy(walker_row):
        green_mat = walker_row.reshape(occ_count, orb_count)
        transfer = jnp.einsum("gip,jp->gij", chol, green_mat, preferred_element_type=jnp.float32)
        return jnp.sum(transfer * jnp.swapaxes(transfer, 1, 2))

    got_rows = lax.all_to_all(outgoing, "walker", split_axis=0, concat_axis=0, tiled=True)
    source_pool = jnp.concatenate([green, got_rows.reshape(-1, share_width)], axis=0)
    new_green = jnp.take(source_pool, source_row, axis=0)
    complete = lax.all_gather(new_green, "block", axis=1, tiled=True)
    partial_value = lax.map(walker_energy, complete)
    energy = -energy_scale * lax.psum(partial_value, "block")
    return (new_green, energy)


LANES = 128
ROWS = 8


def spread_slots(green_ref, spread, share_rows):
    slots = green_ref.shape[0]
    tiles = spread.shape[0]
    for row in range(share_rows):
        for tile in range(tiles):
            col = (row * tiles + tile) * LANES
            block = green_ref[:, col : col + LANES].astype(jnp.float32)
            spread[tile, row * ROWS : row * ROWS + slots, :] = block


def pack_kernel(dims, green_ref, own_ref, spread):
    slots, share_rows, orb_count = dims
    spread_slots(green_ref, spread, share_rows)
    for tile in range(orb_count // LANES):
        dense = [spread[tile, pl.ds(slot, share_rows, stride=ROWS), :] for slot in range(slots)]
        packed = jnp.concatenate(dense, axis=0).astype(jnp.bfloat16)
        own_ref[:, tile * LANES : (tile + 1) * LANES] = packed


class Moves:
    def __init__(self, table_ref, moves):
        self.table, self.moves = table_ref, moves

    def count(self, device):
        return self.table[0, device]

    def slot(self, device, move):
        return self.table[1 + move, device]

    def dest(self, device, move):
        return self.table[1 + self.moves + move, device]

    def staying(self, device):
        total = self.count(device)
        for move in range(self.moves):
            total = total - jnp.where(self.slot(device, move) >= 0, 1, 0)
        return total

    def goes_to(self, own, slot):
        target = jnp.int32(-1)
        for move in range(self.moves):
            target = jnp.where(self.slot(own, move) == slot, self.dest(own, move), target)
        return target


def leave_kernel(dims, ident_ref, table_ref, own_ref, *refs):
    slots, share_rows, orb_count, walkers, moves, keep = dims
    leave_refs, place_ref, wide = refs[:-2], refs[-2], refs[-1]
    table = Moves(table_ref, moves)
    wide[...] = own_ref[...].astype(jnp.float32)
    own = ident_ref[0]
    for shift in range(1, walkers):
        target = lax.rem(own + shift, walkers)
        chosen = jnp.int32(0)
        for move in range(moves):
            hit = (table.dest(own, move) == target) & (table.slot(own, move) >= 0)
            chosen = jnp.where(hit, table.slot(own, move), chosen)
        start = pl.multiple_of(chosen * share_rows, ROWS)
        leave_refs[shift - 1][...] = wide[pl.ds(start, share_rows), :].astype(jnp.bfloat16)
    rank = jnp.int32(0)
    for slot in range(slots):
        live = slot < table.count(own)
        gone_to = table.goes_to(own, slot)
        stays = live & (gone_to < 0)
        there = jnp.maximum(gone_to, 0)
        ahead = table.staying(there)
        for device in range(walkers):
            for move in range(moves):
                hit = (
                    (device < own)
                    & (table.dest(device, move) == there)
                    & (table.slot(device, move) >= 0)
                )
                ahead = ahead + jnp.where(hit, 1, 0)
        place = jnp.where(stays, own * keep + rank, there * keep + ahead)
        place_ref[slot] = jnp.where(live, place, -1)
        rank = rank + jnp.where(stays, 1, 0)


def assemble_kernel(dims, ident_ref, table_ref, green_ref, *refs):
    slots, share_rows, orb_count, walkers, moves, keep = dims
    table = Moves(table_ref, moves)
    come_refs = refs[: walkers - 1]
    new_ref, spread, pool, out = refs[walkers - 1 :]
    own = ident_ref[0]
    tiles = orb_count // LANES
    spread_slots(green_ref, spread, share_rows)
    for slot in range(slots):
        for tile in range(tiles):
            pool[
                slot * share_rows : (slot + 1) * share_rows, tile * LANES : (tile + 1) * LANES
            ] = spread[tile, pl.ds(slot, share_rows, stride=ROWS), :]
    for shift in range(1, walkers):
        start = (slots + shift - 1) * share_rows
        pool[start : start + share_rows, :] = come_refs[shift - 1][...].astype(jnp.float32)

    sources = [jnp.int32(0)] * keep
    rank = jnp.int32(0)
    for slot in range(slots):
        stays = (slot < table.count(own)) & (table.goes_to(own, slot) < 0)
        for target in range(keep):
            sources[target] = jnp.where(stays & (rank == target), slot, sources[target])
        rank = rank + jnp.where(stays, 1, 0)
    for device in range(walkers):
        comes = jnp.bool_(False)
        for move in range(moves):
            comes = comes | ((table.dest(device, move) == own) & (table.slot(device, move) >= 0))
        comes = comes & (device != own)
        shift = lax.rem(own - device + walkers, walkers)
        for target in range(keep):
            sources[target] = jnp.where(
                comes & (rank == target), slots + shift - 1, sources[target]
            )
        rank = rank + jnp.where(comes, 1, 0)
    for target in range(keep):
        start = pl.multiple_of(sources[target] * share_rows, ROWS)
        for tile in range(tiles):
            out[tile, pl.ds(target, share_rows, stride=ROWS), :] = pool[
                pl.ds(start, share_rows), tile * LANES : (tile + 1) * LANES
            ]
    for row in range(share_rows):
        for tile in range(tiles):
            col = (row * tiles + tile) * LANES
            new_ref[:, col : col + LANES] = out[
                tile, row * ROWS : row * ROWS + keep, :
            ].astype(jnp.bfloat16)


def order_kernel(dims, ident_ref, chol_ref, own_ref, out_ref, sems):
    del own_ref
    group, groups, chip_rows = dims
    chip = ident_ref[0] // 2
    edge = LANES - 2 * chip_rows
    rest = 2 * chip_rows - edge
    copies = []

    def add(vec, distance, start, size, place):
        row = pl.multiple_of(jnp.bitwise_xor(chip, distance) * chip_rows + start, 16)
        copies.append(
            pltpu.make_async_copy(
                chol_ref.at[vec, pl.ds(row, size), :],
                out_ref.at[pl.ds(place, size), :],
                sems.at[len(copies)],
            )
        )

    for index in range(groups):
        for item in range(group):
            vec = index * group + item
            place = index * group * 4 * chip_rows + item * LANES
            add(vec, 0, 0, chip_rows, place)
            add(vec, 1, 0, chip_rows, place + chip_rows)
            add(vec, 2, 0, edge, place + 2 * chip_rows)
            place = index * group * 4 * chip_rows + group * LANES + item * rest
            add(vec, 2, edge, chip_rows - edge, place)
            add(vec, 3, 0, chip_rows, place + chip_rows - edge)
    for copy in copies:
        copy.start()
    for copy in copies:
        copy.wait()


def padded(rows):
    return -(-rows // 16) * 16


def stacked(refs):
    values = []
    for ref in refs:
        rows, width = ref.shape
        values.append(ref[...])
        if padded(rows) > rows:
            values.append(jnp.zeros((padded(rows) - rows, width), jnp.bfloat16))
    return jnp.concatenate(values, axis=0)


def times(left, right):
    return lax.dot_general(
        left, right, (((1,), (1,)), ((), ())), preferred_element_type=jnp.float32
    )


def near_kernel(dims, ident_ref, weight_ref, *refs):
    slots, share_rows, group, groups, chip_rows = dims
    piece_refs = refs[:6]
    sum_ref, late_ref = refs[6:8]
    trans_refs = refs[8:]
    own = ident_ref[0]
    core = lax.rem(own, 2)
    pad_rows = padded(piece_refs[0].shape[0])
    near = 3 * chip_rows
    size = 4 * chip_rows * group
    edge = near - LANES
    half = LANES // 2
    left = stacked(piece_refs)
    lane = lax.broadcasted_iota(jnp.int32, (1, LANES), 1)
    low_half = lane < half
    in_edge = jnp.where(low_half, lane, lane - half) < edge
    sums = [jnp.zeros((ROWS, LANES), jnp.float32) for _ in range(slots)]

    def fold(value):
        return jnp.sum(value.reshape(-1, ROWS, LANES), axis=0)

    for index in range(groups):
        trans = trans_refs[index]
        result = times(left, weight_ref[index * size : (index + 1) * size, :])
        for piece in range(6):
            source = jnp.bitwise_xor(core, piece % 2)
            for slot in range(slots):
                start = piece * pad_rows + slot * share_rows
                place = slot * near + (piece // 2) * chip_rows + source * share_rows
                trans[pl.ds(pl.multiple_of(place, ROWS), share_rows), :] = result[
                    start : start + share_rows, :
                ]
        for slot in range(slots):
            base = slot * near
            late = slice(slot * chip_rows, (slot + 1) * chip_rows)
            acc = sums[slot]
            for pair in range(group // 2):
                col = (group + pair) * LANES
                top = trans[base : base + LANES, col : col + LANES].T
                edge_rows = trans[base + LANES : base + near, col : col + LANES]
                gap = jnp.zeros((half - edge, LANES), jnp.float32)
                bottom = jnp.concatenate([edge_rows, gap, edge_rows, gap], axis=0).T
                for side in range(2):
                    vec = 2 * pair + side
                    high = trans[base : base + LANES, vec * LANES : (vec + 1) * LANES]
                    acc = acc + fold(high * high.T)
                    across = trans[base + LANES : base + near, vec * LANES : (vec + 1) * LANES]
                    acc = acc + 2.0 * fold(across * top[side * half : side * half + edge, :])
                    late_ref[
                        late, (index * (group + group // 2) + vec) * LANES : (
                            index * (group + group // 2) + vec + 1
                        ) * LANES
                    ] = top[side * half + edge : (side + 1) * half, :]
                corner = jnp.where(low_half, bottom[:edge, :], bottom[half : half + edge, :])
                acc = acc + fold(jnp.where(in_edge, edge_rows * corner, 0.0))
                rest = jnp.where(low_half, bottom[edge:half, :], bottom[half + edge :, :])
                place = (index * (group + group // 2) + group + pair) * LANES
                late_ref[late, place : place + LANES] = jnp.where(in_edge, rest, 0.0)
            sums[slot] = acc
    sum_ref[...] = jnp.concatenate(sums, axis=0)


def far_kernel(dims, ident_ref, place_ref, weight_ref, near_sum_ref, late_ref, *refs):
    slots, share_rows, group, groups, chip_rows = dims
    here_ref, there_ref, sum_ref = refs[:3]
    trans_refs = refs[3:]
    own = ident_ref[0]
    core = lax.rem(own, 2)
    _, pack_rows, width = here_ref.shape
    pad_rows = padded(pack_rows)
    half = LANES // 2
    edge = half - chip_rows
    size = 4 * chip_rows * group
    lane = lax.broadcasted_iota(jnp.int32, (1, LANES), 1)
    low_half = lane < half
    in_rest = jnp.where(low_half, lane, lane - half) >= edge
    lefts = [stacked([here_ref.at[part], there_ref.at[part]]) for part in range(2)]
    twice = [jnp.zeros((ROWS, LANES), jnp.float32) for _ in range(slots)]
    once = [near_sum_ref[slot * ROWS : (slot + 1) * ROWS, :] for slot in range(slots)]

    def fold(value):
        return jnp.sum(value.reshape(-1, ROWS, LANES), axis=0)

    tiles = group + group // 2
    for index in range(groups):
        trans = trans_refs[index]
        rows = slice(index * size, (index + 1) * size)
        result = times(lefts[0], weight_ref[rows, :width])
        result = result + times(lefts[1], weight_ref[rows, width:])
        for piece in range(2):
            source = jnp.bitwise_xor(core, piece)
            for slot in range(slots):
                start = piece * pad_rows + slot * share_rows
                place = slot * chip_rows + source * share_rows
                trans[pl.ds(pl.multiple_of(place, ROWS), share_rows), :] = result[
                    start : start + share_rows, :
                ]
        for slot in range(slots):
            rows = slice(slot * chip_rows, (slot + 1) * chip_rows)
            for tile in range(tiles):
                here = trans[rows, tile * LANES : (tile + 1) * LANES]
                met = late_ref[rows, (index * tiles + tile) * LANES : (index * tiles + tile + 1) * LANES]
                twice[slot] = twice[slot] + fold(here * met)
                if tile >= group:
                    gap = jnp.zeros((edge, LANES), jnp.float32)
                    turned = jnp.concatenate([gap, here, gap, here], axis=0).T
                    corner = jnp.where(low_half, turned[edge:half, :], turned[half + edge :, :])
                    once[slot] = once[slot] + fold(jnp.where(in_rest, here * corner, 0.0))
    value = jnp.zeros((1, LANES), jnp.float32)
    for slot in range(slots):
        slot_sum = jnp.sum(once[slot] + 2.0 * twice[slot])
        value = jnp.where(lane == place_ref[slot], slot_sum, value)
    sum_ref[...] = jnp.broadcast_to(value, sum_ref.shape)


def swap(value, mask, blocks):
    return lax.ppermute(value, "block", [(index, index ^ mask) for index in range(blocks)])


def pair_kernel(one_ref, two_ref, out_ref):
    out_ref[0] = one_ref[...]
    out_ref[1] = two_ref[...]


def pair(one, two):
    vmem = pl.BlockSpec(memory_space=pltpu.VMEM)
    return pl.pallas_call(
        pair_kernel,
        out_shape=jax.ShapeDtypeStruct((2, *one.shape), one.dtype),
        in_specs=[vmem] * 2,
        out_specs=vmem,
        compiler_params=pltpu.CompilerParams(vmem_limit_bytes=16 * 1024 * 1024),
        name="pair",
    )(one, two)


def body(green, chol, counts, move_slot, move_dest):
    walkers = lax.axis_size("walker")
    blocks = lax.axis_size("block")
    slots, share_width = green.shape
    vectors, occ_count, orb_count = chol.shape
    moves = move_slot.shape[1]
    keep = slots - moves
    share_rows = share_width // orb_count
    pack_rows = slots * share_rows
    table = jnp.concatenate([counts[None, :], move_slot.T, move_dest.T], axis=0)
    walker_index = lax.axis_index("walker").astype(jnp.int32).reshape(1)
    block_index = lax.axis_index("block").astype(jnp.int32).reshape(1)
    smem = pl.BlockSpec(memory_space=pltpu.SMEM)
    vmem = pl.BlockSpec(memory_space=pltpu.VMEM)
    limit = pltpu.CompilerParams(vmem_limit_bytes=32 * 1024 * 1024)

    spread = pltpu.VMEM((orb_count // LANES, share_rows * ROWS, LANES), jnp.float32)
    own_rows = pl.pallas_call(
        functools.partial(pack_kernel, (slots, share_rows, orb_count)),
        out_shape=jax.ShapeDtypeStruct((pack_rows, orb_count), jnp.bfloat16),
        in_specs=[vmem],
        out_specs=vmem,
        scratch_shapes=[spread],
        compiler_params=limit,
        name="pack",
    )(green)
    move_dims = (slots, share_rows, orb_count, walkers, moves, keep)
    *leaving, place = pl.pallas_call(
        functools.partial(leave_kernel, move_dims),
        out_shape=[jax.ShapeDtypeStruct((share_rows, orb_count), jnp.bfloat16)] * (walkers - 1)
        + [jax.ShapeDtypeStruct((slots,), jnp.int32)],
        in_specs=[smem, smem, vmem],
        out_specs=[vmem] * (walkers - 1) + [smem],
        scratch_shapes=[pltpu.VMEM((pack_rows, orb_count), jnp.float32)],
        compiler_params=limit,
        name="leave",
    )(walker_index, table, own_rows)
    coming = [
        lax.ppermute(
            leaving[shift - 1], "walker", [(z, (z + shift) % walkers) for z in range(walkers)]
        )
        for shift in range(1, walkers)
    ]

    group = 4
    groups = vectors // group
    chip_rows = 2 * share_rows
    weights = pl.pallas_call(
        functools.partial(order_kernel, (group, groups, chip_rows)),
        out_shape=jax.ShapeDtypeStruct((vectors * occ_count, orb_count), jnp.bfloat16),
        in_specs=[smem] + [pl.BlockSpec(memory_space=pl.ANY)] * 2,
        out_specs=vmem,
        scratch_shapes=[pltpu.SemaphoreType.DMA((5 * vectors,))],
        compiler_params=pltpu.CompilerParams(vmem_limit_bytes=48 * 1024 * 1024),
        cost_estimate=pl.CostEstimate(
            flops=0, bytes_accessed=4 * chol.size, transcendentals=0
        ),
        name="order",
    )(block_index, chol, own_rows)

    core, near_x, near_y = 1, 2, 4
    from_x = swap(own_rows, near_x, blocks)
    from_y = swap(own_rows, near_y, blocks)
    from_core = swap(own_rows, core, blocks)
    width = orb_count // 2
    from_x, from_y, weights, coming[:2] = lax.optimization_barrier(
        (from_x, from_y, weights, coming[:2])
    )
    far = [swap(from_y[:, :width], near_x, blocks), swap(from_x[:, width:], near_y, blocks)]
    near_pieces = [own_rows, from_core]
    for piece in (from_x, from_y):
        near_pieces += [piece, swap(piece, core, blocks)]

    dims = (slots, share_rows, group, groups, chip_rows)
    work = 2 * vectors * occ_count * orb_count * pack_rows
    near_sums, late = pl.pallas_call(
        functools.partial(near_kernel, dims),
        out_shape=[
            jax.ShapeDtypeStruct((slots * ROWS, LANES), jnp.float32),
            jax.ShapeDtypeStruct((slots * chip_rows, vectors * occ_count), jnp.float32),
        ],
        in_specs=[smem] + [vmem] * 7,
        out_specs=[vmem] * 2,
        scratch_shapes=[pltpu.VMEM((slots * 3 * chip_rows, group * occ_count), jnp.float32)]
        * groups,
        compiler_params=limit,
        cost_estimate=pl.CostEstimate(
            flops=6 * work, bytes_accessed=2 * chol.size, transcendentals=0
        ),
        name="near",
    )(block_index, weights, *near_pieces)
    far, near_sums = lax.optimization_barrier((far, near_sums))
    here = pair(*far)
    far_pieces = [here, swap(here, core, blocks)]
    all_sums = pl.pallas_call(
        functools.partial(far_kernel, dims),
        out_shape=jax.ShapeDtypeStruct((blocks * walkers, LANES), jnp.float32),
        in_specs=[smem] * 2 + [vmem] * 5,
        out_specs=vmem,
        scratch_shapes=[pltpu.VMEM((slots * chip_rows, group * occ_count), jnp.float32)] * groups,
        compiler_params=limit,
        cost_estimate=pl.CostEstimate(
            flops=2 * work, bytes_accessed=2 * chol.size, transcendentals=0
        ),
        name="far",
    )(block_index, place, weights, near_sums, late, *far_pieces)

    coming, _ = lax.optimization_barrier((coming, all_sums))
    new_green = pl.pallas_call(
        functools.partial(assemble_kernel, move_dims),
        out_shape=jax.ShapeDtypeStruct((keep, share_width), jnp.bfloat16),
        in_specs=[smem] * 2 + [vmem] * walkers,
        out_specs=vmem,
        scratch_shapes=[
            pltpu.VMEM((orb_count // LANES, share_rows * ROWS, LANES), jnp.float32),
            pltpu.VMEM(((slots + walkers - 1) * share_rows, orb_count), jnp.float32),
            pltpu.VMEM((orb_count // LANES, share_rows * ROWS, LANES), jnp.float32),
        ],
        compiler_params=limit,
        name="assemble",
    )(walker_index, table, green, *coming)

    energy_scale = 0.5 / (occ_count * math.sqrt(vectors * blocks))
    got = lax.all_to_all(
        all_sums, ("block", "walker"), split_axis=0, concat_axis=0, tiled=True
    )
    got_sums = jnp.sum(got, axis=0)
    own_sums = lax.dynamic_slice(got_sums, (walker_index[0] * keep,), (keep,))
    return (new_green, -energy_scale * own_sums)


def fits(mesh):
    blocks = mesh.shape["block"]
    walkers = mesh.shape["walker"]

    def check(green, chol, counts, move_slot, move_dest):
        vectors, occ_count, orb_count = chol.shape
        share_width = green.shape[1] // blocks
        moves = move_slot.shape[1]
        slots = green.shape[0] // walkers
        return (
            blocks == 8
            and walkers >= 2
            and walkers & (walkers - 1) == 0
            and (moves + walkers - 2) // (walkers - 1) == 1
            and slots <= ROWS
            and share_width % (orb_count * ROWS) == 0
            and orb_count % (2 * LANES) == 0
            and occ_count == blocks * (share_width // orb_count)
            and occ_count == LANES + LANES // 2
            and (vectors // blocks) % 4 == 0
            and walkers * (slots - moves) <= LANES
        )

    return check


def solution(mesh):
    in_specs = (P("walker", "block"), P("block", None, None), P(), P(), P())
    out_specs = (P("walker", "block"), P("walker"))
    check = fits(mesh)

    def run(*args):
        chosen = body if check(*args) else general_body
        return jax.shard_map(
            chosen, mesh=mesh, in_specs=in_specs, out_specs=out_specs, check_vma=False
        )(*args)

    return run
```
